32 devices in a mesh: section: 2 (over x), tensor: 4 (over y, core), dp: 4 (over z).
Axes of the slice: x: 2, y: 2, z: 4, core: 2. Of those that a mesh axis runs over, the one named last changes fastest.
Arguments:
- images: bfloat16 [8, 256, 1152], P('dp', 'tensor'), may hold values from -6 to 6
- timesteps: int32 [8], P('dp'), may hold values from 0 to 999
- t_table: bfloat16 [1000, 1152], replicated, may hold values from -6 to 6
- rel_index: int32 [256, 256], replicated, may hold values from 0 to 960, as said below
- w_qkv: bfloat16 [2, 1152, 3, 1152], P('section', None, None, 'tensor'), may hold values from -0.1875 to 0.1875
- w_time: bfloat16 [2, 1152, 3, 1152], P('section', None, None, 'tensor'), may hold values from -0.1875 to 0.1875
- w_out: bfloat16 [2, 1152, 1152], P('section', 'tensor'), may hold values from -0.5 to 0.5
- w_fc1: bfloat16 [2, 1152, 4608], P('section', None, 'tensor'), may hold values from -0.1875 to 0.1875
- w_fc2: bfloat16 [2, 4608, 1152], P('section', 'tensor'), may hold values from -0.09375 to 0.09375
- rel_table: float32 [2, 961, 16], P('section', None, 'tensor'), may hold values from -4 to 4
- norm_gain: float32 [2, 2, 1152], P('section'), may hold values from 0.1 to 1.9
- norm_shift: float32 [2, 2, 1152], P('section'), may hold values from -2 to 2
- cotangent: bfloat16 [8, 256, 1152], P('dp', 'tensor'), may hold values from -6 to 6
Outputs:
- output: bfloat16 [8, 256, 1152], P('dp', 'tensor')
- input_grads: bfloat16 [2, 8, 256, 1152], P('section', 'dp', 'tensor')
- g_qkv: float32 [2, 1152, 3, 1152], P('section', 'dp', None, 'tensor')
- g_time: float32 [2, 1152, 3, 1152], P('section', 'dp', None, 'tensor')
- g_out: float32 [2, 1152, 1152], P('section', 'tensor', 'dp')
- g_fc1: float32 [2, 1152, 4608], P('section', 'dp', 'tensor')
- g_fc2: float32 [2, 4608, 1152], P('section', 'tensor', 'dp')
- g_table: float32 [2, 961, 16], P('section', None, 'tensor')
- g_gain: float32 [2, 2, 1152], P('section')
- g_shift: float32 [2, 2, 1152], P('section')
The draws below stay inside these ranges and needn't reach their ends.
Inputs may be any that keep to these rules, and one draw needn't show every extreme that they name: `rel_index`: tokens at the same offset between rows and between columns of the patch grid share a bucket; every bucket is used.
All inputs are finite; a program needn't handle non-finite values.
Results may differ from the reference program's by a relative error of at most 0.02.
Values may be sent and summed in bfloat16 or wider, within the bound.
A program may use at most 256 MiB of HBM per device.

```python
import jax
import jax.numpy as jnp
from jax import lax

D = 1152
HEADS = 16
HEAD_DIM = 72
FF = 4608
GRID = 16
NSTEPS = 1000
BLOCKS = 2
SEQ = 256
RELPOS = 961
IMAGES = 8


def draw_rel_index(key, part):
    key = jax.random.fold_in(key, 7)
    order = jax.random.permutation(key, RELPOS)
    cells = jnp.arange(SEQ)
    rows = cells // GRID
    cols = cells % GRID
    span = 2 * GRID - 1
    offset = (rows[:, None] - rows[None, :] + GRID - 1) * span + (cols[:, None] - cols[None, :] + GRID - 1)
    return order[offset].astype(jnp.int32)


def with_ends(drawn, stream_key, least, largest):
    place = [jax.random.randint(jax.random.fold_in(stream_key, axis), (), 0, length) for axis, length in enumerate(drawn.shape)]
    longest = drawn.shape.index(max(drawn.shape))
    beside = place[:longest] + [(place[longest] + 1) % drawn.shape[longest]] + place[longest + 1:]
    return drawn.at[tuple(place)].set(least).at[tuple(beside)].set(largest)


def steps_of(key, shape, cuts, least, top_value):
    def one(position, parts):
        heights = jax.random.uniform(jax.random.fold_in(jax.random.fold_in(key, 6), position), (parts,), jnp.float32, least / len(cuts), top_value / len(cuts))
        return jnp.repeat(jnp.exp(heights), shape[position] // parts).reshape((-1,) + (1,) * (len(shape) - position - 1))

    factor_of = one(*cuts[0])
    for cut in cuts[1:]:
        factor_of = factor_of * one(*cut)
    return factor_of


def normal_values(key, dims, scale, most, split=(), held_as=jnp.bfloat16):
    level = steps_of(key, dims, split, -0.22, 0.18) if split else 1.0
    entries = jax.random.normal(key, dims, jnp.float32) * scale * level
    return jnp.minimum(jnp.maximum(entries, -most), most).astype(held_as)


def setup_inputs(seed: int = 0) -> dict:
    streams_of = jax.random.split(jax.random.key(seed), 14)
    return {
        "images": normal_values(streams_of[0], (IMAGES, SEQ, D), 1.0, 6.0, ((0, 4), (1, 4))),
        "timesteps": with_ends(jax.random.randint(streams_of[1], (IMAGES,), 0, NSTEPS), jax.random.fold_in(streams_of[1], 1), 0, NSTEPS - 1).astype(jnp.int32),
        "t_table": normal_values(streams_of[2], (NSTEPS, D), 1.0, 6.0),
        "rel_index": draw_rel_index(jax.random.fold_in(streams_of[13], 71), 0),
        "w_qkv": normal_values(streams_of[4], (BLOCKS, D, 3, D), D ** -0.5, 0.1875, ((0, 2), (3, 4))),
        "w_time": normal_values(streams_of[5], (BLOCKS, D, 3, D), D ** -0.5, 0.1875, ((0, 2), (3, 4))),
        "w_out": normal_values(streams_of[6], (BLOCKS, D, D), (D // 8) ** -0.5, 0.5, ((0, 2), (1, 4))),
        "w_fc1": normal_values(streams_of[7], (BLOCKS, D, FF), D ** -0.5, 0.1875, ((0, 2), (2, 4))),
        "w_fc2": normal_values(streams_of[8], (BLOCKS, FF, D), FF ** -0.5, 0.09375, ((0, 2), (1, 4))),
        "rel_table": normal_values(streams_of[9], (BLOCKS, RELPOS, HEADS), 1.0, 4.0, ((0, 2), (2, 4)), jnp.float32),
        "norm_gain": jnp.clip(1.0 + 0.18 * jax.random.normal(streams_of[10], (BLOCKS, 2, D), jnp.float32), 0.1, 1.9),
        "norm_shift": normal_values(streams_of[11], (BLOCKS, 2, D), 0.3, 2.0, ((0, 2),), jnp.float32),
        "cotangent": normal_values(streams_of[12], (IMAGES, SEQ, D), 1.0, 6.0, ((0, 4), (1, 4))),
    }


@jax.custom_vjp
def low(v):
    return lax.optimization_barrier(v.astype(jnp.bfloat16)).astype(jnp.float32)

@jax.custom_vjp
def low_back(v):
    return v

def low_keep(v):
    return (low(v), None)

def low_pass(kept, grad):
    return (grad,)

def back_keep(v):
    return (v, None)

def back_low(kept, grad):
    return (low(grad),)
low.defvjp(low_keep, low_pass)
low_back.defvjp(back_keep, back_low)

def layer_norm(rows, gain, shift):
    centre = rows - lax.optimization_barrier(jnp.mean(rows, axis=-1, keepdims=True))
    spread = lax.optimization_barrier(jnp.mean(centre * centre, axis=-1, keepdims=True))
    return centre * lax.rsqrt(spread + 1e-06) * gain + shift

def gelu_tanh(values):
    return jax.nn.gelu(values, approximate=True)

def one_block(x, tvec, params, layer, rel_index):
    w_qkv, w_time, w_out, w_fc1, w_fc2, rel_table, norm_gain, norm_shift = params
    highest = lax.Precision.HIGHEST
    seq = x.shape[0]
    a_first = low(layer_norm(x, norm_gain[layer, 0], norm_shift[layer, 0]))
    time_term = jnp.einsum('d,dcj->cj', tvec, w_time[layer], precision=highest)
    qkv = jnp.einsum('sd,dcj->scj', a_first, w_qkv[layer], precision=highest) + time_term[None]
    qkv = low(low_back(qkv))
    query = qkv[:, 0].reshape(seq, HEADS, HEAD_DIM)
    keys = qkv[:, 1].reshape(seq, HEADS, HEAD_DIM)
    values = qkv[:, 2].reshape(seq, HEADS, HEAD_DIM)
    bias = jnp.transpose(rel_table[layer][rel_index], (2, 0, 1))
    scores = jnp.einsum('qhe,khe->hqk', query, keys, precision=highest) * HEAD_DIM ** (-0.5) + bias
    scores = low_back(scores)
    probs = low(jax.nn.softmax(scores, axis=-1))
    attended = jnp.einsum('hqk,khe->qhe', probs, values, precision=highest).reshape(seq, D)
    attended = low(low_back(attended))
    y_mid = x + low_back(jnp.dot(attended, w_out[layer], precision=highest))
    a_second = low(layer_norm(y_mid, norm_gain[layer, 1], norm_shift[layer, 1]))
    hidden = low_back(jnp.dot(a_second, w_fc1[layer], precision=highest))
    active = low(gelu_tanh(hidden))
    return y_mid + low_back(jnp.dot(active, w_fc2[layer], precision=highest))

def reference(images, timesteps, t_table, rel_index, w_qkv, w_time, w_out, w_fc1, w_fc2, rel_table, norm_gain, norm_shift, cotangent):
    embedded = t_table[timesteps].astype(jnp.float32)
    params = (w_qkv.astype(jnp.float32), w_time.astype(jnp.float32), w_out.astype(jnp.float32), w_fc1.astype(jnp.float32), w_fc2.astype(jnp.float32), rel_table.astype(jnp.float32), norm_gain.astype(jnp.float32), norm_shift.astype(jnp.float32))

    def network(inputs, weights, poke):

        def per_image(triple):
            x_rows, tvec, added = triple
            mid = one_block(x_rows, tvec, weights, 0, rel_index)
            mid = low(low_back(mid)) + added
            return one_block(mid, tvec, weights, 1, rel_index)
        return lax.map(jax.checkpoint(per_image), (inputs, embedded, poke))
    poke = jnp.zeros(images.shape, jnp.float32)
    result, pullback = jax.vjp(network, images.astype(jnp.float32), params, poke)
    grad_images, grads, grad_mid = pullback(cotangent.astype(jnp.float32))
    g_qkv, g_time, g_out, g_fc1, g_fc2, g_table, g_gain, g_shift = grads
    input_grads = jnp.stack([grad_images, grad_mid]).astype(jnp.bfloat16)
    return (result.astype(jnp.bfloat16), input_grads, g_qkv, g_time, g_out, g_fc1, g_fc2, g_table, g_gain, g_shift)
```

```python
import jax
import jax.numpy as jnp
from jax import lax
from jax.sharding import PartitionSpec as P

MICRO = 2


norm_eps = 1e-06


def from_behind(x, axis, by):
    length = lax.axis_size(axis)
    return lax.ppermute(x, axis, [(i, (i + by) % length) for i in range(length)])


def from_behind_2(block, axis, distance):
    devices = range(lax.axis_size(axis))
    route = [(i - distance, i) for i in devices if i - distance in devices]
    return lax.ppermute(block, axis, route)


def layer_norm(rows, gain, shift):
    centre = rows - jnp.mean(rows, axis=-1, keepdims=True)
    spread = jnp.mean(centre * centre, axis=-1, keepdims=True)
    return centre * lax.rsqrt(spread + norm_eps) * gain + shift


def gelu_tanh(values):
    return jax.nn.gelu(values, approximate=True)


def gather_rows(rows):
    return lax.all_gather(rows, "tensor", axis=1, tiled=True)


def sum_rows(terms):
    return lax.psum_scatter(
        terms.astype(jnp.bfloat16), "tensor", scatter_dimension=1, tiled=True
    ).astype(jnp.float32)


def gather_grads(rows):
    return lax.all_gather(rows, "tensor", axis=1, tiled=True)


def sum_grads(terms):
    return lax.psum_scatter(
        terms.astype(jnp.bfloat16), "tensor", scatter_dimension=1, tiled=True
    ).astype(jnp.float32)


def offset_buckets(rel_index):
    seq = rel_index.shape[0]
    grid = int(round(seq**0.5))
    cells = rel_index.reshape(grid, grid, grid, grid)
    after = jnp.transpose(cells[0], (1, 0, 2))
    before = jnp.flip(cells[1:, :, 0, :], axis=0)
    by_row = jnp.concatenate([before, after], axis=0)
    right = by_row[:, 0, :]
    left = jnp.flip(by_row[:, 1:, 0], axis=1)
    return jnp.concatenate([left, right], axis=1)


def expand_bias(table, chosen):
    heads = table.shape[1]
    span = int(round(table.shape[0] ** 0.5))
    grid = (span + 1) // 2
    by_offset = jnp.dot(chosen, table, precision=lax.Precision.HIGHEST)
    by_offset = by_offset.T.reshape(heads, span, span)
    cols = jnp.stack(
        [by_offset[:, :, grid - 1 - c : span - c] for c in range(grid)], axis=1
    )
    bias = jnp.stack([cols[:, :, grid - 1 - r : span - r] for r in range(grid)], axis=1)
    return bias.reshape(heads, grid * grid, grid * grid)


def fold_bias(grads, chosen):
    heads, seq, _ = grads.shape
    grid = int(round(seq**0.5))
    span = 2 * grid - 1
    cells = grads.reshape(heads, grid, grid, grid, grid)
    cols = sum(
        jnp.pad(cells[:, r], ((0, 0), (0, 0), (grid - 1 - r, r), (0, 0))) for r in range(grid)
    )
    offsets = sum(
        jnp.pad(cols[:, c], ((0, 0), (0, 0), (grid - 1 - c, c))) for c in range(grid)
    )
    flat = offsets.reshape(heads, span * span)
    return jnp.einsum("hn,nr->rh", flat, chosen, precision=lax.Precision.HIGHEST)


def split_heads(qkv, heads):
    count, seq, _, local = qkv.shape
    width = local // heads
    query = qkv[:, :, 0].reshape(count, seq, heads, width)
    keys = qkv[:, :, 1].reshape(count, seq, heads, width)
    values = qkv[:, :, 2].reshape(count, seq, heads, width)
    return (query, keys, values, width ** (-0.5))


def head_scores(query, keys, bias_heads, scale):
    return (
        jnp.einsum("iqhe,ikhe->ihqk", query, keys, preferred_element_type=jnp.float32) * scale
        + bias_heads[None]
    )


def forward_block(x_rows, time_part, weights, bias_heads):
    w_qkv, w_out, w_fc1, w_fc2, gains, shifts = weights
    a_first = layer_norm(x_rows, gains[0], shifts[0]).astype(jnp.bfloat16)
    a_whole = gather_rows(a_first)
    qkv = (
        jnp.einsum("isd,dcj->iscj", a_whole, w_qkv, preferred_element_type=jnp.float32)
        + time_part[:, None]
    )
    qkv = qkv.astype(jnp.bfloat16)
    count, seq, _, local = qkv.shape
    query, keys, values, scale = split_heads(qkv, bias_heads.shape[0])
    scores = head_scores(query, keys, bias_heads, scale)
    top = jnp.max(scores, axis=-1, keepdims=True)
    expo = jnp.exp(scores - top)
    total = jnp.sum(expo, axis=-1, keepdims=True)
    probs = (expo / total).astype(jnp.bfloat16)
    log_total = top + jnp.log(total)
    attended = jnp.einsum("ihqk,ikhe->iqhe", probs, values, preferred_element_type=jnp.float32)
    attended = attended.reshape(count, seq, local).astype(jnp.bfloat16)
    branch = sum_rows(
        jnp.einsum("isj,jd->isd", attended, w_out, preferred_element_type=jnp.float32)
    )
    y_mid = x_rows + branch
    a_second = layer_norm(y_mid, gains[1], shifts[1]).astype(jnp.bfloat16)
    a_whole2 = gather_rows(a_second)
    hidden = jnp.einsum("isd,df->isf", a_whole2, w_fc1, preferred_element_type=jnp.float32)
    active = gelu_tanh(hidden).astype(jnp.bfloat16)
    mixed = sum_rows(jnp.einsum("isf,fd->isd", active, w_fc2, preferred_element_type=jnp.float32))
    return (y_mid + mixed, (a_whole, qkv, log_total, attended, y_mid, a_whole2, hidden, active))


def input_part(grad_out, x_rows, cache, weights, bias_heads):
    w_qkv, w_out, w_fc1, w_fc2, gains, shifts = weights
    a_whole, qkv, log_total, attended, y_mid, a_whole2, hidden, active = cache
    grad_mlp = gather_grads(grad_out.astype(jnp.bfloat16))
    grad_active = jnp.einsum("isd,fd->isf", grad_mlp, w_fc2, preferred_element_type=jnp.float32)
    gelu_back = jax.vjp(gelu_tanh, hidden)[1]
    grad_hidden = gelu_back(grad_active)[0].astype(jnp.bfloat16)
    grad_norm2 = sum_grads(
        jnp.einsum("isf,df->isd", grad_hidden, w_fc1, preferred_element_type=jnp.float32)
    )
    norm_back2 = jax.vjp(layer_norm, y_mid, gains[1], shifts[1])[1]
    grad_ln2, g_gain2, g_shift2 = norm_back2(grad_norm2)
    grad_ymid = grad_out + grad_ln2
    grad_branch = gather_grads(grad_ymid.astype(jnp.bfloat16))
    grad_att = jnp.einsum(
        "isd,jd->isj", grad_branch, w_out, preferred_element_type=jnp.float32
    ).astype(jnp.bfloat16)
    count, seq, _, local = qkv.shape
    heads = bias_heads.shape[0]
    query, keys, values, scale = split_heads(qkv, heads)
    grad_att = grad_att.reshape(count, seq, heads, local // heads)
    scores = head_scores(query, keys, bias_heads, scale)
    probs = jnp.exp(scores - log_total)
    grad_probs = jnp.einsum("iqhe,ikhe->ihqk", grad_att, values, preferred_element_type=jnp.float32)
    inner = jnp.sum(probs * grad_probs, axis=-1, keepdims=True)
    grad_scores = (probs * (grad_probs - inner)).astype(jnp.bfloat16)
    grad_query = (
        jnp.einsum("ihqk,ikhe->iqhe", grad_scores, keys, preferred_element_type=jnp.float32) * scale
    )
    grad_keys = (
        jnp.einsum("ihqk,iqhe->ikhe", grad_scores, query, preferred_element_type=jnp.float32)
        * scale
    )
    grad_values = jnp.einsum(
        "ihqk,iqhe->ikhe", probs.astype(jnp.bfloat16), grad_att, preferred_element_type=jnp.float32
    )
    grad_qkv = jnp.stack(
        [
            grad_query.reshape(count, seq, local),
            grad_keys.reshape(count, seq, local),
            grad_values.reshape(count, seq, local),
        ],
        axis=2,
    ).astype(jnp.bfloat16)
    score_sum = jnp.sum(grad_scores.astype(jnp.float32), axis=0)
    grad_norm1 = sum_grads(
        jnp.einsum("iscj,dcj->isd", grad_qkv, w_qkv, preferred_element_type=jnp.float32)
    )
    norm_back1 = jax.vjp(layer_norm, x_rows, gains[0], shifts[0])[1]
    grad_ln1, g_gain1, g_shift1 = norm_back1(grad_norm1)
    grad_x = grad_ymid + grad_ln1
    small_terms = (
        score_sum,
        jnp.stack([g_gain1, g_gain2])[None],
        jnp.stack([g_shift1, g_shift2])[None],
    )
    operands = (
        active,
        grad_mlp,
        a_whole2,
        grad_hidden,
        attended,
        grad_branch,
        a_whole,
        grad_qkv,
    )
    return (grad_x, small_terms, operands)


def weight_part(operands):
    active, grad_mlp, a_whole2, grad_hidden, attended, grad_branch, a_whole, grad_qkv = (
        operands
    )
    g_fc2 = jnp.einsum("isf,isd->fd", active, grad_mlp, preferred_element_type=jnp.float32)
    g_fc1 = jnp.einsum("isd,isf->df", a_whole2, grad_hidden, preferred_element_type=jnp.float32)
    g_out = jnp.einsum("isj,isd->jd", attended, grad_branch, preferred_element_type=jnp.float32)
    g_qkv = jnp.einsum("isd,iscj->dcj", a_whole, grad_qkv, preferred_element_type=jnp.float32)
    token_sums = jnp.sum(grad_qkv.astype(jnp.float32), axis=1)
    return (g_qkv[None], g_out[None], g_fc1[None], g_fc2[None]), token_sums


def settle(operands):
    return weight_part(operands)


def add_terms(total, terms):
    if total is None:
        return terms
    return jax.tree.map(lambda left, right: left + right, total, terms)


def per_device(
    images,
    timesteps,
    t_table,
    rel_index,
    w_qkv,
    w_time,
    w_out,
    w_fc1,
    w_fc2,
    rel_table,
    norm_gain,
    norm_shift,
    cotangent,
):
    first = lax.axis_index("section") == 0
    per = images.shape[0] // MICRO
    embedded = t_table[timesteps]
    weights = (w_qkv[0], w_out[0], w_fc1[0], w_fc2[0], norm_gain[0], norm_shift[0])
    buckets = offset_buckets(rel_index).reshape(-1, 1)
    chosen = (buckets == jnp.arange(rel_table.shape[1])[None, :]).astype(jnp.float32)
    bias_heads = expand_bias(rel_table[0], chosen)
    time_all = jnp.einsum("id,dcj->icj", embedded, w_time[0], preferred_element_type=jnp.float32)

    def pick(array, micro):
        return array[micro * per : (micro + 1) * per]

    received = jnp.zeros_like(pick(images, 0))
    inputs, times, outputs = ([], [], [])
    for tick in range(MICRO + 1):
        own = min(tick, MICRO - 1)
        before = max(tick - 1, 0)
        block_in = jnp.where(first, pick(images, own), received)
        time_part = jnp.where(first, pick(time_all, own), pick(time_all, before))
        result, cache = forward_block(block_in.astype(jnp.float32), time_part, weights, bias_heads)
        sent = result.astype(jnp.bfloat16)
        received = from_behind(sent, "section", 1)
        inputs.append(block_in)
        times.append(time_part)
        if tick >= 1:
            outputs.append(jnp.where(first, received, sent))
    back_in = jnp.zeros_like(pick(cotangent, 0))
    weight_total = None
    small_total = None
    sent_grads = []
    tick_sums = []
    for tick in range(MICRO + 1):
        lower = max(tick - 1, 0)
        upper = min(tick + 1, MICRO)
        valid = jnp.where(first, tick >= 1, tick < MICRO)
        grad_in = jnp.where(first, back_in, pick(cotangent, min(tick, MICRO - 1)))
        grad_in = jnp.where(valid, grad_in, jnp.zeros_like(grad_in))
        x_rows = jnp.where(first, inputs[lower], inputs[upper]).astype(jnp.float32)
        time_part = jnp.where(first, times[lower], times[upper])
        cache = forward_block(x_rows, time_part, weights, bias_heads)[1]
        grad_x, small_terms, operands = input_part(
            grad_in.astype(jnp.float32), x_rows, cache, weights, bias_heads
        )
        small_total = add_terms(small_total, small_terms)
        grad_sent = grad_x.astype(jnp.bfloat16)
        back_in = from_behind_2(grad_sent, "section", -1)
        weight_terms, token_sums = settle(operands)
        weight_total = add_terms(weight_total, weight_terms)
        tick_sums.append(token_sums)
        sent_grads.append(grad_sent)
    g_qkv, g_out, g_fc1, g_fc2 = [
        lax.psum_scatter(
            total.astype(jnp.bfloat16), "dp", scatter_dimension=split, tiled=True
        ).astype(jnp.float32)
        for total, split in zip(weight_total, (1, 2, 1, 2))
    ]
    image_sums = jnp.concatenate(
        [jnp.where(first, tick_sums[k + 1], tick_sums[k]) for k in range(MICRO)], axis=0
    )
    all_sums = lax.all_gather(image_sums, "dp", axis=0, tiled=True)
    all_embedded = lax.all_gather(embedded, "dp", axis=0, tiled=True)
    width = embedded.shape[1] // lax.axis_size("dp")
    mine = lax.dynamic_slice_in_dim(all_embedded, lax.axis_index("dp") * width, width, axis=1)
    g_time = jnp.einsum(
        "id,icj->dcj", mine.astype(jnp.float32), all_sums, precision=lax.Precision.HIGHEST
    )[None]
    g_table = lax.psum(fold_bias(small_total[0], chosen), "dp")[None]
    g_gain, g_shift = lax.psum((small_total[1], small_total[2]), ("tensor", "dp"))
    output = jnp.concatenate(outputs, axis=0)
    own_grads = [
        jnp.where(first, sent_grads[tick], sent_grads[tick - 1]) for tick in range(1, MICRO + 1)
    ]
    input_grads = jnp.concatenate(own_grads, axis=0)[None]
    return (output, input_grads, g_qkv, g_time, g_out, g_fc1, g_fc2, g_table, g_gain, g_shift)


def solution(mesh):
    in_specs = (
        P("dp", "tensor", None),
        P("dp"),
        P(),
        P(),
        P("section", None, None, "tensor"),
        P("section", None, None, "tensor"),
        P("section", "tensor", None),
        P("section", None, "tensor"),
        P("section", "tensor", None),
        P("section", None, "tensor"),
        P("section", None, None),
        P("section", None, None),
        P("dp", "tensor", None),
    )
    out_specs = (
        P("dp", "tensor", None),
        P("section", "dp", "tensor", None),
        P("section", "dp", None, "tensor"),
        P("section", "dp", None, "tensor"),
        P("section", "tensor", "dp"),
        P("section", "dp", "tensor"),
        P("section", "tensor", "dp"),
        P("section", None, "tensor"),
        P("section", None, None),
        P("section", None, None),
    )
    return jax.shard_map(
        per_device, mesh=mesh, in_specs=in_specs, out_specs=out_specs, check_vma=False
    )
```

```python
import functools

import jax
import jax.numpy as jnp
from jax import lax
from jax.experimental import pallas as pl
from jax.experimental.pallas import tpu as pltpu
from jax.sharding import PartitionSpec as P

MESH = pl.DeviceIdType.MESH
F32 = jnp.float32
BF16 = jnp.bfloat16
EPS = 1e-06
GELU_A = 0.7978845608028654
GELU_B = 0.044715
ATT, MLP, DMLP, DATT = range(4)


def mm(a, b):
    return lax.dot_general(a, b, (((1,), (0,)), ((), ())), preferred_element_type=F32)


def mm_nt(a, b):
    return lax.dot_general(a, b, (((1,), (1,)), ((), ())), preferred_element_type=F32)


def mm_tn(a, b):
    return lax.dot_general(a, b, (((0,), (0,)), ((), ())), preferred_element_type=F32)


def head_windows(heads, local):
    width = local // heads
    found = []
    for h in range(heads):
        lo = h * width // 128 * 128
        hi = min(-(-(h + 1) * width // 128) * 128, local)
        found.append((lo, hi, h * width - lo, (h + 1) * width - lo))
    return found


def only(x, start, stop):
    lane = lax.broadcasted_iota(jnp.int32, x.shape, 1)
    return jnp.where((lane >= start) & (lane < stop), x, jnp.zeros_like(x))


def block_kernel(
    cfg,
    x_ref, cot_ref, wq_ref, wo_ref, w1_ref, w2_ref, tp_ref, gain_ref, shift_ref, tx_ref,
    out_ref, ig_ref, gq_ref, go_ref, g1_ref, g2_ref, tok_ref, fold_ref, small_ref,
    xin, gin, mid, gath, keep, rcv_c, rcv_y, snd_c, snd_y, bias, prob, qkv, att, act, dgel,
    xhat, inv, ymid, dy1, dqkv, dh, datt, acc, dsum,
    ag_s, ag_r, rs_s, rs_r, sec_s, sec_r,
):
    count, rows, seq, heads = cfg
    half_rows = 2 * rows
    width = x_ref.shape[-1]
    local = wo_ref.shape[0]
    grid = int(round(seq**0.5))
    windows = head_windows(heads, local)
    scale = (local // heads) ** (-0.5)

    s = lax.axis_index("section")
    t = lax.axis_index("tensor")
    core = t + 1 - 2 * (t % 2)
    far = (t + 2) % 4
    fcore = (core + 2) % 4
    here = t // 2
    there = 1 - here
    own = pl.ds(pl.multiple_of(t * rows, rows), rows)

    barrier = pltpu.get_barrier_semaphore()
    for peer in ({"tensor": core}, {"tensor": far}, {"section": 1 - s}):
        pl.semaphore_signal(barrier, inc=1, device_id=peer, device_id_type=MESH)
    pl.semaphore_wait(barrier, 3)

    def rows_of(owner):
        return pl.ds(pl.multiple_of(owner * rows, rows), rows)

    def half_of(half):
        return pl.ds(pl.multiple_of(half * half_rows, half_rows), half_rows)

    def ag_copy(k, i, which):
        owner, to = ((t, core), (t, far), (far, core))[which]
        ref = gath.at[k, i, rows_of(owner), :]
        return pltpu.make_async_remote_copy(
            src_ref=ref, dst_ref=ref, send_sem=ag_s.at[k, i, which], recv_sem=ag_r.at[k, i, which],
            device_id={"tensor": to}, device_id_type=MESH,
        )

    def ag_start(k, i):
        ag_copy(k, i, 1).start()
        ag_copy(k, i, 0).start()

    def ag_near(k, i):
        ag_copy(k, i, 0).wait_recv()

    def ag_pass(k, i):
        ag_copy(k, i, 1).wait_recv()
        ag_copy(k, i, 2).start()

    def ag_rest(k, i):
        ag_copy(k, i, 2).wait_recv()

    def ag_done(k, i):
        for which in range(3):
            ag_copy(k, i, which).wait_send()

    def rs_copy(k, i, which):
        if which < 2:
            src, dst, to = snd_c.at[k, i, which], rcv_c.at[k, i, which], core
        else:
            src, dst, to = snd_y.at[k, i], rcv_y.at[k, i], far
        return pltpu.make_async_remote_copy(
            src_ref=src, dst_ref=dst, send_sem=rs_s.at[k, i, which], recv_sem=rs_r.at[k, i, which],
            device_id={"tensor": to}, device_id_type=MESH,
        )

    mine = pl.ds(pl.multiple_of((t % 2) * rows, rows), rows)
    other = pl.ds(pl.multiple_of((1 - t % 2) * rows, rows), rows)

    def rs_give(k, i, which, part):
        keep[i, which] = part
        snd_c[k, i, which] = keep[i, which, other, :].astype(BF16)
        rs_copy(k, i, which).start()

    def rs_pass(k, i):
        rs_copy(k, i, 0).wait_recv()
        snd_y[k, i] = (keep[i, 0, mine, :] + rcv_c[k, i, 0].astype(F32)).astype(BF16)
        rs_copy(k, i, 2).start()

    def rs_take(k, i):
        rs_copy(k, i, 1).wait_recv()
        near = keep[i, 1, mine, :] + rcv_c[k, i, 1].astype(F32)
        rs_copy(k, i, 2).wait_recv()
        return near + rcv_y[k, i].astype(F32)

    def rs_done(k, i):
        for which in range(3):
            rs_copy(k, i, which).wait_send()

    def sec_copy(j, src, dst):
        return lambda i: pltpu.make_async_remote_copy(
            src_ref=src.at[i], dst_ref=dst.at[i], send_sem=sec_s.at[j, i], recv_sem=sec_r.at[j, i],
            device_id={"section": 1 - s}, device_id_type=MESH,
        )

    mid_copy = sec_copy(0, mid, xin)
    grad_copy = sec_copy(1, ig_ref, gin)
    out_copy = sec_copy(2, out_ref, out_ref)

    def each_image(body):
        def run(i, carry):
            body(i)
            return carry

        lax.fori_loop(0, count, run, 0)

    def norm(x, which, i):
        mean = jnp.mean(x, axis=-1, keepdims=True)
        centre = x - mean
        root = lax.rsqrt(jnp.mean(centre * centre, axis=-1, keepdims=True) + EPS)
        hat = centre * root
        xhat[which, i] = hat
        inv[which, i] = jnp.broadcast_to(root, (rows, 128))
        return (hat * gain_ref[which : which + 1, :] + shift_ref[which : which + 1, :]).astype(BF16)

    def norm_back(da, which, i):
        hat = xhat[which, i]
        small_ref[which : which + 1, :] += jnp.sum(da * hat, axis=0, keepdims=True)
        small_ref[2 + which : 3 + which, :] += jnp.sum(da, axis=0, keepdims=True)
        dhat = da * gain_ref[which : which + 1, :]
        m1 = jnp.mean(dhat, axis=-1, keepdims=True)
        m2 = jnp.mean(dhat * hat, axis=-1, keepdims=True)
        return inv[which, i][:, :1] * (dhat - m1 - hat * m2)

    small_ref[...] = jnp.zeros_like(small_ref)

    @pl.when(s == 1)
    def _():
        def begin(i):
            gath[DMLP, i, own, :] = cot_ref[i]
            ag_start(DMLP, i)

        each_image(begin)

    def take_input(i):
        @pl.when(s == 0)
        def _():
            xin[i] = x_ref[i]

        @pl.when(s == 1)
        def _():
            mid_copy(i).wait_recv()

        gath[ATT, i, own, :] = norm(xin[i].astype(F32), 0, i)
        ag_start(ATT, i)

    def expand(h, carry):
        for r in range(grid):
            shift = (2 * seq - grid * (grid - 1 - r)) % (2 * seq)
            bias[h, r * grid : (r + 1) * grid, :] = pltpu.roll(tx_ref[h], shift, 1)[:, :seq]
        return carry

    @pl.when(s == 1)
    def _():
        lax.fori_loop(0, heads, expand, 0)
        each_image(lambda i: ag_pass(DMLP, i))

    each_image(take_input)

    @pl.when(s == 0)
    def _():
        lax.fori_loop(0, heads, expand, 0)

    def project(i, half):
        a = gath[ATT, i, half_of(half), :]
        for c in range(3):
            qkv[c, i, half_of(half), :] = (mm_nt(a, wq_ref[c]) + tp_ref[i, c : c + 1, :]).astype(BF16)

    def att_near(i):
        ag_near(ATT, i)
        project(i, here)

    each_image(att_near)

    def att_rest(i):
        ag_pass(ATT, i)
        ag_rest(ATT, i)
        project(i, there)
        acc[...] = jnp.zeros_like(acc)
        for h, (lo, hi, start, stop) in enumerate(windows):
            q = only(qkv[0, i, :, lo:hi], start, stop)
            scores = mm_nt(q, qkv[1, i, :, lo:hi]) * scale + bias[h]
            top = jnp.max(scores, axis=-1, keepdims=True)
            expo = jnp.exp(scores - top)
            p = expo / jnp.sum(expo, axis=-1, keepdims=True)
            prob[i, h] = p
            acc[0, :, lo:hi] += mm(p.astype(BF16), only(qkv[2, i, :, lo:hi], start, stop))
        att[i] = acc[0].astype(BF16)
        rs_give(ATT, i, 0, mm(att[i, half_of(there), :], wo_ref[...]))
        rs_give(ATT, i, 1, mm(att[i, half_of(here), :], wo_ref[...]))
        rs_pass(ATT, i)

    each_image(att_rest)

    def att_end(i):
        y = xin[i].astype(F32) + rs_take(ATT, i)
        ymid[i] = y
        gath[MLP, i, own, :] = norm(y, 1, i)
        ag_start(MLP, i)

    each_image(att_end)

    def mlp_half(i, half, which):
        a = gath[MLP, i, half_of(half), :]
        v = mm(a, w1_ref[...])
        th = jnp.tanh(GELU_A * (v + GELU_B * (v * v * v)))
        up = 0.5 * (1.0 + th)
        act[i, half_of(half), :] = (v * up).astype(BF16)
        dgel[i, half_of(half), :] = up + (0.5 * GELU_A) * v * (1.0 - th * th) * (
            1.0 + (3.0 * GELU_B) * (v * v)
        )
        rs_give(MLP, i, which, mm(act[i, half_of(half), :], w2_ref[...]))

    def mlp_near(i):
        ag_near(MLP, i)
        mlp_half(i, here, 1)

    each_image(mlp_near)

    def mlp_rest(i):
        ag_pass(MLP, i)
        ag_rest(MLP, i)
        mlp_half(i, there, 0)
        rs_pass(MLP, i)

    each_image(mlp_rest)

    def mlp_end(i):
        mid[i] = (ymid[i] + rs_take(MLP, i)).astype(BF16)

        @pl.when(s == 0)
        def _():
            mid_copy(i).start()

        @pl.when(s == 1)
        def _():
            out_ref[i] = mid[i]
            out_copy(i).start()

    each_image(mlp_end)

    def take_grad(i):
        mid_copy(i).wait_send()
        grad_copy(i).wait_recv()
        gath[DMLP, i, own, :] = gin[i]
        ag_start(DMLP, i)

    @pl.when(s == 0)
    def _():
        each_image(take_grad)

    @pl.when(s == 1)
    def _():
        def keep_cot(i):
            gin[i] = cot_ref[i]

        each_image(keep_cot)

    def dmlp_half(i, half, which):
        dact = mm_nt(gath[DMLP, i, half_of(half), :], w2_ref[...])
        dh[i, half_of(half), :] = (dact * dgel[i, half_of(half), :]).astype(BF16)
        rs_give(DMLP, i, which, mm_nt(dh[i, half_of(half), :], w1_ref[...]))

    def dmlp_near(i):
        ag_near(DMLP, i)
        dmlp_half(i, here, 1)

    each_image(dmlp_near)

    def dmlp_rest(i):
        @pl.when(s == 0)
        def _():
            ag_pass(DMLP, i)

        ag_rest(DMLP, i)
        dmlp_half(i, there, 0)
        rs_pass(DMLP, i)

    each_image(dmlp_rest)

    tokens = count * seq

    def weight_grad(k, right, dst):
        left = gath[k].reshape(tokens, width)
        dst[...] = mm_tn(left, right.reshape(tokens, right.shape[-1])).astype(BF16)

    weight_grad(MLP, dh[...], g1_ref)

    def dmlp_end(i):
        grad = gin[i].astype(F32) + norm_back(rs_take(DMLP, i), 1, i)
        dy1[i] = grad
        gath[DATT, i, own, :] = grad.astype(BF16)
        ag_start(DATT, i)

    each_image(dmlp_end)

    weight_grad(DMLP, act[...], g2_ref)

    def datt_part(i, half):
        datt[i, half_of(half), :] = mm_nt(gath[DATT, i, half_of(half), :], wo_ref[...]).astype(BF16)

    def datt_near(i):
        ag_near(DATT, i)
        datt_part(i, here)

    each_image(datt_near)

    def datt_rest(i):
        ag_pass(DATT, i)
        ag_rest(DATT, i)
        datt_part(i, there)
        acc[...] = jnp.zeros_like(acc)
        for h, (lo, hi, start, stop) in enumerate(windows):
            q = only(qkv[0, i, :, lo:hi], start, stop)
            k = only(qkv[1, i, :, lo:hi], start, stop)
            d = only(datt[i, :, lo:hi], start, stop)
            p = prob[i, h]
            dp = mm_nt(d, qkv[2, i, :, lo:hi])
            inner = jnp.sum(p * dp, axis=-1, keepdims=True)
            ds = (p * (dp - inner)).astype(BF16)

            @pl.when(i == 0)
            def _():
                dsum[h] = ds.astype(F32)

            @pl.when(i > 0)
            def _():
                dsum[h] += ds.astype(F32)

            acc[0, :, lo:hi] += mm(ds, k)
            acc[1, :, lo:hi] += mm_tn(ds, q)
            acc[2, :, lo:hi] += mm_tn(p.astype(BF16), d)
        for c, by in enumerate((scale, scale, 1.0)):
            part = (acc[c] * by).astype(BF16)
            dqkv[c, i] = part
            tok_ref[i, c : c + 1, :] = jnp.sum(part.astype(F32), axis=0, keepdims=True)
        for which, half in ((0, there), (1, here)):
            rs_give(
                DATT, i, which,
                sum(mm(dqkv[c, i, half_of(half), :], wq_ref[c]) for c in range(3)),
            )
        rs_pass(DATT, i)

    each_image(datt_rest)

    left = gath[ATT].reshape(tokens, width)
    for c in range(3):
        gq_ref[c] = mm_tn(left, dqkv[c].reshape(tokens, local)).astype(BF16)

    def datt_end(i):
        grad = dy1[i] + norm_back(rs_take(DATT, i), 0, i)
        ig_ref[i] = grad.astype(BF16)

        @pl.when(s == 1)
        def _():
            grad_copy(i).start()

    each_image(datt_end)

    weight_grad(DATT, att[...], go_ref)

    def fold(h, carry):
        total = jnp.zeros((grid, 2 * seq), F32)
        for r in range(grid):
            part = dsum[h, r * grid : (r + 1) * grid, :]
            wide = jnp.concatenate([part, jnp.zeros_like(part)], axis=1)
            shift = grid * (grid - 1 - r)
            total += wide if shift == 0 else pltpu.roll(wide, shift, 1)
        fold_ref[h] = total
        return carry

    lax.fori_loop(0, heads, fold, 0)

    def finish(i):
        for k in range(4):
            ag_done(k, i)
            rs_done(k, i)

        @pl.when(s == 0)
        def _():
            out_copy(i).wait_recv()

        @pl.when(s == 1)
        def _():
            out_copy(i).wait_send()
            grad_copy(i).wait_send()

    each_image(finish)


def run_block(x, cot, wq, wo, w1, w2, tp, gain, shift, tx, seq):
    count, rows, width = x.shape
    heads = tx.shape[0]
    local = wo.shape[0]
    hidden = w1.shape[1]
    dims = (count, rows, seq, heads)
    out_shape = [
        jax.ShapeDtypeStruct((count, rows, width), BF16),
        jax.ShapeDtypeStruct((count, rows, width), BF16),
        jax.ShapeDtypeStruct((3, width, local), BF16),
        jax.ShapeDtypeStruct((width, local), BF16),
        jax.ShapeDtypeStruct((width, hidden), BF16),
        jax.ShapeDtypeStruct((width, hidden), BF16),
        jax.ShapeDtypeStruct((count, 3, local), F32),
        jax.ShapeDtypeStruct(tx.shape, F32),
        jax.ShapeDtypeStruct((4, width), F32),
    ]
    vm = pltpu.VMEM
    dma = pltpu.SemaphoreType.DMA
    scratch = [
        vm((count, rows, width), BF16),
        vm((count, rows, width), BF16),
        vm((count, rows, width), BF16),
        vm((4, count, seq, width), BF16),
        vm((count, 2, 2 * rows, width), F32),
        vm((4, count, 2, rows, width), BF16),
        vm((4, count, rows, width), BF16),
        vm((4, count, 2, rows, width), BF16),
        vm((4, count, rows, width), BF16),
        vm((heads, seq, seq), F32),
        vm((count, heads, seq, seq), F32),
        vm((3, count, seq, local), BF16),
        vm((count, seq, local), BF16),
        vm((count, seq, hidden), BF16),
        vm((count, seq, hidden), F32),
        vm((2, count, rows, width), F32),
        vm((2, count, rows, 128), F32),
        vm((count, rows, width), F32),
        vm((count, rows, width), F32),
        vm((3, count, seq, local), BF16),
        vm((count, seq, hidden), BF16),
        vm((count, seq, local), BF16),
        vm((3, seq, local), F32),
        vm((heads, seq, seq), F32),
        dma((4, count, 3)),
        dma((4, count, 3)),
        dma((4, count, 3)),
        dma((4, count, 3)),
        dma((3, count)),
        dma((3, count)),
    ]
    whole = pl.BlockSpec(memory_space=pltpu.VMEM)
    return pl.pallas_call(
        functools.partial(block_kernel, dims),
        out_shape=out_shape,
        in_specs=[whole] * 10,
        out_specs=[whole] * len(out_shape),
        scratch_shapes=scratch,
        compiler_params=pltpu.CompilerParams(
            collective_id=0, has_side_effects=True, vmem_limit_bytes=62 * 2**20
        ),
        name="blocks",
    )(x, cot, wq, wo, w1, w2, tp, gain, shift, tx)


def offset_buckets(rel_index):
    seq = rel_index.shape[0]
    grid = int(round(seq**0.5))
    cells = rel_index.reshape(grid, grid, grid, grid)
    after = jnp.transpose(cells[0], (1, 0, 2))
    before = jnp.flip(cells[1:, :, 0, :], axis=0)
    by_row = jnp.concatenate([before, after], axis=0)
    right = by_row[:, 0, :]
    left = jnp.flip(by_row[:, 1:, 0], axis=1)
    return jnp.concatenate([left, right], axis=1)


def spread_table(table, chosen):
    heads, buckets = table.shape
    span = int(round(buckets**0.5))
    grid = (span + 1) // 2
    by_offset = jnp.dot(table, chosen.T, precision=lax.Precision.HIGHEST).reshape(heads, span, span)
    cols = jnp.stack([by_offset[:, :, grid - 1 - c : span - c] for c in range(grid)], axis=1)
    cols = jnp.pad(cols, ((0, 0), (0, 0), (0, 1), (0, 0)))
    return cols.reshape(heads, grid, (span + 1) * grid)


def gather_table(folded, chosen):
    heads, grid, _ = folded.shape
    span = 2 * grid - 1
    cols = folded.reshape(heads, grid, span + 1, grid)[:, :, :span]
    offsets = sum(jnp.pad(cols[:, c], ((0, 0), (0, 0), (grid - 1 - c, c))) for c in range(grid))
    flat = offsets.reshape(heads, span * span)
    return jnp.dot(chosen.T, flat.T, precision=lax.Precision.HIGHEST)


def per_device(
    images, timesteps, t_table, rel_index, w_qkv, w_time, w_out, w_fc1, w_fc2, rel_table,
    norm_gain, norm_shift, cotangent,
):
    seq = rel_index.shape[0]
    buckets = offset_buckets(rel_index).reshape(-1, 1)
    chosen = (buckets == jnp.arange(rel_table.shape[1])[None, :]).astype(F32)
    tx = spread_table(rel_table[0].T, chosen)
    embedded = t_table[timesteps]
    wq = jnp.transpose(w_qkv[0], (1, 2, 0))
    wt = jnp.transpose(w_time[0], (1, 2, 0))
    tp = jnp.einsum("id,cjd->icj", embedded, wt, preferred_element_type=F32)
    output, in_grad, gq, go, g1, g2, tok, folded, small = run_block(
        images, cotangent, wq, w_out[0], w_fc1[0], w_fc2[0], tp, norm_gain[0], norm_shift[0], tx, seq
    )

    def scatter(grad, axis):
        return lax.psum_scatter(grad, "dp", scatter_dimension=axis, tiled=True).astype(F32)

    g_qkv = jnp.transpose(scatter(gq, 1), (1, 0, 2))[None]
    g_fc1 = scatter(g1, 0)[None]
    g_fc2 = scatter(g2, 0).T[None]
    g_out = scatter(go, 0).T[None]
    all_sums = lax.all_gather(tok, "dp", axis=0, tiled=True)
    all_embedded = lax.all_gather(embedded, "dp", axis=0, tiled=True)
    cut = embedded.shape[1] // lax.axis_size("dp")
    mine = lax.dynamic_slice_in_dim(all_embedded, lax.axis_index("dp") * cut, cut, axis=1)
    g_time = jnp.einsum(
        "id,icj->dcj", mine.astype(F32), all_sums, precision=lax.Precision.HIGHEST
    )[None]
    g_table = lax.psum(gather_table(folded, chosen), "dp")[None]
    small = lax.psum(small, ("tensor", "dp"))
    return (
        output, in_grad[None], g_qkv, g_time, g_out, g_fc1, g_fc2, g_table,
        small[None, :2], small[None, 2:],
    )


def solution(mesh):
    in_specs = (
        P("dp", "tensor", None),
        P("dp"),
        P(),
        P(),
        P("section", None, None, "tensor"),
        P("section", None, None, "tensor"),
        P("section", "tensor", None),
        P("section", None, "tensor"),
        P("section", "tensor", None),
        P("section", None, "tensor"),
        P("section", None, None),
        P("section", None, None),
        P("dp", "tensor", None),
    )
    out_specs = (
        P("dp", "tensor", None),
        P("section", "dp", "tensor", None),
        P("section", "dp", None, "tensor"),
        P("section", "dp", None, "tensor"),
        P("section", "tensor", "dp"),
        P("section", "dp", "tensor"),
        P("section", "tensor", "dp"),
        P("section", None, "tensor"),
        P("section", None, None),
        P("section", None, None),
    )
    return jax.shard_map(
        per_device, mesh=mesh, in_specs=in_specs, out_specs=out_specs, check_vma=False
    )
```

```python
import functools

import jax
import jax.numpy as jnp
from jax import lax
from jax.experimental import pallas as pl
from jax.experimental.pallas import tpu as pltpu
from jax.sharding import PartitionSpec as P

MESH = pl.DeviceIdType.MESH
F32 = jnp.float32
BF16 = jnp.bfloat16
EPS = 1e-06
GELU_A = 0.7978845608028654
GELU_B = 0.044715
ATT, MLP, DMLP, DATT = range(4)


def mm(a, b):
    return lax.dot_general(a, b, (((1,), (0,)), ((), ())), preferred_element_type=F32)


def mm_nt(a, b):
    return lax.dot_general(a, b, (((1,), (1,)), ((), ())), preferred_element_type=F32)


def mm_tn(a, b):
    return lax.dot_general(a, b, (((0,), (0,)), ((), ())), preferred_element_type=F32)


def head_windows(heads, local):
    width = local // heads
    found = []
    for h in range(heads):
        lo = h * width // 128 * 128
        hi = min(-(-(h + 1) * width // 128) * 128, local)
        found.append((lo, hi, h * width - lo, (h + 1) * width - lo))
    return found


def only(x, start, stop):
    lane = lax.broadcasted_iota(jnp.int32, x.shape, 1)
    return jnp.where((lane >= start) & (lane < stop), x, jnp.zeros_like(x))


def in_thirds(x):
    high = x.astype(BF16)
    rest = x - high.astype(F32)
    middle = rest.astype(BF16)
    low = (rest - middle.astype(F32)).astype(BF16)
    return jnp.concatenate([high, middle, low], axis=0)


def add_thirds(x):
    rows = x.shape[0] // 3
    return x[:rows] + x[rows : 2 * rows] + x[2 * rows :]


def wider(x, lanes):
    return jnp.concatenate([x, jnp.zeros((x.shape[0], lanes - x.shape[1]), x.dtype)], axis=1)


def block_kernel(
    cfg,
    x_ref, cot_ref, wq_hbm, wt_hbm, wo_hbm, w1_hbm, w2_hbm, temb_ref, gain_ref, shift_ref, rel_ref, tab_ref,
    out_ref, ig_ref, tot_ref, tok_ref, emb_ref, gtab_ref, small_ref,
    wq_ref, wt_ref, wo_ref, w1_ref, w2_ref, tp_ref, tx_ref, chosen, tab, partial, arrived,
    tiny_s, small_r,
    xin, gin, mid, gath, keep, rcv_c, rcv_y, snd_c, snd_y, bias, prob, qkv, att, act, dgel,
    xhat, inv, ymid, dy1, dqkv, dh, datt, acc, turned, far_att,
    load_s, ag_s, ag_r, rs_s, rs_r, sec_s, sec_r, ch_s, ch_r, ti_s, ti_r, sm_s, sm_r,
):
    count, rows, seq, heads, ring, chained = cfg
    half_rows = 2 * rows
    width = x_ref.shape[-1]
    local = wo_ref.shape[0]
    grid = int(round(seq**0.5))
    windows = head_windows(heads, local)
    scale = (local // heads) ** (-0.5)
    blocks = partial.shape[1] if chained else tot_ref.shape[1]
    cut = width // blocks
    lanes = dqkv.shape[-1]
    parts = partial if chained else tot_ref

    s = lax.axis_index("section")
    t = lax.axis_index("tensor")
    z = lax.axis_index("dp")
    core = t + 1 - 2 * (t % 2)
    far = (t + 2) % 4
    fcore = (core + 2) % 4
    here = t // 2
    there = 1 - here
    own = pl.ds(pl.multiple_of(t * rows, rows), rows)

    loads = [
        pltpu.make_async_copy(src, dst, load_s.at[n])
        for n, (src, dst) in enumerate(
            ((wt_hbm, wt_ref), (wq_hbm, wq_ref), (wo_hbm, wo_ref), (w1_hbm, w1_ref), (w2_hbm, w2_ref))
        )
    ]
    for load in loads:
        load.start()

    barrier = pltpu.get_barrier_semaphore()
    for peer in ({"tensor": core}, {"tensor": far}, {"tensor": fcore}, {"section": 1 - s}):
        pl.semaphore_signal(barrier, inc=1, device_id=peer, device_id_type=MESH)

    def greet(j, carry):
        pl.semaphore_signal(barrier, inc=1, device_id={"dp": (z + j) % ring}, device_id_type=MESH)
        return carry

    lax.fori_loop(1, ring, greet, 0)
    pl.semaphore_wait(barrier, 3 + ring)

    def rows_of(owner):
        return pl.ds(pl.multiple_of(owner * rows, rows), rows)

    def half_of(half):
        return pl.ds(pl.multiple_of(half * half_rows, half_rows), half_rows)

    def ag_copy(k, i, which):
        owner, to = ((t, core), (t, far), (far, core))[which]
        ref = gath.at[k, i, rows_of(owner), :]
        return pltpu.make_async_remote_copy(
            src_ref=ref, dst_ref=ref, send_sem=ag_s.at[k, i, which], recv_sem=ag_r.at[k, i, which],
            device_id={"tensor": to}, device_id_type=MESH,
        )

    def ag_start(k, i):
        ag_copy(k, i, 1).start()
        ag_copy(k, i, 0).start()

    def ag_near(k, i):
        ag_copy(k, i, 0).wait_recv()

    def ag_pass(k, i):
        ag_copy(k, i, 1).wait_recv()
        ag_copy(k, i, 2).start()

    def ag_rest(k, i):
        ag_copy(k, i, 2).wait_recv()

    def ag_done(k, i):
        for which in range(3):
            ag_copy(k, i, which).wait_send()

    def rs_copy(k, i, which):
        if which < 2:
            src, dst, to = snd_c.at[k % 2, i, which], rcv_c.at[k % 2, i, which], core
        else:
            src, dst, to = snd_y.at[k % 2, i], rcv_y.at[k % 2, i], far
        return pltpu.make_async_remote_copy(
            src_ref=src, dst_ref=dst, send_sem=rs_s.at[k, i, which], recv_sem=rs_r.at[k, i, which],
            device_id={"tensor": to}, device_id_type=MESH,
        )

    mine = pl.ds(pl.multiple_of((t % 2) * rows, rows), rows)
    other = pl.ds(pl.multiple_of((1 - t % 2) * rows, rows), rows)

    def rs_give(k, i, which, part):
        keep[i, which] = part
        snd_c[k % 2, i, which] = keep[i, which, other, :].astype(BF16)
        rs_copy(k, i, which).start()

    def rs_pass(k, i):
        rs_copy(k, i, 0).wait_recv()
        snd_y[k % 2, i] = (keep[i, 0, mine, :] + rcv_c[k % 2, i, 0].astype(F32)).astype(BF16)
        rs_copy(k, i, 2).start()

    def rs_take(k, i):
        rs_copy(k, i, 1).wait_recv()
        near = keep[i, 1, mine, :] + rcv_c[k % 2, i, 1].astype(F32)
        rs_copy(k, i, 2).wait_recv()
        return near + rcv_y[k % 2, i].astype(F32)

    def rs_done(k, i):
        for which in range(3):
            rs_copy(k, i, which).wait_send()

    def sec_copy(j, src, dst):
        return lambda i: pltpu.make_async_remote_copy(
            src_ref=src.at[i], dst_ref=dst.at[i], send_sem=sec_s.at[j, i], recv_sem=sec_r.at[j, i],
            device_id={"section": 1 - s}, device_id_type=MESH,
        )

    mid_copy = sec_copy(0, mid, xin)
    grad_copy = sec_copy(1, ig_ref, gin)
    out_copy = sec_copy(2, out_ref, out_ref)

    def tiny_copy(n, j):
        ref = (emb_ref, tok_ref)[n]
        return pltpu.make_async_remote_copy(
            src_ref=ref.at[z], dst_ref=ref.at[z], send_sem=ti_s.at[n, j], recv_sem=ti_r.at[n, j],
            device_id={"dp": (z + j) % ring}, device_id_type=MESH,
        )

    def over_ring(body):
        def run(j, carry):
            body(j)
            return carry

        lax.fori_loop(1, ring, run, 0)

    def small_copy(n, j):
        return pltpu.make_async_remote_copy(
            src_ref=tiny_s.at[n], dst_ref=small_r.at[n, j], send_sem=sm_s.at[n, j], recv_sem=sm_r.at[n, j],
            device_id={"tensor": (core, far, fcore)[j]}, device_id_type=MESH,
        )

    def chain_copy(w, b, right):
        slot = b if right else b + (ring - b) * ((b + 1) // z)
        return pltpu.make_async_remote_copy(
            src_ref=partial.at[w, b], dst_ref=arrived.at[w, slot], send_sem=ch_s.at[w, b],
            recv_sem=ch_r.at[w, slot], device_id={"dp": z + 1 if right else z - 1}, device_id_type=MESH,
        )

    def arrival(w, slot):
        ref = arrived.at[w, slot]
        return pltpu.make_async_remote_copy(
            src_ref=partial.at[w, 0], dst_ref=ref, send_sem=ch_s.at[w, 0], recv_sem=ch_r.at[w, slot],
            device_id={"dp": (z + 1) % ring}, device_id_type=MESH,
        )

    flip = (2 * z) // ring

    def by_distance(body):
        def run(j, carry):
            body(flip * j + (1 - flip) * (blocks - 1 - j))
            return carry

        lax.fori_loop(0, blocks, run, 0)

    def give_blocks(w, block_of):
        def one(b):
            parts[w, b] = block_of(pl.ds(pl.multiple_of(b * cut, cut), cut))
            if chained:

                @pl.when((z == 0) & (b > 0))
                def _():
                    chain_copy(w, b, True).start()

                @pl.when((z == ring - 1) & (b < ring - 1))
                def _():
                    chain_copy(w, b, False).start()

        by_distance(one)

    def relay(w):
        def one(b):
            def add():
                arrival(w, b).wait_recv()
                partial[w, b] = (partial[w, b].astype(F32) + arrived[w, b].astype(F32)).astype(BF16)

            @pl.when((z > 0) & (b > z))
            def _():
                add()
                chain_copy(w, b, True).start()

            @pl.when((z < ring - 1) & (b < z))
            def _():
                add()
                chain_copy(w, b, False).start()

        by_distance(one)

    def settle(w):
        tot_ref[w] = partial[w, z]

        @pl.when(z > 0)
        def _():
            arrival(w, z).wait_recv()
            tot_ref[w] = (tot_ref[w].astype(F32) + arrived[w, z].astype(F32)).astype(BF16)

        @pl.when(z < ring - 1)
        def _():
            arrival(w, ring).wait_recv()
            tot_ref[w] = (tot_ref[w].astype(F32) + arrived[w, ring].astype(F32)).astype(BF16)

    def chain_done(w):
        def one(b):
            @pl.when(b > z)
            def _():
                chain_copy(w, b, True).wait_send()

            @pl.when(b < z)
            def _():
                chain_copy(w, b, False).wait_send()

        by_distance(one)

    def turn(k, n):
        for i in range(count):
            turned[n, :, i * seq : (i + 1) * seq] = gath[k, i].T

    def each_image(body):
        def run(i, carry):
            body(i)
            return carry

        lax.fori_loop(0, count, run, 0)

    def norm(x, which, i):
        mean = jnp.mean(x, axis=-1, keepdims=True)
        centre = x - mean
        root = lax.rsqrt(jnp.mean(centre * centre, axis=-1, keepdims=True) + EPS)
        hat = centre * root
        xhat[which, i] = hat
        inv[which, i] = jnp.broadcast_to(root, (rows, 128))
        return (hat * gain_ref[which : which + 1, :] + shift_ref[which : which + 1, :]).astype(BF16)

    def norm_back(da, which, i):
        hat = xhat[which, i]
        tiny_s[0, which : which + 1, :] += jnp.sum(da * hat, axis=0, keepdims=True)
        tiny_s[0, 2 + which : 3 + which, :] += jnp.sum(da, axis=0, keepdims=True)
        dhat = da * gain_ref[which : which + 1, :]
        m1 = jnp.mean(dhat, axis=-1, keepdims=True)
        m2 = jnp.mean(dhat * hat, axis=-1, keepdims=True)
        return inv[which, i][:, :1] * (dhat - m1 - hat * m2)

    tiny_s[...] = jnp.zeros_like(tiny_s)
    tok_ref[z] = jnp.zeros_like(tok_ref[z])
    emb_ref[z] = jnp.zeros_like(emb_ref[z])
    emb_ref[z, :count, :] = temb_ref[...].astype(F32)
    over_ring(lambda j: tiny_copy(0, j).start())

    @pl.when(s == 1)
    def _():
        def begin(i):
            gath[DMLP, i, own, :] = cot_ref[i]
            ag_start(DMLP, i)

        each_image(begin)

    def take_input(i):
        @pl.when(s == 0)
        def _():
            xin[i] = x_ref[i]

        @pl.when(s == 1)
        def _():
            mid_copy(i).wait_recv()

        gath[ATT, i, own, :] = norm(xin[i].astype(F32), 0, i)
        ag_start(ATT, i)

    lane = lax.broadcasted_iota(jnp.int32, (1, 2 * seq), 1)

    def tables():
        valid = lane < (2 * grid - 1) * grid
        slab = pltpu.roll(wider(rel_ref[:grid, :], 2 * seq), grid * (grid - 1), 1)
        for k in range(grid - 1):
            r = grid - 1 - k
            block = only(rel_ref[r * grid : (r + 1) * grid, :128], 0, grid)
            slab += pltpu.roll(wider(block, 2 * seq), k * grid, 1)
        none = jnp.full((1, 2 * seq), -1, jnp.int32)
        before = none
        for c in range(1, grid):
            moved = pltpu.roll(slab[c : c + 1, :], grid - c, 1)
            before = jnp.where((lane % grid == grid - c) & valid, moved, before)
        order = jnp.concatenate([jnp.where(valid, slab[:1, :], none), before], axis=1)
        step = 128
        for r in range(0, chosen.shape[0], step):
            bucket = r + lax.broadcasted_iota(jnp.int32, (step, 4 * seq), 0)
            chosen[r : r + step, :] = jnp.where(bucket == order, 1.0, 0.0).astype(BF16)
        tab[...] = jnp.zeros_like(tab)
        tab[:heads, : tab_ref.shape[1]] = tab_ref[...]
        found = add_thirds(mm(in_thirds(tab[...]), chosen[...]))
        after, before = found[:, : 2 * seq], found[:, 2 * seq :]
        for c in range(grid):
            low = pltpu.roll(after, c, 1) if c else after
            high = pltpu.roll(before, 2 * seq - (grid - c), 1)
            row = jnp.where(lane % grid >= c, low, high)
            for h in range(heads):
                tx_ref[h, c : c + 1, :] = row[h : h + 1, :]

        def expand(h, carry):
            for r in range(grid):
                shift = (2 * seq - grid * (grid - 1 - r)) % (2 * seq)
                bias[h, r * grid : (r + 1) * grid, :] = pltpu.roll(tx_ref[h], shift, 1)[:, :seq]
            return carry

        lax.fori_loop(0, heads, expand, 0)
        loads[0].wait()
        tp_ref[...] = jnp.zeros_like(tp_ref)
        emb = jnp.concatenate([temb_ref[...], jnp.zeros((16 - count, width), BF16)], axis=0)
        for c in range(3):
            tp_ref[c] = mm_nt(emb, wt_ref[c * local : (c + 1) * local, :])

    @pl.when(s == 1)
    def _():
        tables()
        each_image(lambda i: ag_pass(DMLP, i))

    each_image(take_input)

    @pl.when(s == 0)
    def _():
        tables()

    loads[1].wait()
    loads[2].wait()

    def project(i, half):
        a = gath[ATT, i, half_of(half), :]
        for c in range(3):
            part = mm_nt(a, wq_ref[c * local : (c + 1) * local, :])
            qkv[c, i, half_of(half), :] = (part + tp_ref[c, pl.ds(i, 1), :]).astype(BF16)

    def att_near(i):
        ag_near(ATT, i)
        project(i, here)

    each_image(att_near)

    def att_rest(i):
        ag_pass(ATT, i)
        ag_rest(ATT, i)
        project(i, there)
        acc[0] = jnp.zeros_like(acc[0])
        for h, (lo, hi, start, stop) in enumerate(windows):
            q = only(qkv[0, i, :, lo:hi], start, stop)
            scores = mm_nt(q, qkv[1, i, :, lo:hi]) * scale + bias[h]
            top = jnp.max(scores, axis=-1, keepdims=True)
            expo = jnp.exp(scores - top)
            p = expo / jnp.sum(expo, axis=-1, keepdims=True)
            prob[i, h] = p
            acc[0, :, lo:hi] += mm(p.astype(BF16), only(qkv[2, i, :, lo:hi], start, stop))
        att[i] = acc[0, :, :local].astype(BF16)
        far_att[i] = pltpu.roll(acc[0], far_att.shape[-1] - local, 1).astype(BF16)
        rs_give(ATT, i, 0, mm(att[i, half_of(there), :], wo_ref[...]))
        rs_give(ATT, i, 1, mm(att[i, half_of(here), :], wo_ref[...]))
        rs_pass(ATT, i)

    each_image(att_rest)

    def att_end(i):
        y = xin[i].astype(F32) + rs_take(ATT, i)
        ymid[i] = y
        gath[MLP, i, own, :] = norm(y, 1, i)
        ag_start(MLP, i)

    each_image(att_end)

    loads[3].wait()
    loads[4].wait()

    def mlp_half(i, half, which):
        a = gath[MLP, i, half_of(half), :]
        v = mm(a, w1_ref[...])
        th = jnp.tanh(GELU_A * (v + GELU_B * (v * v * v)))
        up = 0.5 * (1.0 + th)
        act[i, half_of(half), :] = (v * up).astype(BF16)
        dgel[i, half_of(half), :] = up + (0.5 * GELU_A) * v * (1.0 - th * th) * (
            1.0 + (3.0 * GELU_B) * (v * v)
        )
        rs_give(MLP, i, which, mm(act[i, half_of(half), :], w2_ref[...]))

    def mlp_near(i):
        ag_near(MLP, i)
        mlp_half(i, here, 1)

    each_image(mlp_near)

    def mlp_rest(i):
        ag_pass(MLP, i)
        ag_rest(MLP, i)
        mlp_half(i, there, 0)
        rs_pass(MLP, i)

    each_image(mlp_rest)

    tokens = count * seq

    def give_fc2():
        turn(DMLP, 0)
        give_blocks(0, lambda at: mm(turned[0, at, :], act[...].reshape(tokens, -1)).astype(BF16))

    @pl.when(s == 1)
    def _():
        each_image(lambda i: (ag_near(DMLP, i), ag_rest(DMLP, i)))
        give_fc2()

    def mlp_end(i):
        mid[i] = (ymid[i] + rs_take(MLP, i)).astype(BF16)

        @pl.when(s == 0)
        def _():
            mid_copy(i).start()

        @pl.when(s == 1)
        def _():
            out_ref[i] = mid[i]
            out_copy(i).start()

    each_image(mlp_end)

    def take_grad(i):
        mid_copy(i).wait_send()
        grad_copy(i).wait_recv()
        gath[DMLP, i, own, :] = gin[i]
        ag_start(DMLP, i)

    @pl.when(s == 0)
    def _():
        each_image(take_grad)

    @pl.when(s == 1)
    def _():
        def keep_cot(i):
            gin[i] = cot_ref[i]

        each_image(keep_cot)

    def dmlp_half(i, half, which):
        dact = mm_nt(gath[DMLP, i, half_of(half), :], w2_ref[...])
        dh[i, half_of(half), :] = (dact * dgel[i, half_of(half), :]).astype(BF16)
        rs_give(DMLP, i, which, mm_nt(dh[i, half_of(half), :], w1_ref[...]))

    def dmlp_near(i):
        rs_done(ATT, i)

        @pl.when(s == 0)
        def _():
            ag_near(DMLP, i)

        dmlp_half(i, here, 1)

    each_image(dmlp_near)

    def dmlp_rest(i):
        @pl.when(s == 0)
        def _():
            ag_pass(DMLP, i)
            ag_rest(DMLP, i)

        dmlp_half(i, there, 0)
        rs_pass(DMLP, i)

    each_image(dmlp_rest)

    turn(MLP, 1)
    give_blocks(1, lambda at: mm(turned[1, at, :], dh[...].reshape(tokens, -1)).astype(BF16))

    def dmlp_end(i):
        grad = gin[i].astype(F32) + norm_back(rs_take(DMLP, i), 1, i)
        dy1[i] = grad
        gath[DATT, i, own, :] = grad.astype(BF16)
        ag_start(DATT, i)

    each_image(dmlp_end)

    @pl.when(s == 0)
    def _():
        give_fc2()

    def datt_part(i, half):
        datt[i, half_of(half), :] = mm_nt(gath[DATT, i, half_of(half), :], wo_ref[...]).astype(BF16)

    def datt_near(i):
        rs_done(MLP, i)
        ag_near(DATT, i)
        datt_part(i, here)

    each_image(datt_near)

    def datt_rest(i):
        ag_pass(DATT, i)
        ag_rest(DATT, i)
        datt_part(i, there)
        acc[...] = jnp.zeros_like(acc)
        for h, (lo, hi, start, stop) in enumerate(windows):
            q = only(qkv[0, i, :, lo:hi], start, stop)
            k = only(qkv[1, i, :, lo:hi], start, stop)
            d = only(datt[i, :, lo:hi], start, stop)
            p = prob[i, h]
            dp = mm_nt(d, qkv[2, i, :, lo:hi])
            inner = jnp.sum(p * dp, axis=-1, keepdims=True)
            ds = (p * (dp - inner)).astype(BF16)

            @pl.when(i == 0)
            def _():
                bias[h] = ds.astype(F32)

            @pl.when(i > 0)
            def _():
                bias[h] += ds.astype(F32)

            acc[0, :, lo:hi] += mm(ds, k)
            acc[1, :, lo:hi] += mm_tn(ds, q)
            acc[2, :, lo:hi] += mm_tn(p.astype(BF16), d)
        total = jnp.zeros((seq, lanes), F32)
        for c, by in enumerate((scale, scale, 1.0)):
            lo = c * local // 128 * 128
            moved = acc[c] * by
            if c * local > lo:
                moved = pltpu.roll(moved, c * local - lo, 1)
            pieces = [jnp.zeros((seq, lo), F32)] * (lo > 0) + [moved]
            if lo + moved.shape[1] < lanes:
                pieces.append(jnp.zeros((seq, lanes - lo - moved.shape[1]), F32))
            total += jnp.concatenate(pieces, axis=1)
        dqkv[i] = total.astype(BF16)
        tok_ref[z, pl.ds(i, 1), :lanes] = jnp.sum(dqkv[i].astype(F32), axis=0, keepdims=True)
        for which, half in ((0, there), (1, here)):
            rs_give(DATT, i, which, mm(dqkv[i, half_of(half), : 3 * local], wq_ref[...]))
        rs_pass(DATT, i)

    each_image(datt_rest)

    turn(ATT, 0)
    turn(DATT, 1)

    def rest_block(at):
        first = mm(turned[0, at, :], dqkv[...].reshape(tokens, lanes))
        last = mm(turned[1, at, :], far_att[...].reshape(tokens, -1))
        seam = width - last.shape[1]
        over = lanes - seam
        return jnp.concatenate(
            [first[:, :seam], first[:, seam:] + last[:, :over], last[:, over:]], axis=1
        ).astype(BF16)

    give_blocks(2, rest_block)

    def datt_end(i):
        grad = dy1[i] + norm_back(rs_take(DATT, i), 0, i)
        ig_ref[i] = grad.astype(BF16)

        @pl.when(s == 1)
        def _():
            grad_copy(i).start()

    each_image(datt_end)

    for j in range(3):
        small_copy(0, j).start()

    def fold(h, carry):
        total = jnp.zeros((grid, 2 * seq), F32)
        for r in range(grid):
            part = wider(bias[h, r * grid : (r + 1) * grid, :], 2 * seq)
            shift = grid * (grid - 1 - r)
            total += part if shift == 0 else pltpu.roll(part, shift, 1)
        after = total[:1, :]
        before = jnp.zeros((1, 2 * seq), F32)
        for c in range(1, grid):
            row = total[c : c + 1, :]
            late = lane % grid >= c
            after += pltpu.roll(jnp.where(late, row, 0.0), 2 * seq - c, 1)
            before += pltpu.roll(jnp.where(late, 0.0, row), grid - c, 1)
        tok_ref[z, pl.ds(count + h, 1), : 4 * seq] = jnp.concatenate([after, before], axis=1)
        return carry

    lax.fori_loop(0, heads, fold, 0)
    for j in range(3):
        small_copy(0, j).wait_recv()
    over_tensor = tiny_s[0] + small_r[0, 0] + small_r[0, 1] + small_r[0, 2]
    row = lax.broadcasted_iota(jnp.int32, over_tensor.shape, 0)
    tok_ref[z, count + heads : count + heads + 1, :] = jnp.sum(
        jnp.where(row == t, over_tensor, 0.0), axis=0, keepdims=True
    )
    over_ring(lambda j: tiny_copy(1, j).start())
    if chained:
        for w in range(3):
            relay(w)
        settle(0)
    over_ring(lambda j: tiny_copy(1, j).wait_recv())

    def add_slot(j, total):
        return total + tok_ref[j]

    total = lax.fori_loop(0, ring, add_slot, jnp.zeros(tok_ref.shape[1:], F32))
    tiny_s[1] = total
    tab[...] = jnp.zeros_like(tab)
    tab[:heads, :] = tiny_s[1, count : count + heads, : 4 * seq]
    found = add_thirds(mm_nt(in_thirds(tab[...]), chosen[...]))
    gtab_ref[...] = found[:heads, : gtab_ref.shape[1]]
    for j in range(3):
        small_copy(1, j).start()
    for w in (1, 2) if chained else ():
        settle(w)
    for j in range(3):
        small_copy(1, j).wait_recv()
    last = count + heads
    small_ref[pl.ds(t, 1), :] = tiny_s[1, last : last + 1, :]
    for j, owner in enumerate((core, far, fcore)):
        small_ref[pl.ds(owner, 1), :] = small_r[1, j, last : last + 1, :]

    def finish(i):
        for k in range(4):
            ag_done(k, i)
        rs_done(DMLP, i)
        rs_done(DATT, i)

        @pl.when(s == 0)
        def _():
            out_copy(i).wait_recv()

        @pl.when(s == 1)
        def _():
            out_copy(i).wait_send()
            grad_copy(i).wait_send()

    each_image(finish)

    def tiny_left(j):
        tiny_copy(0, j).wait_recv()
        tiny_copy(0, j).wait_send()
        tiny_copy(1, j).wait_send()

    over_ring(tiny_left)
    for j in range(3):
        small_copy(0, j).wait_send()
        small_copy(1, j).wait_send()
    if chained:
        for w in range(3):
            chain_done(w)


def run_block(x, cot, wq, wt, wo, w1, w2, temb, gain, shift, rel, table, ring):
    count, rows, width = x.shape
    seq = rel.shape[0]
    heads = table.shape[0]
    local = wo.shape[0]
    hidden = w1.shape[1]
    chained = width // ring % 16 == 0
    blocks = ring if chained else 4
    cut = width // blocks
    padded = -(-local // 128) * 128
    lanes = -(-3 * local // 128) * 128
    dims = (count, rows, seq, heads, ring, chained)
    total = (3, cut, width) if chained else (3, blocks, cut, width)
    out_shape = [
        jax.ShapeDtypeStruct((count, rows, width), BF16),
        jax.ShapeDtypeStruct((count, rows, width), BF16),
        jax.ShapeDtypeStruct(total, BF16),
        jax.ShapeDtypeStruct((ring, 8, width), F32),
        jax.ShapeDtypeStruct((ring, 8, width), F32),
        jax.ShapeDtypeStruct(table.shape, F32),
        jax.ShapeDtypeStruct((4, width), F32),
    ]
    vm = pltpu.VMEM
    dma = pltpu.SemaphoreType.DMA
    scratch = [
        vm(wq.shape, BF16),
        vm(wt.shape, BF16),
        vm(wo.shape, BF16),
        vm(w1.shape, BF16),
        vm(w2.shape, BF16),
        vm((3, 16, local), F32),
        vm((heads, int(round(seq**0.5)), 2 * seq), F32),
        vm((4 * seq, 4 * seq), BF16),
        vm((16, 4 * seq), F32),
        vm((3, blocks, cut, width) if chained else (16, 128), BF16),
        vm((3, blocks + 1, cut, width) if chained else (16, 128), BF16),
        vm((2, 8, width), F32),
        vm((2, 3, 8, width), F32),
        vm((count, rows, width), BF16),
        vm((count, rows, width), BF16),
        vm((count, rows, width), BF16),
        vm((4, count, seq, width), BF16),
        vm((count, 2, 2 * rows, width), F32),
        vm((2, count, 2, rows, width), BF16),
        vm((2, count, rows, width), BF16),
        vm((2, count, 2, rows, width), BF16),
        vm((2, count, rows, width), BF16),
        vm((heads, seq, seq), F32),
        vm((count, heads, seq, seq), F32),
        vm((3, count, seq, local), BF16),
        vm((count, seq, local), BF16),
        vm((count, seq, hidden), BF16),
        vm((count, seq, hidden), F32),
        vm((2, count, rows, width), F32),
        vm((2, count, rows, 128), F32),
        vm((count, rows, width), F32),
        vm((count, rows, width), F32),
        vm((count, seq, lanes), BF16),
        vm((count, seq, hidden), BF16),
        vm((count, seq, local), BF16),
        vm((3, seq, padded), F32),
        vm((2, width, count * seq), BF16),
        vm((count, seq, padded), BF16),
        dma((5,)),
        dma((4, count, 3)),
        dma((4, count, 3)),
        dma((4, count, 3)),
        dma((4, count, 3)),
        dma((3, count)),
        dma((3, count)),
        dma((3, blocks)),
        dma((3, blocks + 1)),
        dma((2, ring)),
        dma((2, ring)),
        dma((2, 3)),
        dma((2, 3)),
    ]
    whole = pl.BlockSpec(memory_space=pltpu.VMEM)
    lies = pl.BlockSpec(memory_space=pl.ANY)
    return pl.pallas_call(
        functools.partial(block_kernel, dims),
        out_shape=out_shape,
        in_specs=[whole] * 2 + [lies] * 5 + [whole] * 5,
        out_specs=[whole] * len(out_shape),
        scratch_shapes=scratch,
        compiler_params=pltpu.CompilerParams(
            collective_id=0, has_side_effects=True, vmem_limit_bytes=63 * 2**20
        ),
        name="blocks",
    )(x, cot, wq, wt, wo, w1, w2, temb, gain, shift, rel, table)


def per_device(
    images, timesteps, t_table, rel_index, w_qkv, w_time, w_out, w_fc1, w_fc2, rel_table,
    norm_gain, norm_shift, cotangent,
):
    ring = lax.axis_size("dp")
    count = images.shape[0]
    width = images.shape[-1]
    local = w_out.shape[1]
    cut = width // ring
    embedded = t_table[timesteps]
    wq = jnp.transpose(w_qkv[0], (1, 2, 0)).reshape(3 * local, width)
    wt = jnp.transpose(w_time[0], (1, 2, 0)).reshape(3 * local, width)
    output, in_grad, total, sums, emb, g_table, small = run_block(
        images, cotangent, wq, wt, w_out[0], w_fc1[0], w_fc2[0], embedded, norm_gain[0], norm_shift[0],
        rel_index, rel_table[0].T, ring,
    )
    if total.ndim == 4:
        total = lax.psum_scatter(
            total.reshape(3, width, width), "dp", scatter_dimension=1, tiled=True
        )
    total = total.astype(F32)
    g_fc2 = total[0].T
    g_fc1 = total[1]
    g_qkv = total[2, :, : 3 * local].reshape(cut, 3, local)
    g_out = total[2, :, 3 * local :].T
    sums = sums[:, :count, : 3 * local].reshape(ring * count, 3, local)
    emb = emb[:, :count].reshape(ring * count, width)
    emb = lax.dynamic_slice_in_dim(emb, lax.axis_index("dp") * cut, cut, axis=1)
    g_time = jnp.einsum("id,icj->dcj", emb, sums, precision=lax.Precision.HIGHEST)
    return (
        output, in_grad[None], g_qkv[None], g_time[None], g_out[None], g_fc1[None], g_fc2[None],
        g_table.T[None], small[None, :2], small[None, 2:],
    )


def solution(mesh):
    in_specs = (
        P("dp", "tensor", None),
        P("dp"),
        P(),
        P(),
        P("section", None, None, "tensor"),
        P("section", None, None, "tensor"),
        P("section", "tensor", None),
        P("section", None, "tensor"),
        P("section", "tensor", None),
        P("section", None, "tensor"),
        P("section", None, None),
        P("section", None, None),
        P("dp", "tensor", None),
    )
    out_specs = (
        P("dp", "tensor", None),
        P("section", "dp", "tensor", None),
        P("section", "dp", None, "tensor"),
        P("section", "dp", None, "tensor"),
        P("section", "tensor", "dp"),
        P("section", "dp", "tensor"),
        P("section", "tensor", "dp"),
        P("section", None, "tensor"),
        P("section", None, None),
        P("section", None, None),
    )
    return jax.shard_map(
        per_device, mesh=mesh, in_specs=in_specs, out_specs=out_specs, check_vma=False
    )
```

```python
import functools

import jax
import jax.numpy as jnp
from jax import lax
from jax.experimental import pallas as pl
from jax.experimental.pallas import tpu as pltpu
from jax.sharding import PartitionSpec as P

MESH = pl.DeviceIdType.MESH
F32 = jnp.float32
BF16 = jnp.bfloat16
EPS = 1e-06
GELU_A = 0.7978845608028654
GELU_B = 0.044715
ATT, MLP, DMLP, DATT = range(4)


def mm(a, b):
    return lax.dot_general(a, b, (((1,), (0,)), ((), ())), preferred_element_type=F32)


def mm_nt(a, b):
    return lax.dot_general(a, b, (((1,), (1,)), ((), ())), preferred_element_type=F32)


def mm_tn(a, b):
    return lax.dot_general(a, b, (((0,), (0,)), ((), ())), preferred_element_type=F32)


def head_windows(heads, local):
    width = local // heads
    found = []
    for h in range(heads):
        lo = h * width // 128 * 128
        hi = min(-(-(h + 1) * width // 128) * 128, local)
        found.append((lo, hi, h * width - lo, (h + 1) * width - lo))
    return found


def only(x, start, stop):
    lane = lax.broadcasted_iota(jnp.int32, x.shape, 1)
    return jnp.where((lane >= start) & (lane < stop), x, jnp.zeros_like(x))


def in_thirds(x):
    high = x.astype(BF16)
    rest = x - high.astype(F32)
    middle = rest.astype(BF16)
    low = (rest - middle.astype(F32)).astype(BF16)
    return jnp.concatenate([high, middle, low], axis=0)


def add_thirds(x):
    rows = x.shape[0] // 3
    return x[:rows] + x[rows : 2 * rows] + x[2 * rows :]


def wider(x, lanes):
    return jnp.concatenate([x, jnp.zeros((x.shape[0], lanes - x.shape[1]), x.dtype)], axis=1)


def block_kernel(
    cfg,
    x_ref, cot_ref, wq_hbm, wt_hbm, wo_hbm, w1_hbm, w2_hbm, temb_ref, gain_ref, shift_ref, rel_ref, tab_ref,
    out_ref, ig_ref, tot_ref, tok_ref, emb_ref, gtab_ref, small_ref,
    wq_ref, spare, wo_ref, w1_ref, w2_ref, tp_ref, tx_ref, chosen, tab, partial, arrived,
    tiny_s, small_r,
    xin, gin, mid, gath, keep, rcv_c, rcv_y, snd_c, snd_y, bias, prob, qkv, att, act, dgel,
    xhat, inv, ymid, dqkv, dh, datt, acc, turned, far_att, act2, dh2, dqkv2, far_att2,
    load_s, ag_s, ag_r, rs_s, rs_r, sec_s, sec_r, ch_s, ch_r, fac_s, fac_r, ti_s, ti_r, sm_s, sm_r,
):
    count, rows, seq, heads, ring, chained = cfg
    half_rows = 2 * rows
    width = x_ref.shape[-1]
    local = wo_ref.shape[0]
    grid = int(round(seq**0.5))
    windows = head_windows(heads, local)
    scale = (local // heads) ** (-0.5)
    blocks = partial.shape[1] if chained else tot_ref.shape[1]
    cut = width // blocks
    pieces = partial.shape[2] if chained else 1
    slim = cut // pieces
    lanes = dqkv.shape[-1]

    s = lax.axis_index("section")
    t = lax.axis_index("tensor")
    z = lax.axis_index("dp")
    core = t + 1 - 2 * (t % 2)
    far = (t + 2) % 4
    fcore = (core + 2) % 4
    here = t // 2
    there = 1 - here
    own = pl.ds(pl.multiple_of(t * rows, rows), rows)

    wt_ref = partial.at[2, :3] if chained else spare

    loads = [
        pltpu.make_async_copy(src, dst, load_s.at[n])
        for n, (src, dst) in enumerate(
            ((wt_hbm, wt_ref), (wq_hbm, wq_ref), (wo_hbm, wo_ref), (w1_hbm, w1_ref), (w2_hbm, w2_ref))
        )
    ]
    for load in loads:
        load.start()

    barrier = pltpu.get_barrier_semaphore()
    for peer in ({"tensor": core}, {"tensor": far}, {"tensor": fcore}, {"section": 1 - s}):
        pl.semaphore_signal(barrier, inc=1, device_id=peer, device_id_type=MESH)

    def greet(j, carry):
        pl.semaphore_signal(barrier, inc=1, device_id={"dp": (z + j) % ring}, device_id_type=MESH)
        return carry

    lax.fori_loop(1, ring, greet, 0)
    pl.semaphore_wait(barrier, 3 + ring)

    def rows_of(owner):
        return pl.ds(pl.multiple_of(owner * rows, rows), rows)

    def half_of(half):
        return pl.ds(pl.multiple_of(half * half_rows, half_rows), half_rows)

    def ag_copy(k, i, which):
        owner, to = ((t, core), (t, far), (far, core))[which]
        ref = gath.at[k % 3, i, rows_of(owner), :]
        return pltpu.make_async_remote_copy(
            src_ref=ref, dst_ref=ref, send_sem=ag_s.at[k, i, which], recv_sem=ag_r.at[k, i, which],
            device_id={"tensor": to}, device_id_type=MESH,
        )

    def ag_start(k, i):
        ag_copy(k, i, 1).start()
        ag_copy(k, i, 0).start()

    def ag_near(k, i):
        ag_copy(k, i, 0).wait_recv()

    def ag_pass(k, i):
        ag_copy(k, i, 1).wait_recv()
        ag_copy(k, i, 2).start()

    def ag_rest(k, i):
        ag_copy(k, i, 2).wait_recv()

    def ag_done(k, i):
        for which in range(3):
            ag_copy(k, i, which).wait_send()

    def rs_copy(k, i, which):
        if which < 2:
            src, dst, to = snd_c.at[k % 2, i, which], rcv_c.at[k % 2, i, which], core
        else:
            src, dst, to = snd_y.at[k % 2, i], rcv_y.at[k % 2, i], far
        return pltpu.make_async_remote_copy(
            src_ref=src, dst_ref=dst, send_sem=rs_s.at[k, i, which], recv_sem=rs_r.at[k, i, which],
            device_id={"tensor": to}, device_id_type=MESH,
        )

    def rs_give(k, i, which, part):
        odd = t % 2 == 1
        low, high = part[:rows], part[rows:]
        snd_c[k % 2, i, which] = jnp.where(odd, low, high).astype(BF16)
        rs_copy(k, i, which).start()
        keep[i, which] = jnp.where(odd, high, low)

    def rs_pass(k, i):
        rs_copy(k, i, 0).wait_recv()
        snd_y[k % 2, i] = (keep[i, 0] + rcv_c[k % 2, i, 0].astype(F32)).astype(BF16)
        rs_copy(k, i, 2).start()

    def rs_take(k, i):
        rs_copy(k, i, 1).wait_recv()
        near = keep[i, 1] + rcv_c[k % 2, i, 1].astype(F32)
        rs_copy(k, i, 2).wait_recv()
        return near + rcv_y[k % 2, i].astype(F32)

    def rs_done(k, i):
        for which in range(3):
            rs_copy(k, i, which).wait_send()

    def sec_copy(j, src, dst):
        return lambda i: pltpu.make_async_remote_copy(
            src_ref=src.at[i], dst_ref=dst.at[i], send_sem=sec_s.at[j, i], recv_sem=sec_r.at[j, i],
            device_id={"section": 1 - s}, device_id_type=MESH,
        )

    mid_copy = sec_copy(0, mid, xin)
    grad_copy = sec_copy(1, ig_ref, gin)
    out_copy = sec_copy(2, out_ref, out_ref)

    def tiny_copy(n, j):
        ref = (emb_ref, tok_ref)[n]
        return pltpu.make_async_remote_copy(
            src_ref=ref.at[z], dst_ref=ref.at[z], send_sem=ti_s.at[n, j], recv_sem=ti_r.at[n, j],
            device_id={"dp": (z + j) % ring}, device_id_type=MESH,
        )

    def over_ring(body):
        def run(j, carry):
            body(j)
            return carry

        lax.fori_loop(1, ring, run, 0)

    def small_copy(n, j):
        return pltpu.make_async_remote_copy(
            src_ref=tiny_s.at[n], dst_ref=small_r.at[n, j], send_sem=sm_s.at[n, j], recv_sem=sm_r.at[n, j],
            device_id={"tensor": (core, far, fcore)[j]}, device_id_type=MESH,
        )

    mate = z + 1 - 2 * (z % 2)
    across = 3 - z
    beyond = 3 * (2 - z)
    is_end = (z == 0) | (z == 3)
    is_mate = (z == 1) | (z == 2)

    def factor_copy(n):
        if n < 4:
            src, dst = turned.at[n, t % 2], turned.at[n, count + t % 2]
        else:
            src, dst = ((act, act2), (dh, dh2), (dqkv, dqkv2), (far_att, far_att2))[n - 4]
        return pltpu.make_async_remote_copy(
            src_ref=src, dst_ref=dst, send_sem=fac_s.at[n], recv_sem=fac_r.at[n],
            device_id={"dp": mate}, device_id_type=MESH,
        )

    def share_copy(k):
        ref = turned.at[k, count + t % 2]
        return pltpu.make_async_remote_copy(
            src_ref=ref, dst_ref=ref, send_sem=fac_s.at[8 + k], recv_sem=fac_r.at[8 + k],
            device_id={"tensor": core}, device_id_type=MESH,
        )

    def give_factor(*which):
        if chained:

            @pl.when(is_end)
            def _():
                for n in which:
                    factor_copy(n).start()

    def share_factor(k):
        if chained:

            @pl.when(is_mate)
            def _():
                factor_copy(k).wait_recv()
                share_copy(k).start()

    def cross_copy(w, slot, c):
        return pltpu.make_async_remote_copy(
            src_ref=partial.at[w, (beyond, across)[slot], c], dst_ref=arrived.at[w, slot, c],
            send_sem=ch_s.at[w, slot, c], recv_sem=ch_r.at[w, slot, c],
            device_id={"dp": across}, device_id_type=MESH,
        )

    def home_copy(w, c):
        return pltpu.make_async_remote_copy(
            src_ref=partial.at[w, mate, c], dst_ref=arrived.at[w, 0, c],
            send_sem=ch_s.at[w, 2, c], recv_sem=ch_r.at[w, 0, c],
            device_id={"dp": mate}, device_id_type=MESH,
        )

    def each_piece(body):
        def run(c, carry):
            body(c)
            return carry

        lax.fori_loop(0, pieces, run, 0)

    def give_blocks(w, needs, product):
        if not chained:

            def whole(b, carry):
                tot_ref[w, b] = product(pl.ds(pl.multiple_of(b * cut, cut), cut), 0).astype(BF16)
                return carry

            lax.fori_loop(0, blocks, whole, 0)
            return

        def rows_at(b, c):
            return pl.ds(pl.multiple_of(b * cut + c * slim, slim), slim)

        def alone(b):
            def one(c):
                partial[w, b, c] = product(rows_at(b, c), 0).astype(BF16)

            each_piece(one)

        def both(b, slot=None):
            def one(c):
                at = rows_at(b, c)
                partial[w, b, c] = (product(at, 0) + product(at, 1)).astype(BF16)
                if slot is not None:
                    cross_copy(w, slot, c).start()

            each_piece(one)

        @pl.when(is_end)
        def _():
            alone(z)

        @pl.when(is_mate)
        def _():
            for n in needs:
                if n < 4:
                    share_copy(n).wait_recv()
                else:
                    factor_copy(n).wait_recv()
            both(beyond, 0)
            both(across, 1)
            both(z)
            alone(mate)

    def relay(w):
        @pl.when(is_mate)
        def _():
            def one(c):
                cross_copy(w, 0, c).wait_recv()
                partial[w, mate, c] = (
                    partial[w, mate, c].astype(F32) + arrived[w, 0, c].astype(F32)
                ).astype(BF16)
                home_copy(w, c).start()

            each_piece(one)

    def settle(w):
        def finish(slot, copy):
            def one(c):
                copy(c).wait_recv()
                tot_ref[w, c] = (partial[w, z, c].astype(F32) + arrived[w, slot, c].astype(F32)).astype(BF16)

            each_piece(one)

        @pl.when(is_mate)
        def _():
            finish(1, lambda c: cross_copy(w, 1, c))

        @pl.when(is_end)
        def _():
            finish(0, lambda c: home_copy(w, c))

    def weights_left():
        @pl.when(is_end)
        def _():
            for n in range(8):
                factor_copy(n).wait_send()

        @pl.when(is_mate)
        def _():
            for k in range(4):
                share_copy(k).wait_send()
            for w in range(3):
                for c in range(pieces):
                    cross_copy(w, 0, c).wait_send()
                    cross_copy(w, 1, c).wait_send()
                    home_copy(w, c).wait_send()

    def turn(k):
        for i in range(count):
            turned[k, i] = gath[k % 3, i].T

    def product(k, mine, theirs):
        def rows_of_product(at, side):
            right = (mine, theirs)[side]
            return sum(mm(turned[k, side * count + i, at, :], right[i]) for i in range(count))

        return rows_of_product

    def each_image(body):
        def run(i, carry):
            body(i)
            return carry

        lax.fori_loop(0, count, run, 0)

    def norm(x, which, i):
        mean = jnp.mean(x, axis=-1, keepdims=True)
        centre = x - mean
        root = lax.rsqrt(jnp.mean(centre * centre, axis=-1, keepdims=True) + EPS)
        hat = centre * root
        xhat[which, i] = hat
        inv[which, i] = jnp.broadcast_to(root, (rows, 128))
        return (hat * gain_ref[which : which + 1, :] + shift_ref[which : which + 1, :]).astype(BF16)

    def norm_back(da, which, i):
        hat = xhat[which, i]
        tiny_s[0, which : which + 1, :] += jnp.sum(da * hat, axis=0, keepdims=True)
        tiny_s[0, 2 + which : 3 + which, :] += jnp.sum(da, axis=0, keepdims=True)
        dhat = da * gain_ref[which : which + 1, :]
        m1 = jnp.mean(dhat, axis=-1, keepdims=True)
        m2 = jnp.mean(dhat * hat, axis=-1, keepdims=True)
        return inv[which, i][:, :1] * (dhat - m1 - hat * m2)

    tiny_s[...] = jnp.zeros_like(tiny_s)
    tok_ref[z] = jnp.zeros_like(tok_ref[z])
    emb_ref[z] = jnp.zeros_like(emb_ref[z])
    emb_ref[z, :count, :] = temb_ref[...].astype(F32)
    over_ring(lambda j: tiny_copy(0, j).start())

    @pl.when(s == 1)
    def _():
        def begin(i):
            gath[DMLP, i, own, :] = cot_ref[i]
            ag_start(DMLP, i)

        each_image(begin)

    def take_input(i):
        @pl.when(s == 0)
        def _():
            xin[i] = x_ref[i]

        @pl.when(s == 1)
        def _():
            mid_copy(i).wait_recv()

        gath[ATT, i, own, :] = norm(xin[i].astype(F32), 0, i)
        ag_start(ATT, i)

    lane = lax.broadcasted_iota(jnp.int32, (1, 2 * seq), 1)

    def tables():
        valid = lane < (2 * grid - 1) * grid
        slab = pltpu.roll(wider(rel_ref[:grid, :], 2 * seq), grid * (grid - 1), 1)
        for k in range(grid - 1):
            r = grid - 1 - k
            block = only(rel_ref[r * grid : (r + 1) * grid, :128], 0, grid)
            slab += pltpu.roll(wider(block, 2 * seq), k * grid, 1)
        none = jnp.full((1, 2 * seq), -1, jnp.int32)
        before = none
        for c in range(1, grid):
            moved = pltpu.roll(slab[c : c + 1, :], grid - c, 1)
            before = jnp.where((lane % grid == grid - c) & valid, moved, before)
        order = jnp.concatenate([jnp.where(valid, slab[:1, :], none), before], axis=1)
        step = 128
        for r in range(0, chosen.shape[0], step):
            bucket = r + lax.broadcasted_iota(jnp.int32, (step, 4 * seq), 0)
            chosen[r : r + step, :] = jnp.where(bucket == order, 1.0, 0.0).astype(BF16)
        tab[...] = jnp.zeros_like(tab)
        tab[:heads, : tab_ref.shape[1]] = tab_ref[...]
        found = add_thirds(mm(in_thirds(tab[...]), chosen[...]))
        after, before = found[:, : 2 * seq], found[:, 2 * seq :]
        for c in range(grid):
            low = pltpu.roll(after, c, 1) if c else after
            high = pltpu.roll(before, 2 * seq - (grid - c), 1)
            row = jnp.where(lane % grid >= c, low, high)
            for h in range(heads):
                tx_ref[h, c : c + 1, :] = row[h : h + 1, :]

        def expand(h, carry):
            for r in range(grid):
                shift = (2 * seq - grid * (grid - 1 - r)) % (2 * seq)
                bias[h, r * grid : (r + 1) * grid, :] = pltpu.roll(tx_ref[h], shift, 1)[:, :seq]
            return carry

        lax.fori_loop(0, heads, expand, 0)
        loads[0].wait()
        tp_ref[...] = jnp.zeros_like(tp_ref)
        emb = jnp.concatenate([temb_ref[...], jnp.zeros((16 - count, width), BF16)], axis=0)
        for c in range(3):
            tp_ref[c] = mm_nt(emb, wt_ref[c].reshape(local, width))

    @pl.when(s == 1)
    def _():
        tables()

        def spread_cot(i):
            ag_pass(DMLP, i)
            ag_near(DMLP, i)
            ag_rest(DMLP, i)

        each_image(spread_cot)
        turn(DMLP)
        give_factor(2)

    each_image(take_input)

    @pl.when(s == 0)
    def _():
        tables()

    loads[1].wait()
    loads[2].wait()

    def project(i, half):
        a = gath[ATT, i, half_of(half), :]
        for c in range(3):
            part = mm_nt(a, wq_ref[c * local : (c + 1) * local, :])
            qkv[c, i, half_of(half), :] = (part + tp_ref[c, pl.ds(i, 1), :]).astype(BF16)

    def att_near(i):
        ag_near(ATT, i)
        project(i, here)

    each_image(att_near)

    def att_rest(i):
        ag_pass(ATT, i)
        ag_rest(ATT, i)
        project(i, there)
        acc[0] = jnp.zeros_like(acc[0])
        for h, (lo, hi, start, stop) in enumerate(windows):
            q = only(qkv[0, i, :, lo:hi], start, stop)
            scores = mm_nt(q, qkv[1, i, :, lo:hi]) * scale + bias[h]
            top = jnp.max(scores, axis=-1, keepdims=True)
            expo = jnp.exp(scores - top)
            p = expo / jnp.sum(expo, axis=-1, keepdims=True)
            prob[i, h] = p
            acc[0, :, lo:hi] += mm(p.astype(BF16), only(qkv[2, i, :, lo:hi], start, stop))
        att[i] = acc[0, :, :local].astype(BF16)
        far_att[i] = pltpu.roll(acc[0], far_att.shape[-1] - local, 1).astype(BF16)
        rs_give(ATT, i, 0, mm(att[i, half_of(there), :], wo_ref[...]))
        rs_give(ATT, i, 1, mm(att[i, half_of(here), :], wo_ref[...]))
        rs_pass(ATT, i)

    each_image(att_rest)

    turn(ATT)
    give_factor(0, 7)

    def att_end(i):
        y = xin[i].astype(F32) + rs_take(ATT, i)
        ag_done(ATT, i)
        ymid[i] = y
        gath[MLP, i, own, :] = norm(y, 1, i)
        ag_start(MLP, i)

    each_image(att_end)

    loads[3].wait()
    loads[4].wait()

    def mlp_half(i, half, which):
        a = gath[MLP, i, half_of(half), :]
        v = mm(a, w1_ref[...])
        th = jnp.tanh(GELU_A * (v + GELU_B * (v * v * v)))
        up = 0.5 * (1.0 + th)
        act[i, half_of(half), :] = (v * up).astype(BF16)
        slope = up + (0.5 * GELU_A) * v * (1.0 - th * th) * (1.0 + (3.0 * GELU_B) * (v * v))
        dgel[i, half_of(half), :] = slope.astype(BF16)
        rs_give(MLP, i, which, mm(act[i, half_of(half), :], w2_ref[...]))

    def mlp_near(i):
        ag_near(MLP, i)
        mlp_half(i, here, 1)

    each_image(mlp_near)

    def mlp_rest(i):
        ag_pass(MLP, i)
        ag_rest(MLP, i)
        mlp_half(i, there, 0)
        rs_pass(MLP, i)

    each_image(mlp_rest)

    turn(MLP)
    give_factor(1, 4)

    def mlp_end(i):
        mid[i] = (ymid[i] + rs_take(MLP, i)).astype(BF16)

        @pl.when(s == 0)
        def _():
            mid_copy(i).start()

        @pl.when(s == 1)
        def _():
            out_ref[i] = mid[i]
            out_copy(i).start()

    each_image(mlp_end)

    def take_grad(i):
        mid_copy(i).wait_send()
        grad_copy(i).wait_recv()
        gath[DMLP, i, own, :] = gin[i]
        ag_start(DMLP, i)

    @pl.when(s == 0)
    def _():
        each_image(take_grad)

    @pl.when(s == 1)
    def _():
        def keep_cot(i):
            gin[i] = cot_ref[i]

        each_image(keep_cot)

    def dmlp_half(i, half, which):
        dact = mm_nt(gath[DMLP, i, half_of(half), :], w2_ref[...])
        dh[i, half_of(half), :] = (dact * dgel[i, half_of(half), :]).astype(BF16)
        rs_give(DMLP, i, which, mm_nt(dh[i, half_of(half), :], w1_ref[...]))

    def dmlp_near(i):
        rs_done(ATT, i)

        @pl.when(s == 0)
        def _():
            ag_near(DMLP, i)

        dmlp_half(i, here, 1)

    each_image(dmlp_near)

    def dmlp_rest(i):
        @pl.when(s == 0)
        def _():
            ag_pass(DMLP, i)
            ag_rest(DMLP, i)

        dmlp_half(i, there, 0)
        rs_pass(DMLP, i)

    each_image(dmlp_rest)

    @pl.when(s == 0)
    def _():
        turn(DMLP)
        give_factor(2)
        share_factor(ATT)
        share_factor(MLP)

    give_factor(5)

    def dmlp_end(i):
        grad = gin[i].astype(F32) + norm_back(rs_take(DMLP, i), 1, i)
        ymid[i] = grad
        gath[DATT % 3, i, own, :] = grad.astype(BF16)
        ag_start(DATT, i)

    each_image(dmlp_end)

    def job_fc2():
        give_blocks(0, (2, 4), product(DMLP, act, act2))

    def job_fc1():
        give_blocks(1, (1, 5), product(MLP, dh, dh2))

    @pl.when(s == 0)
    def _():
        share_factor(DMLP)
        job_fc2()

    def datt_part(i, half):
        datt[i, half_of(half), :] = mm_nt(gath[DATT % 3, i, half_of(half), :], wo_ref[...]).astype(BF16)

    def datt_near(i):
        rs_done(MLP, i)
        ag_near(DATT, i)
        datt_part(i, here)

    each_image(datt_near)

    def datt_rest(i):
        ag_pass(DATT, i)
        ag_rest(DATT, i)
        datt_part(i, there)
        acc[...] = jnp.zeros_like(acc)
        for h, (lo, hi, start, stop) in enumerate(windows):
            q = only(qkv[0, i, :, lo:hi], start, stop)
            k = only(qkv[1, i, :, lo:hi], start, stop)
            d = only(datt[i, :, lo:hi], start, stop)
            p = prob[i, h]
            dp = mm_nt(d, qkv[2, i, :, lo:hi])
            inner = jnp.sum(p * dp, axis=-1, keepdims=True)
            ds = (p * (dp - inner)).astype(BF16)

            @pl.when(i == 0)
            def _():
                bias[h] = ds.astype(F32)

            @pl.when(i > 0)
            def _():
                bias[h] += ds.astype(F32)

            acc[0, :, lo:hi] += mm(ds, k)
            acc[1, :, lo:hi] += mm_tn(ds, q)
            acc[2, :, lo:hi] += mm_tn(p.astype(BF16), d)
        total = jnp.zeros((seq, lanes), F32)
        for c, by in enumerate((scale, scale, 1.0)):
            lo = c * local // 128 * 128
            moved = acc[c] * by
            if c * local > lo:
                moved = pltpu.roll(moved, c * local - lo, 1)
            pieces = [jnp.zeros((seq, lo), F32)] * (lo > 0) + [moved]
            if lo + moved.shape[1] < lanes:
                pieces.append(jnp.zeros((seq, lanes - lo - moved.shape[1]), F32))
            total += jnp.concatenate(pieces, axis=1)
        dqkv[i] = total.astype(BF16)
        tok_ref[z, pl.ds(i, 1), :lanes] = jnp.sum(dqkv[i].astype(F32), axis=0, keepdims=True)
        for which, half in ((0, there), (1, here)):
            rs_give(DATT, i, which, mm(dqkv[i, half_of(half), : 3 * local], wq_ref[...]))
        rs_pass(DATT, i)

    each_image(datt_rest)

    give_factor(6)
    turn(DATT)
    give_factor(3)

    @pl.when(s == 0)
    def _():
        job_fc1()

    def datt_end(i):
        grad = ymid[i] + norm_back(rs_take(DATT, i), 0, i)
        ig_ref[i] = grad.astype(BF16)

        @pl.when(s == 1)
        def _():
            grad_copy(i).start()

    each_image(datt_end)

    for j in range(3):
        small_copy(0, j).start()

    def fold(h, carry):
        total = jnp.zeros((grid, 2 * seq), F32)
        for r in range(grid):
            part = wider(bias[h, r * grid : (r + 1) * grid, :], 2 * seq)
            shift = grid * (grid - 1 - r)
            total += part if shift == 0 else pltpu.roll(part, shift, 1)
        after = total[:1, :]
        before = jnp.zeros((1, 2 * seq), F32)
        for c in range(1, grid):
            row = total[c : c + 1, :]
            late = lane % grid >= c
            after += pltpu.roll(jnp.where(late, row, 0.0), 2 * seq - c, 1)
            before += pltpu.roll(jnp.where(late, 0.0, row), grid - c, 1)
        tok_ref[z, pl.ds(count + h, 1), : 4 * seq] = jnp.concatenate([after, before], axis=1)
        return carry

    lax.fori_loop(0, heads, fold, 0)
    for j in range(3):
        small_copy(0, j).wait_recv()
    over_tensor = tiny_s[0] + small_r[0, 0] + small_r[0, 1] + small_r[0, 2]
    row = lax.broadcasted_iota(jnp.int32, over_tensor.shape, 0)
    tok_ref[z, count + heads : count + heads + 1, :] = jnp.sum(
        jnp.where(row == t, over_tensor, 0.0), axis=0, keepdims=True
    )
    over_ring(lambda j: tiny_copy(1, j).start())

    @pl.when(s == 1)
    def _():
        share_factor(DMLP)
        share_factor(ATT)
        share_factor(MLP)
        job_fc2()
        job_fc1()

    if chained:
        relay(0)

    share_factor(DATT)
    from_qkv = product(ATT, dqkv, dqkv2)
    from_out = product(DATT, far_att, far_att2)

    def rest_product(at, side):
        first, last = from_qkv(at, side), from_out(at, side)
        seam = width - last.shape[1]
        over = lanes - seam
        return jnp.concatenate(
            [first[:, :seam], first[:, seam:] + last[:, :over], last[:, over:]], axis=1
        )

    give_blocks(2, (0, 3, 6, 7), rest_product)
    if chained:
        relay(1)
        settle(0)
        relay(2)
    over_ring(lambda j: tiny_copy(1, j).wait_recv())

    def add_slot(j, total):
        return total + tok_ref[j]

    total = lax.fori_loop(0, ring, add_slot, jnp.zeros(tok_ref.shape[1:], F32))
    tiny_s[1] = total
    tab[...] = jnp.zeros_like(tab)
    tab[:heads, :] = tiny_s[1, count : count + heads, : 4 * seq]
    found = add_thirds(mm_nt(in_thirds(tab[...]), chosen[...]))
    gtab_ref[...] = found[:heads, : gtab_ref.shape[1]]
    for j in range(3):
        small_copy(1, j).start()
    for w in (1, 2) if chained else ():
        settle(w)
    for j in range(3):
        small_copy(1, j).wait_recv()
    last = count + heads
    small_ref[pl.ds(t, 1), :] = tiny_s[1, last : last + 1, :]
    for j, owner in enumerate((core, far, fcore)):
        small_ref[pl.ds(owner, 1), :] = small_r[1, j, last : last + 1, :]

    def finish(i):
        for k in (MLP, DMLP, DATT):
            ag_done(k, i)
        rs_done(DMLP, i)
        rs_done(DATT, i)

        @pl.when(s == 0)
        def _():
            out_copy(i).wait_recv()

        @pl.when(s == 1)
        def _():
            out_copy(i).wait_send()
            grad_copy(i).wait_send()

    each_image(finish)

    def tiny_left(j):
        tiny_copy(0, j).wait_recv()
        tiny_copy(0, j).wait_send()
        tiny_copy(1, j).wait_send()

    over_ring(tiny_left)
    for j in range(3):
        small_copy(0, j).wait_send()
        small_copy(1, j).wait_send()
    if chained:
        weights_left()


def run_block(x, cot, wq, wt, wo, w1, w2, temb, gain, shift, rel, table, ring):
    count, rows, width = x.shape
    seq = rel.shape[0]
    heads = table.shape[0]
    local = wo.shape[0]
    hidden = w1.shape[1]
    chained = ring == 4 and count == 2 and width % (16 * ring) == 0
    blocks = 4
    pieces = 3 if width // 4 % 48 == 0 else 1
    cut = width // blocks
    chained = chained and local == width // 4
    if chained:
        wt = wt.reshape(3, pieces, local // pieces, width)
    padded = -(-local // 128) * 128
    lanes = -(-3 * local // 128) * 128
    dims = (count, rows, seq, heads, ring, chained)
    total = (3, pieces, cut // pieces, width) if chained else (3, blocks, cut, width)
    out_shape = [
        jax.ShapeDtypeStruct((count, rows, width), BF16),
        jax.ShapeDtypeStruct((count, rows, width), BF16),
        jax.ShapeDtypeStruct(total, BF16),
        jax.ShapeDtypeStruct((ring, 8, width), F32),
        jax.ShapeDtypeStruct((ring, 8, width), F32),
        jax.ShapeDtypeStruct(table.shape, F32),
        jax.ShapeDtypeStruct((4, width), F32),
    ]
    vm = pltpu.VMEM
    dma = pltpu.SemaphoreType.DMA
    scratch = [
        vm(wq.shape, BF16),
        vm((16, 128) if chained else wt.shape, BF16),
        vm(wo.shape, BF16),
        vm(w1.shape, BF16),
        vm(w2.shape, BF16),
        vm((3, 16, local), F32),
        vm((heads, int(round(seq**0.5)), 2 * seq), F32),
        vm((4 * seq, 4 * seq), BF16),
        vm((16, 4 * seq), F32),
        vm((3, blocks, pieces, cut // pieces, width) if chained else (16, 128), BF16),
        vm((3, 2, pieces, cut // pieces, width) if chained else (16, 128), BF16),
        vm((2, 8, width), F32),
        vm((2, 3, 8, width), F32),
        vm((count, rows, width), BF16),
        vm((count, rows, width), BF16),
        vm((count, rows, width), BF16),
        vm((3, count, seq, width), BF16),
        vm((count, 2, rows, width), F32),
        vm((2, count, 2, rows, width), BF16),
        vm((2, count, rows, width), BF16),
        vm((2, count, 2, rows, width), BF16),
        vm((2, count, rows, width), BF16),
        vm((heads, seq, seq), F32),
        vm((count, heads, seq, seq), F32),
        vm((3, count, seq, local), BF16),
        vm((count, seq, local), BF16),
        vm((count, seq, hidden), BF16),
        vm((count, seq, hidden), BF16),
        vm((2, count, rows, width), F32),
        vm((2, count, rows, 128), F32),
        vm((count, rows, width), F32),
        vm((count, seq, lanes), BF16),
        vm((count, seq, hidden), BF16),
        vm((count, seq, local), BF16),
        vm((3, seq, padded), F32),
        vm((4, 2 * count if chained else count, width, seq), BF16),
        vm((count, seq, padded), BF16),
        vm((count, seq, hidden) if chained else (16, 128), BF16),
        vm((count, seq, hidden) if chained else (16, 128), BF16),
        vm((count, seq, lanes) if chained else (16, 128), BF16),
        vm((count, seq, padded) if chained else (16, 128), BF16),
        dma((5,)),
        dma((4, count, 3)),
        dma((4, count, 3)),
        dma((4, count, 3)),
        dma((4, count, 3)),
        dma((3, count)),
        dma((3, count)),
        dma((3, 3, pieces)),
        dma((3, 2, pieces)),
        dma((12,)),
        dma((12,)),
        dma((2, ring)),
        dma((2, ring)),
        dma((2, 3)),
        dma((2, 3)),
    ]
    whole = pl.BlockSpec(memory_space=pltpu.VMEM)
    lies = pl.BlockSpec(memory_space=pl.ANY)
    return pl.pallas_call(
        functools.partial(block_kernel, dims),
        out_shape=out_shape,
        in_specs=[whole] * 2 + [lies] * 5 + [whole] * 5,
        out_specs=[whole] * len(out_shape),
        scratch_shapes=scratch,
        compiler_params=pltpu.CompilerParams(
            collective_id=0, has_side_effects=True, vmem_limit_bytes=63 * 2**20
        ),
        name="blocks",
    )(x, cot, wq, wt, wo, w1, w2, temb, gain, shift, rel, table)


def per_device(
    images, timesteps, t_table, rel_index, w_qkv, w_time, w_out, w_fc1, w_fc2, rel_table,
    norm_gain, norm_shift, cotangent,
):
    ring = lax.axis_size("dp")
    count = images.shape[0]
    width = images.shape[-1]
    local = w_out.shape[1]
    cut = width // ring
    embedded = t_table[timesteps]
    wq = jnp.transpose(w_qkv[0], (1, 2, 0)).reshape(3 * local, width)
    wt = jnp.transpose(w_time[0], (1, 2, 0))
    output, in_grad, total, sums, emb, g_table, small = run_block(
        images, cotangent, wq, wt, w_out[0], w_fc1[0], w_fc2[0], embedded, norm_gain[0], norm_shift[0],
        rel_index, rel_table[0].T, ring,
    )
    total = total.reshape(3, -1, width)
    if total.shape[1] != cut:
        total = lax.psum_scatter(total, "dp", scatter_dimension=1, tiled=True)
    total = total.astype(F32)
    g_fc2 = total[0].T
    g_fc1 = total[1]
    g_qkv = total[2, :, : 3 * local].reshape(cut, 3, local)
    g_out = total[2, :, 3 * local :].T
    sums = sums[:, :count, : 3 * local].reshape(ring * count, 3, local)
    emb = emb[:, :count].reshape(ring * count, width)
    emb = lax.dynamic_slice_in_dim(emb, lax.axis_index("dp") * cut, cut, axis=1)
    g_time = jnp.einsum("id,icj->dcj", emb, sums, precision=lax.Precision.HIGHEST)
    return (
        output, in_grad[None], g_qkv[None], g_time[None], g_out[None], g_fc1[None], g_fc2[None],
        g_table.T[None], small[None, :2], small[None, 2:],
    )


def solution(mesh):
    in_specs = (
        P("dp", "tensor", None),
        P("dp"),
        P(),
        P(),
        P("section", None, None, "tensor"),
        P("section", None, None, "tensor"),
        P("section", "tensor", None),
        P("section", None, "tensor"),
        P("section", "tensor", None),
        P("section", None, "tensor"),
        P("section", None, None),
        P("section", None, None),
        P("dp", "tensor", None),
    )
    out_specs = (
        P("dp", "tensor", None),
        P("section", "dp", "tensor", None),
        P("section", "dp", None, "tensor"),
        P("section", "dp", None, "tensor"),
        P("section", "tensor", "dp"),
        P("section", "dp", "tensor"),
        P("section", "tensor", "dp"),
        P("section", None, "tensor"),
        P("section", None, None),
        P("section", None, None),
    )
    return jax.shard_map(
        per_device, mesh=mesh, in_specs=in_specs, out_specs=out_specs, check_vma=False
    )
```

```python
import functools

import jax
import jax.numpy as jnp
from jax import lax
from jax.experimental import pallas as pl
from jax.experimental.pallas import tpu as pltpu
from jax.sharding import PartitionSpec as P

MESH = pl.DeviceIdType.MESH
F32 = jnp.float32
BF16 = jnp.bfloat16
EPS = 1e-06
GELU_A = 0.7978845608028654
GELU_B = 0.044715
ATT, MLP, DMLP, DATT = range(4)


def mm(a, b):
    return lax.dot_general(a, b, (((1,), (0,)), ((), ())), preferred_element_type=F32)


def mm_nt(a, b):
    return lax.dot_general(a, b, (((1,), (1,)), ((), ())), preferred_element_type=F32)


def mm_tn(a, b):
    return lax.dot_general(a, b, (((0,), (0,)), ((), ())), preferred_element_type=F32)


def head_windows(heads, local):
    width = local // heads
    found = []
    for h in range(heads):
        lo = h * width // 128 * 128
        hi = min(-(-(h + 1) * width // 128) * 128, local)
        found.append((lo, hi, h * width - lo, (h + 1) * width - lo))
    return found


def only(x, start, stop):
    lane = lax.broadcasted_iota(jnp.int32, x.shape, 1)
    return jnp.where((lane >= start) & (lane < stop), x, jnp.zeros_like(x))


def in_thirds(x):
    high = x.astype(BF16)
    rest = x - high.astype(F32)
    middle = rest.astype(BF16)
    low = (rest - middle.astype(F32)).astype(BF16)
    return jnp.concatenate([high, middle, low], axis=0)


def add_thirds(x):
    rows = x.shape[0] // 3
    return x[:rows] + x[rows : 2 * rows] + x[2 * rows :]


def wider(x, lanes):
    return jnp.concatenate([x, jnp.zeros((x.shape[0], lanes - x.shape[1]), x.dtype)], axis=1)


def block_kernel(
    cfg,
    x_ref, cot_ref, wq_hbm, wt_hbm, wo_hbm, w1_hbm, w2_hbm, temb_ref, gain_ref, shift_ref, rel_ref, tab_ref,
    out_ref, ig_ref, tot_ref, tok_ref, emb_ref, gtab_ref, small_ref,
    wq_ref, wo_ref, w1_ref, w2_ref, tp_ref, tx_ref, chosen, tab, partial, arrived,
    tiny_s, small_r,
    xin, gin, mid, gath, keep, rcv_c, rcv_y, snd_c, snd_y, bias, prob, qkv, att, act, dgel,
    xhat, inv, ymid, dqkv, dh, datt, acc, turned, far_att, act2, dh2, dqkv2, far_att2,
    load_s, ag_s, ag_r, rs_s, rs_r, sec_s, sec_r, ch_s, ch_r, fac_s, fac_r, ti_s, ti_r, sm_s, sm_r,
):
    count, rows, seq, heads, ring, chained = cfg
    half_rows = 2 * rows
    wide = -(-wo_ref.shape[0] // 128) * 128
    width = x_ref.shape[-1]
    local = wo_ref.shape[0]
    grid = int(round(seq**0.5))
    windows = head_windows(heads, local)
    scale = (local // heads) ** (-0.5)
    blocks = 4
    cut = width // blocks
    pieces = arrived.shape[2] if chained else 1
    slim = cut // pieces
    lanes = dqkv.shape[-1]

    s = lax.axis_index("section")
    t = lax.axis_index("tensor")
    z = lax.axis_index("dp")
    core = t + 1 - 2 * (t % 2)
    far = (t + 2) % 4
    fcore = (core + 2) % 4
    here = t // 2
    there = 1 - here
    own = pl.ds(pl.multiple_of(t * rows, rows), rows)

    wt_ref = partial.at[2, : 3 * local, :]

    loads = [
        pltpu.make_async_copy(src, dst, load_s.at[n])
        for n, (src, dst) in enumerate(
            ((wt_hbm, wt_ref), (wq_hbm, wq_ref), (wo_hbm, wo_ref), (w1_hbm, w1_ref), (w2_hbm, w2_ref))
        )
    ]
    for load in loads:
        load.start()

    barrier = pltpu.get_barrier_semaphore()
    for peer in ({"tensor": core}, {"tensor": far}, {"tensor": fcore}, {"section": 1 - s}):
        pl.semaphore_signal(barrier, inc=1, device_id=peer, device_id_type=MESH)

    def greet(j, carry):
        pl.semaphore_signal(barrier, inc=1, device_id={"dp": (z + j) % ring}, device_id_type=MESH)
        return carry

    lax.fori_loop(1, ring, greet, 0)
    pl.semaphore_wait(barrier, 3 + ring)

    def rows_of(owner):
        return pl.ds(pl.multiple_of(owner * rows, rows), rows)

    def half_of(half):
        return pl.ds(pl.multiple_of(half * half_rows, half_rows), half_rows)

    def ag_copy(k, i, which):
        owner, to = ((t, core), (t, far), (far, core))[which]
        ref = gath.at[k % 3, i, rows_of(owner), :]
        return pltpu.make_async_remote_copy(
            src_ref=ref, dst_ref=ref, send_sem=ag_s.at[k, i, which], recv_sem=ag_r.at[k, i, which],
            device_id={"tensor": to}, device_id_type=MESH,
        )

    def ag_start(k, i):
        ag_copy(k, i, 1).start()
        ag_copy(k, i, 0).start()

    def ag_near(k, i):
        ag_copy(k, i, 0).wait_recv()

    def ag_pass(k, i):
        ag_copy(k, i, 1).wait_recv()
        ag_copy(k, i, 2).start()

    def ag_rest(k, i):
        ag_copy(k, i, 2).wait_recv()

    def ag_done(k, i):
        for which in range(3):
            ag_copy(k, i, which).wait_send()

    def rs_copy(k, i, which):
        if which < 2:
            src, dst, to = snd_c.at[k % 2, i, which], rcv_c.at[k % 2, i, which], core
        else:
            src, dst, to = snd_y.at[k % 2, i], rcv_y.at[k % 2, i], far
        return pltpu.make_async_remote_copy(
            src_ref=src, dst_ref=dst, send_sem=rs_s.at[k, i, which], recv_sem=rs_r.at[k, i, which],
            device_id={"tensor": to}, device_id_type=MESH,
        )

    def rs_give(k, i, which, part):
        odd = t % 2 == 1
        low, high = part[:rows], part[rows:]
        snd_c[k % 2, i, which] = jnp.where(odd, low, high).astype(BF16)
        rs_copy(k, i, which).start()
        keep[k % 2, i, which] = jnp.where(odd, high, low)

    def rs_pass(k, i):
        rs_copy(k, i, 0).wait_recv()
        snd_y[k % 2, i] = (keep[k % 2, i, 0] + rcv_c[k % 2, i, 0].astype(F32)).astype(BF16)
        rs_copy(k, i, 2).start()

    def rs_take(k, i):
        rs_copy(k, i, 1).wait_recv()
        near = keep[k % 2, i, 1] + rcv_c[k % 2, i, 1].astype(F32)
        rs_copy(k, i, 2).wait_recv()
        return near + rcv_y[k % 2, i].astype(F32)

    def rs_done(k, i):
        for which in range(3):
            rs_copy(k, i, which).wait_send()

    def sec_copy(j, src, dst):
        return lambda i: pltpu.make_async_remote_copy(
            src_ref=src.at[i], dst_ref=dst.at[i], send_sem=sec_s.at[j, i], recv_sem=sec_r.at[j, i],
            device_id={"section": 1 - s}, device_id_type=MESH,
        )

    mid_copy = sec_copy(0, mid, xin)
    grad_copy = sec_copy(1, ig_ref, gin)
    out_copy = sec_copy(2, out_ref, out_ref)

    def tiny_copy(n, j):
        ref = (emb_ref, tok_ref)[n]
        return pltpu.make_async_remote_copy(
            src_ref=ref.at[z], dst_ref=ref.at[z], send_sem=ti_s.at[n, j], recv_sem=ti_r.at[n, j],
            device_id={"dp": (z + j) % ring}, device_id_type=MESH,
        )

    def over_ring(body):
        def run(j, carry):
            body(j)
            return carry

        lax.fori_loop(1, ring, run, 0)

    def small_copy(n, j):
        return pltpu.make_async_remote_copy(
            src_ref=tiny_s.at[n], dst_ref=small_r.at[n, j], send_sem=sm_s.at[n, j], recv_sem=sm_r.at[n, j],
            device_id={"tensor": (core, far, fcore)[j]}, device_id_type=MESH,
        )

    mate = z + 1 - 2 * (z % 2)
    across = 3 - z
    beyond = 3 * (2 - z)
    is_end = (z == 0) | (z == 3)
    is_mate = (z == 1) | (z == 2)

    def rows_at(b, c):
        return pl.ds(pl.multiple_of(b * cut + c * slim, slim), slim)

    def factor_copy(n):
        if n < 4:
            src, dst = turned.at[n, t % 2], turned.at[n, count + t % 2]
        else:
            src, dst = ((act, act2), (dh, dh2), (dqkv, dqkv2), (far_att, far_att2))[n - 4]
        return pltpu.make_async_remote_copy(
            src_ref=src, dst_ref=dst, send_sem=fac_s.at[n], recv_sem=fac_r.at[n],
            device_id={"dp": mate}, device_id_type=MESH,
        )

    def share_copy(k):
        ref = turned.at[k, count + t % 2]
        return pltpu.make_async_remote_copy(
            src_ref=ref, dst_ref=ref, send_sem=fac_s.at[8 + k], recv_sem=fac_r.at[8 + k],
            device_id={"tensor": core}, device_id_type=MESH,
        )

    def give_factor(*which):
        if chained:

            @pl.when(is_end)
            def _():
                for n in which:
                    factor_copy(n).start()

    def share_factor(k):
        if chained:

            @pl.when(is_mate)
            def _():
                factor_copy(k).wait_recv()
                share_copy(k).start()

    def cross_copy(w, slot, c):
        return pltpu.make_async_remote_copy(
            src_ref=partial.at[w, rows_at((beyond, across)[slot], c), :], dst_ref=arrived.at[w, slot, c],
            send_sem=ch_s.at[w, slot, c], recv_sem=ch_r.at[w, slot, c],
            device_id={"dp": across}, device_id_type=MESH,
        )

    def home_copy(w, c):
        return pltpu.make_async_remote_copy(
            src_ref=partial.at[w, rows_at(mate, c), :], dst_ref=arrived.at[w, 0, c],
            send_sem=ch_s.at[w, 2, c], recv_sem=ch_r.at[w, 0, c],
            device_id={"dp": mate}, device_id_type=MESH,
        )

    def each_piece(body):
        def run(c, carry):
            body(c)
            return carry

        lax.fori_loop(0, pieces, run, 0)

    def give_blocks(w, needs, product):
        if not chained:

            def whole(b, carry):
                tot_ref[w, b] = product(pl.ds(pl.multiple_of(b * cut, cut), cut), 0).astype(BF16)
                return carry

            lax.fori_loop(0, blocks, whole, 0)
            return

        def alone(b):
            def one(c):
                at = rows_at(b, c)
                partial[w, at, :] = product(at, 0).astype(BF16)

            each_piece(one)

        def both(b, slot=None):
            def one(c):
                at = rows_at(b, c)
                partial[w, at, :] = (product(at, 0) + product(at, 1)).astype(BF16)
                if slot is not None:
                    cross_copy(w, slot, c).start()

            each_piece(one)

        @pl.when(is_end)
        def _():
            alone(z)

        @pl.when(is_mate)
        def _():
            for n in needs:
                if n < 4:
                    share_copy(n).wait_recv()
                else:
                    factor_copy(n).wait_recv()
            both(beyond, 0)
            both(across, 1)
            both(z)
            alone(mate)

    def relay(w):
        @pl.when(is_mate)
        def _():
            def one(c):
                cross_copy(w, 0, c).wait_recv()
                at = rows_at(mate, c)
                partial[w, at, :] = (
                    partial[w, at, :].astype(F32) + arrived[w, 0, c].astype(F32)
                ).astype(BF16)
                home_copy(w, c).start()

            each_piece(one)

    def settle(w):
        def finish(slot, copy):
            def one(c):
                copy(c).wait_recv()
                tot_ref[w, c] = (partial[w, rows_at(z, c), :].astype(F32) + arrived[w, slot, c].astype(F32)).astype(BF16)

            each_piece(one)

        @pl.when(is_mate)
        def _():
            finish(1, lambda c: cross_copy(w, 1, c))

        @pl.when(is_end)
        def _():
            finish(0, lambda c: home_copy(w, c))

    def weights_left():
        @pl.when(is_end)
        def _():
            for n in range(8):
                factor_copy(n).wait_send()

        @pl.when(is_mate)
        def _():
            for k in range(4):
                share_copy(k).wait_send()
            for w in range(3):
                for c in range(pieces):
                    cross_copy(w, 0, c).wait_send()
                    cross_copy(w, 1, c).wait_send()
                    home_copy(w, c).wait_send()

    def turn(k):
        for i in range(count):
            turned[k, i] = gath[k % 3, i].T

    def product(k, mine, theirs):
        def rows_of_product(at, side):
            right = (mine, theirs)[side]
            return sum(mm(turned[k, side * count + i, at, :], right[i]) for i in range(count))

        return rows_of_product

    def each_image(body):
        def run(i, carry):
            body(i)
            return carry

        lax.fori_loop(0, count, run, 0)

    def norm(x, which, i):
        mean = jnp.mean(x, axis=-1, keepdims=True)
        centre = x - mean
        root = lax.rsqrt(jnp.mean(centre * centre, axis=-1, keepdims=True) + EPS)
        hat = centre * root
        xhat[which, i] = hat
        inv[which, i] = jnp.broadcast_to(root, (rows, 128))
        return (hat * gain_ref[which : which + 1, :] + shift_ref[which : which + 1, :]).astype(BF16)

    def norm_back(da, which, i):
        hat = xhat[which, i]
        tiny_s[0, which : which + 1, :] += jnp.sum(da * hat, axis=0, keepdims=True)
        tiny_s[0, 2 + which : 3 + which, :] += jnp.sum(da, axis=0, keepdims=True)
        dhat = da * gain_ref[which : which + 1, :]
        m1 = jnp.mean(dhat, axis=-1, keepdims=True)
        m2 = jnp.mean(dhat * hat, axis=-1, keepdims=True)
        return inv[which, i][:, :1] * (dhat - m1 - hat * m2)

    def turn_qkv():
        loads[1].wait()
        for r in range(0, width, wide):
            for c in range(3):
                partial[1, r : r + wide, c * wide : c * wide + local] = wq_ref[
                    c * local : (c + 1) * local, r : r + wide
                ].T

    def turn_weight(w, ref):
        for r in range(0, width, wide):
            partial[w, r : r + wide, : ref.shape[0]] = ref[:, r : r + wide].T

    def lead(k, end, near):
        def first(i):
            end(i)

            @pl.when(i == count - 1)
            def _():
                ag_pass(k, 0)

            ag_near(k, i)
            near(i)

        each_image(first)

    def follow(k, rest):
        def second(i):
            ag_rest(k, i)
            rest(i)

            @pl.when(i < count - 1)
            def _():
                ag_pass(k, i + 1)

            rs_pass(k, i)

        each_image(second)

    tiny_s[...] = jnp.zeros_like(tiny_s)
    tok_ref[z] = jnp.zeros_like(tok_ref[z])
    emb_ref[z] = jnp.zeros_like(emb_ref[z])
    emb_ref[z, :count, :] = temb_ref[...].astype(F32)
    over_ring(lambda j: tiny_copy(0, j).start())

    @pl.when(s == 1)
    def _():
        def begin(i):
            gath[DMLP, i, own, :] = cot_ref[i]
            ag_start(DMLP, i)

        each_image(begin)

    def take_input(i):
        @pl.when(s == 0)
        def _():
            xin[i] = x_ref[i]

        @pl.when(s == 1)
        def _():
            mid_copy(i).wait_recv()

        gath[ATT, i, own, :] = norm(xin[i].astype(F32), 0, i)
        ag_start(ATT, i)

    lane = lax.broadcasted_iota(jnp.int32, (1, 2 * seq), 1)

    def tables():
        valid = lane < (2 * grid - 1) * grid
        slab = pltpu.roll(wider(rel_ref[:grid, :], 2 * seq), grid * (grid - 1), 1)
        for k in range(grid - 1):
            r = grid - 1 - k
            block = only(rel_ref[r * grid : (r + 1) * grid, :128], 0, grid)
            slab += pltpu.roll(wider(block, 2 * seq), k * grid, 1)
        none = jnp.full((1, 2 * seq), -1, jnp.int32)
        before = none
        for c in range(1, grid):
            moved = pltpu.roll(slab[c : c + 1, :], grid - c, 1)
            before = jnp.where((lane % grid == grid - c) & valid, moved, before)
        order = jnp.concatenate([jnp.where(valid, slab[:1, :], none), before], axis=1)
        step = 128
        for r in range(0, chosen.shape[0], step):
            bucket = r + lax.broadcasted_iota(jnp.int32, (step, 4 * seq), 0)
            chosen[r : r + step, :] = jnp.where(bucket == order, 1.0, 0.0).astype(BF16)
        tab[...] = jnp.zeros_like(tab)
        tab[:heads, : tab_ref.shape[1]] = tab_ref[...]
        found = add_thirds(mm(in_thirds(tab[...]), chosen[...]))
        after, before = found[:, : 2 * seq], found[:, 2 * seq :]
        for c in range(grid):
            low = pltpu.roll(after, c, 1) if c else after
            high = pltpu.roll(before, 2 * seq - (grid - c), 1)
            row = jnp.where(lane % grid >= c, low, high)
            for h in range(heads):
                tx_ref[h, c : c + 1, :] = row[h : h + 1, :]

        def expand(h, carry):
            for r in range(grid):
                shift = (2 * seq - grid * (grid - 1 - r)) % (2 * seq)
                bias[h, r * grid : (r + 1) * grid, :] = pltpu.roll(tx_ref[h], shift, 1)[:, :seq]
            return carry

        lax.fori_loop(0, heads, expand, 0)
        loads[0].wait()
        tp_ref[...] = jnp.zeros_like(tp_ref)
        emb = jnp.concatenate([temb_ref[...], jnp.zeros((16 - count, width), BF16)], axis=0)
        for c in range(3):
            tp_ref[c] = mm_nt(emb, partial[2, c * local : (c + 1) * local, :])

    @pl.when(s == 1)
    def _():
        tables()

        def spread_cot(i):
            ag_pass(DMLP, i)
            ag_near(DMLP, i)
            ag_rest(DMLP, i)

        each_image(spread_cot)
        turn(DMLP)
        give_factor(2)
        turn_qkv()
        loads[2].wait()
        turn_weight(2, wo_ref)
        loads[3].wait()
        turn_weight(0, w1_ref)
        loads[4].wait()

        def early(i):
            dh[i] = mm_nt(gath[DMLP, i], w2_ref[...]).astype(BF16)

        each_image(early)

    @pl.when(s == 0)
    def _():
        each_image(take_input)
        tables()
        turn_qkv()
        for n in (2, 3, 4):
            loads[n].wait()

    def project(i, half):
        a = gath[ATT, i, half_of(half), :]
        part = mm(a, partial[1, :, : 2 * wide + local])
        for c in range(3):
            qkv[c, i, half_of(half), :] = (
                part[:, c * wide : c * wide + local] + tp_ref[c, pl.ds(i, 1), :]
            ).astype(BF16)

    def att_first(i):
        @pl.when(s == 1)
        def _():
            take_input(i)

    lead(ATT, att_first, lambda i: project(i, here))

    def att_rest(i):
        project(i, there)
        acc[0] = jnp.zeros_like(acc[0])
        for h, (lo, hi, start, stop) in enumerate(windows):
            q = only(qkv[0, i, :, lo:hi], start, stop)
            scores = mm_nt(q, qkv[1, i, :, lo:hi]) * scale + bias[h]
            top = jnp.max(scores, axis=-1, keepdims=True)
            expo = jnp.exp(scores - top)
            p = expo / jnp.sum(expo, axis=-1, keepdims=True)
            prob[i, h] = p
            acc[0, :, lo:hi] += mm(p.astype(BF16), only(qkv[2, i, :, lo:hi], start, stop))
        att[i] = acc[0, :, :local].astype(BF16)
        far_att[i] = pltpu.roll(acc[0], far_att.shape[-1] - local, 1).astype(BF16)
        rs_give(ATT, i, 0, mm(att[i, half_of(there), :], wo_ref[...]))
        rs_give(ATT, i, 1, mm(att[i, half_of(here), :], wo_ref[...]))

    follow(ATT, att_rest)

    turn(ATT)
    give_factor(0, 7)

    def att_end(i):
        y = xin[i].astype(F32) + rs_take(ATT, i)
        ag_done(ATT, i)
        rs_done(ATT, i)
        ymid[i] = y
        gath[MLP, i, own, :] = norm(y, 1, i)
        ag_start(MLP, i)

    def mlp_half(i, half, which):
        a = gath[MLP, i, half_of(half), :]
        v = mm(a, w1_ref[...])
        th = jnp.tanh(GELU_A * (v + GELU_B * (v * v * v)))
        up = 0.5 * (1.0 + th)
        act[i, half_of(half), :] = (v * up).astype(BF16)
        slope = up + (0.5 * GELU_A) * v * (1.0 - th * th) * (1.0 + (3.0 * GELU_B) * (v * v))
        dgel[i, half_of(half), :] = slope.astype(BF16)
        rs_give(MLP, i, which, mm(act[i, half_of(half), :], w2_ref[...]))

    lead(MLP, att_end, lambda i: mlp_half(i, here, 1))
    follow(MLP, lambda i: mlp_half(i, there, 0))
    turn(MLP)
    give_factor(1, 4)

    def mlp_end(i):
        mid[i] = (ymid[i] + rs_take(MLP, i)).astype(BF16)
        rs_done(MLP, i)

        @pl.when(s == 0)
        def _():
            mid_copy(i).start()

        @pl.when(s == 1)
        def _():
            out_ref[i] = mid[i]
            out_copy(i).start()

    def take_grad(i):
        mid_copy(i).wait_send()
        grad_copy(i).wait_recv()
        gath[DMLP, i, own, :] = gin[i]
        ag_start(DMLP, i)

    def dmlp_half(i, half, which):
        @pl.when(s == 0)
        def _():
            dh[i, half_of(half), :] = mm(gath[DMLP, i, half_of(half), :], partial[1]).astype(BF16)

        dact = dh[i, half_of(half), :].astype(F32)
        dh[i, half_of(half), :] = (dact * dgel[i, half_of(half), :].astype(F32)).astype(BF16)
        rs_give(DMLP, i, which, mm(dh[i, half_of(half), :], partial[0]))

    @pl.when(s == 0)
    def _():
        each_image(mlp_end)
        turn_weight(0, w1_ref)
        turn_weight(1, w2_ref)
        turn_weight(2, wo_ref)
        lead(DMLP, take_grad, lambda i: dmlp_half(i, here, 1))

    def dmlp_rest(i):
        @pl.when(s == 0)
        def _():
            ag_rest(DMLP, i)

            @pl.when(i == count - 1)
            def _():
                turn(DMLP)
                give_factor(2)

        dmlp_half(i, there, 0)

        @pl.when(s == 1)
        def _():
            dmlp_half(i, here, 1)

        @pl.when((s == 0) & (i < count - 1))
        def _():
            ag_pass(DMLP, i + 1)

        rs_pass(DMLP, i)

    each_image(dmlp_rest)
    give_factor(5)

    @pl.when(s == 0)
    def _():
        share_factor(ATT)
        share_factor(MLP)

    @pl.when(s == 1)
    def _():
        def keep_cot(i):
            gin[i] = cot_ref[i]
            mlp_end(i)

        each_image(keep_cot)

    def dmlp_end(i):
        grad = gin[i].astype(F32) + norm_back(rs_take(DMLP, i), 1, i)
        ymid[i] = grad
        gath[DATT % 3, i, own, :] = grad.astype(BF16)
        ag_start(DATT, i)

    def job_fc2():
        give_blocks(0, (2, 4), product(DMLP, act, act2))

    def job_fc1():
        give_blocks(1, (1, 5), product(MLP, dh, dh2))

    def datt_part(i, half):
        datt[i, half_of(half), :] = mm(
            gath[DATT % 3, i, half_of(half), :], partial[2, :, :local]
        ).astype(BF16)

    lead(DATT, dmlp_end, lambda i: datt_part(i, here))

    @pl.when(s == 0)
    def _():
        share_factor(DMLP)
        job_fc2()

    def datt_rest(i):
        datt_part(i, there)
        acc[...] = jnp.zeros_like(acc)
        for h, (lo, hi, start, stop) in enumerate(windows):
            q = only(qkv[0, i, :, lo:hi], start, stop)
            k = only(qkv[1, i, :, lo:hi], start, stop)
            d = only(datt[i, :, lo:hi], start, stop)
            p = prob[i, h]
            dp = mm_nt(d, qkv[2, i, :, lo:hi])
            inner = jnp.sum(p * dp, axis=-1, keepdims=True)
            ds = (p * (dp - inner)).astype(BF16)

            @pl.when(i == 0)
            def _():
                bias[h] = ds.astype(F32)

            @pl.when(i > 0)
            def _():
                bias[h] += ds.astype(F32)

            acc[0, :, lo:hi] += mm(ds, k)
            acc[1, :, lo:hi] += mm_tn(ds, q)
            acc[2, :, lo:hi] += mm_tn(p.astype(BF16), d)
        total = jnp.zeros((seq, lanes), F32)
        for c, by in enumerate((scale, scale, 1.0)):
            lo = c * local // 128 * 128
            moved = acc[c] * by
            if c * local > lo:
                moved = pltpu.roll(moved, c * local - lo, 1)
            pieces = [jnp.zeros((seq, lo), F32)] * (lo > 0) + [moved]
            if lo + moved.shape[1] < lanes:
                pieces.append(jnp.zeros((seq, lanes - lo - moved.shape[1]), F32))
            total += jnp.concatenate(pieces, axis=1)
        dqkv[i] = total.astype(BF16)
        tok_ref[z, pl.ds(i, 1), :lanes] = jnp.sum(dqkv[i].astype(F32), axis=0, keepdims=True)
        for which, half in ((0, there), (1, here)):
            rs_give(DATT, i, which, mm(dqkv[i, half_of(half), : 3 * local], wq_ref[...]))

    follow(DATT, datt_rest)

    give_factor(6)
    turn(DATT)
    give_factor(3)

    @pl.when(s == 0)
    def _():
        job_fc1()

    def datt_end(i):
        grad = ymid[i] + norm_back(rs_take(DATT, i), 0, i)
        ig_ref[i] = grad.astype(BF16)

        @pl.when(s == 1)
        def _():
            grad_copy(i).start()

    each_image(datt_end)

    for j in range(3):
        small_copy(0, j).start()

    def fold(h, carry):
        total = jnp.zeros((grid, 2 * seq), F32)
        for r in range(grid):
            part = wider(bias[h, r * grid : (r + 1) * grid, :], 2 * seq)
            shift = grid * (grid - 1 - r)
            total += part if shift == 0 else pltpu.roll(part, shift, 1)
        after = total[:1, :]
        before = jnp.zeros((1, 2 * seq), F32)
        for c in range(1, grid):
            row = total[c : c + 1, :]
            late = lane % grid >= c
            after += pltpu.roll(jnp.where(late, row, 0.0), 2 * seq - c, 1)
            before += pltpu.roll(jnp.where(late, 0.0, row), grid - c, 1)
        tok_ref[z, pl.ds(count + h, 1), : 4 * seq] = jnp.concatenate([after, before], axis=1)
        return carry

    lax.fori_loop(0, heads, fold, 0)
    for j in range(3):
        small_copy(0, j).wait_recv()
    over_tensor = tiny_s[0] + small_r[0, 0] + small_r[0, 1] + small_r[0, 2]
    row = lax.broadcasted_iota(jnp.int32, over_tensor.shape, 0)
    tok_ref[z, count + heads : count + heads + 1, :] = jnp.sum(
        jnp.where(row == t, over_tensor, 0.0), axis=0, keepdims=True
    )
    over_ring(lambda j: tiny_copy(1, j).start())

    @pl.when(s == 1)
    def _():
        share_factor(DMLP)
        share_factor(ATT)
        share_factor(MLP)
        job_fc2()
        job_fc1()

    if chained:
        relay(0)

    share_factor(DATT)
    from_qkv = product(ATT, dqkv, dqkv2)
    from_out = product(DATT, far_att, far_att2)

    def rest_product(at, side):
        first, last = from_qkv(at, side), from_out(at, side)
        seam = width - last.shape[1]
        over = lanes - seam
        return jnp.concatenate(
            [first[:, :seam], first[:, seam:] + last[:, :over], last[:, over:]], axis=1
        )

    give_blocks(2, (0, 3, 6, 7), rest_product)
    if chained:
        relay(1)
        settle(0)
        relay(2)
    over_ring(lambda j: tiny_copy(1, j).wait_recv())

    def add_slot(j, total):
        return total + tok_ref[j]

    total = lax.fori_loop(0, ring, add_slot, jnp.zeros(tok_ref.shape[1:], F32))
    tiny_s[1] = total
    tab[...] = jnp.zeros_like(tab)
    tab[:heads, :] = tiny_s[1, count : count + heads, : 4 * seq]
    found = add_thirds(mm_nt(in_thirds(tab[...]), chosen[...]))
    gtab_ref[...] = found[:heads, : gtab_ref.shape[1]]
    for j in range(3):
        small_copy(1, j).start()
    for w in (1, 2) if chained else ():
        settle(w)
    for j in range(3):
        small_copy(1, j).wait_recv()
    last = count + heads
    small_ref[pl.ds(t, 1), :] = tiny_s[1, last : last + 1, :]
    for j, owner in enumerate((core, far, fcore)):
        small_ref[pl.ds(owner, 1), :] = small_r[1, j, last : last + 1, :]

    def finish(i):
        for k in (MLP, DMLP, DATT):
            ag_done(k, i)
        rs_done(DMLP, i)
        rs_done(DATT, i)

        @pl.when(s == 0)
        def _():
            out_copy(i).wait_recv()

        @pl.when(s == 1)
        def _():
            out_copy(i).wait_send()
            grad_copy(i).wait_send()

    each_image(finish)

    def tiny_left(j):
        tiny_copy(0, j).wait_recv()
        tiny_copy(0, j).wait_send()
        tiny_copy(1, j).wait_send()

    over_ring(tiny_left)
    for j in range(3):
        small_copy(0, j).wait_send()
        small_copy(1, j).wait_send()
    if chained:
        weights_left()


def run_block(x, cot, wq, wt, wo, w1, w2, temb, gain, shift, rel, table, ring):
    count, rows, width = x.shape
    seq = rel.shape[0]
    heads = table.shape[0]
    local = wo.shape[0]
    hidden = w1.shape[1]
    chained = ring == 4 and count == 2 and width % (16 * ring) == 0
    blocks = 4
    pieces = 3 if width // 4 % 48 == 0 else 1
    cut = width // blocks
    padded = -(-local // 128) * 128
    lanes = -(-3 * local // 128) * 128
    dims = (count, rows, seq, heads, ring, chained)
    total = (3, pieces, cut // pieces, width) if chained else (3, blocks, cut, width)
    out_shape = [
        jax.ShapeDtypeStruct((count, rows, width), BF16),
        jax.ShapeDtypeStruct((count, rows, width), BF16),
        jax.ShapeDtypeStruct(total, BF16),
        jax.ShapeDtypeStruct((ring, 8, width), F32),
        jax.ShapeDtypeStruct((ring, 8, width), F32),
        jax.ShapeDtypeStruct(table.shape, F32),
        jax.ShapeDtypeStruct((4, width), F32),
    ]
    vm = pltpu.VMEM
    dma = pltpu.SemaphoreType.DMA
    scratch = [
        vm(wq.shape, BF16),
        vm(wo.shape, BF16),
        vm(w1.shape, BF16),
        vm(w2.shape, BF16),
        vm((3, 16, local), F32),
        vm((heads, int(round(seq**0.5)), 2 * seq), F32),
        vm((4 * seq, 4 * seq), BF16),
        vm((16, 4 * seq), F32),
        vm((3, width, width), BF16),
        vm((3, 2, pieces, cut // pieces, width) if chained else (16, 128), BF16),
        vm((2, 8, width), F32),
        vm((2, 3, 8, width), F32),
        vm((count, rows, width), BF16),
        vm((count, rows, width), BF16),
        vm((count, rows, width), BF16),
        vm((3, count, seq, width), BF16),
        vm((2, count, 2, rows, width), F32),
        vm((2, count, 2, rows, width), BF16),
        vm((2, count, rows, width), BF16),
        vm((2, count, 2, rows, width), BF16),
        vm((2, count, rows, width), BF16),
        vm((heads, seq, seq), F32),
        vm((count, heads, seq, seq), F32),
        vm((3, count, seq, local), BF16),
        vm((count, seq, local), BF16),
        vm((count, seq, hidden), BF16),
        vm((count, seq, hidden), BF16),
        vm((2, count, rows, width), F32),
        vm((2, count, rows, 128), F32),
        vm((count, rows, width), F32),
        vm((count, seq, lanes), BF16),
        vm((count, seq, hidden), BF16),
        vm((count, seq, local), BF16),
        vm((3, seq, padded), F32),
        vm((4, 2 * count if chained else count, width, seq), BF16),
        vm((count, seq, padded), BF16),
        vm((count, seq, hidden) if chained else (16, 128), BF16),
        vm((count, seq, hidden) if chained else (16, 128), BF16),
        vm((count, seq, lanes) if chained else (16, 128), BF16),
        vm((count, seq, padded) if chained else (16, 128), BF16),
        dma((5,)),
        dma((4, count, 3)),
        dma((4, count, 3)),
        dma((4, count, 3)),
        dma((4, count, 3)),
        dma((3, count)),
        dma((3, count)),
        dma((3, 3, pieces)),
        dma((3, 2, pieces)),
        dma((12,)),
        dma((12,)),
        dma((2, ring)),
        dma((2, ring)),
        dma((2, 3)),
        dma((2, 3)),
    ]
    whole = pl.BlockSpec(memory_space=pltpu.VMEM)
    lies = pl.BlockSpec(memory_space=pl.ANY)
    return pl.pallas_call(
        functools.partial(block_kernel, dims),
        out_shape=out_shape,
        in_specs=[whole] * 2 + [lies] * 5 + [whole] * 5,
        out_specs=[whole] * len(out_shape),
        scratch_shapes=scratch,
        compiler_params=pltpu.CompilerParams(
            collective_id=0, has_side_effects=True, vmem_limit_bytes=63 * 2**20
        ),
        name="blocks",
    )(x, cot, wq, wt, wo, w1, w2, temb, gain, shift, rel, table)


def per_device(
    images, timesteps, t_table, rel_index, w_qkv, w_time, w_out, w_fc1, w_fc2, rel_table,
    norm_gain, norm_shift, cotangent,
):
    ring = lax.axis_size("dp")
    count = images.shape[0]
    width = images.shape[-1]
    local = w_out.shape[1]
    cut = width // ring
    embedded = t_table[timesteps]
    wq = jnp.transpose(w_qkv[0], (1, 2, 0)).reshape(3 * local, width)
    wt = jnp.transpose(w_time[0], (1, 2, 0)).reshape(3 * local, width)
    output, in_grad, total, sums, emb, g_table, small = run_block(
        images, cotangent, wq, wt, w_out[0], w_fc1[0], w_fc2[0], embedded, norm_gain[0], norm_shift[0],
        rel_index, rel_table[0].T, ring,
    )
    total = total.reshape(3, -1, width)
    if total.shape[1] != cut:
        total = lax.psum_scatter(total, "dp", scatter_dimension=1, tiled=True)
    total = total.astype(F32)
    g_fc2 = total[0].T
    g_fc1 = total[1]
    g_qkv = total[2, :, : 3 * local].reshape(cut, 3, local)
    g_out = total[2, :, 3 * local :].T
    sums = sums[:, :count, : 3 * local].reshape(ring * count, 3, local)
    emb = emb[:, :count].reshape(ring * count, width)
    emb = lax.dynamic_slice_in_dim(emb, lax.axis_index("dp") * cut, cut, axis=1)
    g_time = jnp.einsum("id,icj->dcj", emb, sums, precision=lax.Precision.HIGHEST)
    return (
        output, in_grad[None], g_qkv[None], g_time[None], g_out[None], g_fc1[None], g_fc2[None],
        g_table.T[None], small[None, :2], small[None, 2:],
    )


def solution(mesh):
    in_specs = (
        P("dp", "tensor", None),
        P("dp"),
        P(),
        P(),
        P("section", None, None, "tensor"),
        P("section", None, None, "tensor"),
        P("section", "tensor", None),
        P("section", None, "tensor"),
        P("section", "tensor", None),
        P("section", None, "tensor"),
        P("section", None, None),
        P("section", None, None),
        P("dp", "tensor", None),
    )
    out_specs = (
        P("dp", "tensor", None),
        P("section", "dp", "tensor", None),
        P("section", "dp", None, "tensor"),
        P("section", "dp", None, "tensor"),
        P("section", "tensor", "dp"),
        P("section", "dp", "tensor"),
        P("section", "tensor", "dp"),
        P("section", None, "tensor"),
        P("section", None, None),
        P("section", None, None),
    )
    return jax.shard_map(
        per_device, mesh=mesh, in_specs=in_specs, out_specs=out_specs, check_vma=False
    )
```

```python
import functools

import jax
import jax.numpy as jnp
from jax import lax
from jax.experimental import pallas as pl
from jax.experimental.pallas import tpu as pltpu
from jax.sharding import PartitionSpec as P

MESH = pl.DeviceIdType.MESH
F32 = jnp.float32
BF16 = jnp.bfloat16
EPS = 1e-06
GELU_A = 0.7978845608028654
GELU_B = 0.044715
ATT, MLP, DMLP, DATT = range(4)


def mm(a, b):
    return lax.dot_general(a, b, (((1,), (0,)), ((), ())), preferred_element_type=F32)


def mm_nt(a, b):
    return lax.dot_general(a, b, (((1,), (1,)), ((), ())), preferred_element_type=F32)


def mm_tn(a, b):
    return lax.dot_general(a, b, (((0,), (0,)), ((), ())), preferred_element_type=F32)


def gelu_parts(v):
    square = v * v
    th = jnp.tanh(v * (GELU_A + (GELU_A * GELU_B) * square))
    up = 0.5 + 0.5 * th
    slope = up + v * (1.0 - th * th) * (0.5 * GELU_A + (1.5 * GELU_A * GELU_B) * square)
    return v * up, slope


def head_windows(heads, local):
    width = local // heads
    found = []
    for h in range(heads):
        lo = h * width // 128 * 128
        hi = min(-(-(h + 1) * width // 128) * 128, local)
        found.append((lo, hi, h * width - lo, (h + 1) * width - lo))
    return found


def only(x, start, stop):
    lane = lax.broadcasted_iota(jnp.int32, x.shape, 1)
    return jnp.where((lane >= start) & (lane < stop), x, jnp.zeros_like(x))


def in_thirds(x):
    high = x.astype(BF16)
    rest = x - high.astype(F32)
    middle = rest.astype(BF16)
    low = (rest - middle.astype(F32)).astype(BF16)
    return jnp.concatenate([high, middle, low], axis=0)


def add_thirds(x):
    rows = x.shape[0] // 3
    return x[:rows] + x[rows : 2 * rows] + x[2 * rows :]


def wider(x, lanes):
    return jnp.concatenate([x, jnp.zeros((x.shape[0], lanes - x.shape[1]), x.dtype)], axis=1)


def block_kernel(
    cfg,
    x_ref, cot_ref, wq_hbm, wt_hbm, wo_hbm, w1_hbm, w2_hbm, temb_ref, gain_ref, shift_ref, rel_ref, tab_ref,
    out_ref, ig_ref, tot_ref, mlp_ref, tok_ref, emb_ref, gtab_ref, small_ref,
    wq_ref, wo_ref, w1_ref, w2_ref, tp_ref, tx_ref, chosen, tab, partial, sums, arrived,
    tiny_s, small_r,
    xin, gin, mid, gath, keep, rcv_c, rcv_y, snd_c, snd_y, bias, prob, qkv, att, act, dgel,
    xhat, inv, ymid, dqkv, dtail, dh, acc, turned, line, far_att, dqkv2, dtail2, far_att2,
    load_s, ag_s, ag_r, rs_s, rs_r, sec_s, sec_r, ch_s, ch_r, fac_s, fac_r, li_s, li_r, ti_s, ti_r, sm_s, sm_r,
):
    count, rows, seq, heads, ring, chained = cfg
    half_rows = 2 * rows
    wide = -(-wo_ref.shape[0] // 128) * 128
    width = x_ref.shape[-1]
    local = wo_ref.shape[0]
    grid = int(round(seq**0.5))
    windows = head_windows(heads, local)
    scale = (local // heads) ** (-0.5)
    blocks = 4
    cut = width // blocks
    pieces = sums.shape[0]
    slim = cut // pieces
    full = dqkv.shape[0]
    lanes = full * dqkv.shape[-1] + dtail.shape[-1]

    s = lax.axis_index("section")
    t = lax.axis_index("tensor")
    z = lax.axis_index("dp")
    core = t + 1 - 2 * (t % 2)
    far = (t + 2) % 4
    fcore = (core + 2) % 4
    here = t // 2
    there = 1 - here
    own = pl.ds(pl.multiple_of(t * rows, rows), rows)

    wt_ref = partial.at[0, : 3 * local, :]

    loads = [
        pltpu.make_async_copy(src, dst, load_s.at[n])
        for n, (src, dst) in enumerate(
            ((wt_hbm, wt_ref), (wq_hbm, wq_ref), (wo_hbm, wo_ref), (w1_hbm, w1_ref), (w2_hbm, w2_ref))
        )
    ]
    for load in loads:
        load.start()

    barrier = pltpu.get_barrier_semaphore()
    for peer in ({"tensor": core}, {"tensor": far}, {"tensor": fcore}, {"section": 1 - s}):
        pl.semaphore_signal(barrier, inc=1, device_id=peer, device_id_type=MESH)

    def greet(j, carry):
        pl.semaphore_signal(barrier, inc=1, device_id={"dp": (z + j) % ring}, device_id_type=MESH)
        return carry

    lax.fori_loop(1, ring, greet, 0)
    pl.semaphore_wait(barrier, 3 + ring)

    def rows_of(owner):
        return pl.ds(pl.multiple_of(owner * rows, rows), rows)

    def half_of(half):
        return pl.ds(pl.multiple_of(half * half_rows, half_rows), half_rows)

    def ag_copy(k, i, which):
        owner, to = ((t, core), (t, far), (far, core))[which]
        ref = gath.at[k % 3, i, rows_of(owner), :]
        return pltpu.make_async_remote_copy(
            src_ref=ref, dst_ref=ref, send_sem=ag_s.at[k, i, which], recv_sem=ag_r.at[k, i, which],
            device_id={"tensor": to}, device_id_type=MESH,
        )

    def ag_start(k, i):
        ag_copy(k, i, 1).start()
        ag_copy(k, i, 0).start()

    def ag_near(k, i):
        ag_copy(k, i, 0).wait_recv()

    def ag_pass(k, i):
        ag_copy(k, i, 1).wait_recv()
        ag_copy(k, i, 2).start()

    def ag_rest(k, i):
        ag_copy(k, i, 2).wait_recv()

    def ag_done(k, i):
        for which in range(3):
            ag_copy(k, i, which).wait_send()

    def rs_copy(k, i, which):
        if which < 2:
            src, dst, to = snd_c.at[k % 2, i, which], rcv_c.at[k % 2, i, which], core
        else:
            src, dst, to = snd_y.at[k % 2, i], rcv_y.at[k % 2, i], far
        return pltpu.make_async_remote_copy(
            src_ref=src, dst_ref=dst, send_sem=rs_s.at[k, i, which], recv_sem=rs_r.at[k, i, which],
            device_id={"tensor": to}, device_id_type=MESH,
        )

    def rs_give(k, i, which, part):
        odd = t % 2 == 1
        low, high = part[:rows], part[rows:]
        snd_c[k % 2, i, which] = jnp.where(odd, low, high).astype(BF16)
        rs_copy(k, i, which).start()
        keep[k % 2, i, which] = jnp.where(odd, high, low)

    def rs_pass(k, i):
        rs_copy(k, i, 0).wait_recv()
        snd_y[k % 2, i] = (keep[k % 2, i, 0] + rcv_c[k % 2, i, 0].astype(F32)).astype(BF16)
        rs_copy(k, i, 2).start()

    def rs_take(k, i):
        rs_copy(k, i, 1).wait_recv()
        near = keep[k % 2, i, 1] + rcv_c[k % 2, i, 1].astype(F32)
        rs_copy(k, i, 2).wait_recv()
        return near + rcv_y[k % 2, i].astype(F32)

    def rs_done(k, i):
        for which in range(3):
            rs_copy(k, i, which).wait_send()

    def sec_copy(j, src, dst):
        return lambda i: pltpu.make_async_remote_copy(
            src_ref=src.at[i], dst_ref=dst.at[i], send_sem=sec_s.at[j, i], recv_sem=sec_r.at[j, i],
            device_id={"section": 1 - s}, device_id_type=MESH,
        )

    mid_copy = sec_copy(0, mid, xin)
    grad_copy = sec_copy(1, ig_ref, gin)
    out_copy = sec_copy(2, out_ref, out_ref)

    def tiny_copy(n, j):
        ref = (emb_ref, tok_ref)[n]
        return pltpu.make_async_remote_copy(
            src_ref=ref.at[z], dst_ref=ref.at[z], send_sem=ti_s.at[n, j], recv_sem=ti_r.at[n, j],
            device_id={"dp": (z + j) % ring}, device_id_type=MESH,
        )

    def over_ring(body):
        def run(j, carry):
            body(j)
            return carry

        lax.fori_loop(1, ring, run, 0)

    def small_copy(n, j):
        return pltpu.make_async_remote_copy(
            src_ref=tiny_s.at[n], dst_ref=small_r.at[n, j], send_sem=sm_s.at[n, j], recv_sem=sm_r.at[n, j],
            device_id={"tensor": (core, far, fcore)[j]}, device_id_type=MESH,
        )

    mate = z + 1 - 2 * (z % 2)
    across = 3 - z
    beyond = 3 * (2 - z)
    is_end = (z == 0) | (z == 3)
    is_mate = (z == 1) | (z == 2)
    base = z * count if chained else 0
    place = {ATT: (turned, 0), DATT: (turned, 1), MLP: (line, 0), DMLP: (line, 1)}

    def block(b):
        return pl.ds(pl.multiple_of(b * cut, cut), cut)

    def factor_copy(n):
        if n < 2:
            src, dst = turned.at[n, t % 2], turned.at[n, count + t % 2]
        else:
            pairs = [(dqkv.at[c], dqkv2.at[c]) for c in range(full)] + [(dtail, dtail2), (far_att, far_att2)]
            src, dst = pairs[n - 2]
        return pltpu.make_async_remote_copy(
            src_ref=src, dst_ref=dst, send_sem=fac_s.at[n], recv_sem=fac_r.at[n],
            device_id={"dp": mate}, device_id_type=MESH,
        )

    def share_copy(k):
        ref = turned.at[k, count + t % 2]
        return pltpu.make_async_remote_copy(
            src_ref=ref, dst_ref=ref, send_sem=fac_s.at[4 + full + k], recv_sem=fac_r.at[4 + full + k],
            device_id={"tensor": core}, device_id_type=MESH,
        )

    def give_factor(*which):
        if chained:

            @pl.when(is_end)
            def _():
                for n in which:
                    factor_copy(n).start()

    def share_factor(k):
        if chained:

            @pl.when(is_mate)
            def _():
                factor_copy(k).wait_recv()
                share_copy(k).start()

    def cross_copy(slot, c):
        return pltpu.make_async_remote_copy(
            src_ref=sums.at[c, block((beyond, across)[slot]), :], dst_ref=arrived.at[slot, c],
            send_sem=ch_s.at[slot, c], recv_sem=ch_r.at[slot, c],
            device_id={"dp": across}, device_id_type=MESH,
        )

    def home_copy(c):
        return pltpu.make_async_remote_copy(
            src_ref=sums.at[c, block(mate), :], dst_ref=arrived.at[0, c],
            send_sem=ch_s.at[2, c], recv_sem=ch_r.at[0, c],
            device_id={"dp": mate}, device_id_type=MESH,
        )

    def rest_product(c, at, side):
        def by(n, right):
            return sum(mm(turned[n, side * count + i, at, :], right[i]) for i in range(count))

        if c < full:
            return by(0, (dqkv, dqkv2)[side].at[c])
        return wider(by(0, (dtail, dtail2)[side]), wide) + by(1, (far_att, far_att2)[side])

    def give_rest(c):
        def alone(b):
            sums[c, block(b), :] = rest_product(c, block(b), 0).astype(BF16)

        def both(b):
            both_sides = rest_product(c, block(b), 0) + rest_product(c, block(b), 1)
            sums[c, block(b), :] = both_sides.astype(BF16)

        @pl.when(is_end)
        def _():
            alone(z)

        @pl.when(is_mate)
        def _():
            if c < full:
                factor_copy(2 + c).wait_recv()
            else:
                share_copy(0).wait_recv()
                share_copy(1).wait_recv()
                factor_copy(2 + full).wait_recv()
                factor_copy(3 + full).wait_recv()
            both(beyond)
            cross_copy(0, c).start()
            both(across)
            cross_copy(1, c).start()
            both(z)
            alone(mate)

    def relay(c):
        @pl.when(is_mate)
        def _():
            cross_copy(0, c).wait_recv()
            home = sums[c, block(mate), :].astype(F32) + arrived[0, c].astype(F32)
            sums[c, block(mate), :] = home.astype(BF16)
            home_copy(c).start()

    def settle(c):
        def finish(slot, copy):
            copy.wait_recv()
            whole = sums[c, block(z), :].astype(F32) + arrived[slot, c].astype(F32)
            tot_ref[:, c * wide : (c + 1) * wide] = whole.astype(BF16)

        @pl.when(is_mate)
        def _():
            finish(1, cross_copy(1, c))

        @pl.when(is_end)
        def _():
            finish(0, home_copy(c))

    def weights_left():
        @pl.when(is_end)
        def _():
            for n in range(4 + full):
                factor_copy(n).wait_send()

        @pl.when(is_mate)
        def _():
            for k in range(2):
                share_copy(k).wait_send()
            for c in range(pieces):
                cross_copy(0, c).wait_send()
                cross_copy(1, c).wait_send()
                home_copy(c).wait_send()

        for n in range(2):
            for right in (True, False):

                @pl.when(z < ring - 1 if right else z > 0)
                def _():
                    line_copy(n, z, right).wait_send()

                for d in range(1, ring):
                    zs, there_is = upstream(d, right)

                    @pl.when(there_is)
                    def _():
                        line_share(n, zs).wait_send()

                        @pl.when(z < ring - 1 if right else z > 0)
                        def _():
                            line_copy(n, zs, right).wait_send()

    def line_copy(n, zs, right):
        ref = line.at[n, zs * count + t % 2]
        way = 0 if right else 1
        return pltpu.make_async_remote_copy(
            src_ref=ref, dst_ref=ref, send_sem=li_s.at[n, way, zs], recv_sem=li_r.at[n, way, zs],
            device_id={"dp": (z + 1) % ring if right else (z + ring - 1) % ring}, device_id_type=MESH,
        )

    def line_share(n, zs):
        ref = line.at[n, zs * count + t % 2]
        return pltpu.make_async_remote_copy(
            src_ref=ref, dst_ref=ref, send_sem=li_s.at[n, 2, zs], recv_sem=li_r.at[n, 2, zs],
            device_id={"tensor": core}, device_id_type=MESH,
        )

    def upstream(d, right):
        return (z - d, z >= d) if right else (z + d, z + d < ring)

    def line_start(n):
        if chained:
            for right in (True, False):

                @pl.when(z < ring - 1 if right else z > 0)
                def _():
                    line_copy(n, z, right).start()

    def line_pass(n, d):
        for right in (True, False) if chained else ():
            zs, there_is = upstream(d, right)

            @pl.when(there_is)
            def _():
                line_copy(n, zs, right).wait_recv()

                @pl.when(z < ring - 1 if right else z > 0)
                def _():
                    line_copy(n, zs, right).start()

                line_share(n, zs).start()

    def mlp_own():
        at = pl.ds(pl.multiple_of(z * cut, cut), cut)
        for m, n, right in ((0, 1, act), (1, 0, dh)):
            mlp_ref[m] = sum(mm(line[n, base + i, at, :], right[i]) for i in range(count))

    def mlp_of(d, right):
        at = pl.ds(pl.multiple_of(z * cut, cut), cut)

        def one(zs):
            for n in range(2):
                line_share(n, zs).wait_recv()

            def step(j, carry):
                slot = zs * count + j // pieces
                cols = pl.ds(pl.multiple_of(j % pieces * (width // pieces), 128), width // pieces)
                v = mm(partial[0, cols, :], line[0, slot])
                value, slope = gelu_parts(v)
                back = (mm(w2_ref[cols, :], line[1, slot]) * slope).astype(BF16)
                mlp_ref[0, :, cols] += mm_nt(line[1, slot, at, :], value.astype(BF16))
                mlp_ref[1, :, cols] += mm_nt(line[0, slot, at, :], back)
                return carry

            lax.fori_loop(0, count * pieces, step, 0)

        zs, there_is = upstream(d, right)
        pl.when(there_is)(functools.partial(one, zs))

    def turn_image(k, i):
        ref, n = place[k]
        ref[n, base + i if ref is line else i] = gath[k % 3, i].T

    def turn(k):
        for i in range(count):
            turn_image(k, i)

    def each_image(body):
        def run(i, carry):
            body(i)
            return carry

        lax.fori_loop(0, count, run, 0)

    def norm(x, which, i):
        mean = jnp.mean(x, axis=-1, keepdims=True)
        centre = x - mean
        root = lax.rsqrt(jnp.mean(centre * centre, axis=-1, keepdims=True) + EPS)
        hat = centre * root
        xhat[which, i] = hat
        inv[which, i] = jnp.broadcast_to(root, (rows, 128))
        return (hat * gain_ref[which : which + 1, :] + shift_ref[which : which + 1, :]).astype(BF16)

    def norm_back(da, which, i):
        hat = xhat[which, i]
        tiny_s[0, which : which + 1, :] += jnp.sum(da * hat, axis=0, keepdims=True)
        tiny_s[0, 2 + which : 3 + which, :] += jnp.sum(da, axis=0, keepdims=True)
        dhat = da * gain_ref[which : which + 1, :]
        m1 = jnp.mean(dhat, axis=-1, keepdims=True)
        m2 = jnp.mean(dhat * hat, axis=-1, keepdims=True)
        return inv[which, i][:, :1] * (dhat - m1 - hat * m2)

    def turn_qkv():
        loads[1].wait()
        for r in range(0, width, wide):
            for c in range(3):
                partial[1, r : r + wide, c * wide : c * wide + local] = wq_ref[
                    c * local : (c + 1) * local, r : r + wide
                ].T

    def turn_weight(to, ref):
        for r in range(0, width, wide):
            to[r : r + wide, : ref.shape[0]] = ref[:, r : r + wide].T

    def lead(k, end, near):
        def first(i):
            end(i)

            @pl.when(i == count - 1)
            def _():
                ag_pass(k, 0)

            ag_near(k, i)
            near(i)

        each_image(first)

    def follow(k, rest):
        def second(i):
            ag_rest(k, i)
            rest(i)

            @pl.when(i < count - 1)
            def _():
                ag_pass(k, i + 1)

            rs_pass(k, i)

        each_image(second)

    tiny_s[...] = jnp.zeros_like(tiny_s)
    tok_ref[z] = jnp.zeros_like(tok_ref[z])
    emb_ref[z] = jnp.zeros_like(emb_ref[z])
    emb_ref[z, :count, :] = temb_ref[...].astype(F32)
    over_ring(lambda j: tiny_copy(0, j).start())

    @pl.when(s == 1)
    def _():
        def begin(i):
            gath[DMLP, i, own, :] = cot_ref[i]
            ag_start(DMLP, i)

        each_image(begin)

    def take_input(i):
        @pl.when(s == 0)
        def _():
            xin[i] = x_ref[i]

        @pl.when(s == 1)
        def _():
            mid_copy(i).wait_recv()

        gath[ATT, i, own, :] = norm(xin[i].astype(F32), 0, i)
        ag_start(ATT, i)

    lane = lax.broadcasted_iota(jnp.int32, (1, 2 * seq), 1)

    def tables():
        valid = lane < (2 * grid - 1) * grid
        slab = pltpu.roll(wider(rel_ref[:grid, :], 2 * seq), grid * (grid - 1), 1)
        for k in range(grid - 1):
            r = grid - 1 - k
            block = only(rel_ref[r * grid : (r + 1) * grid, :128], 0, grid)
            slab += pltpu.roll(wider(block, 2 * seq), k * grid, 1)
        none = jnp.full((1, 2 * seq), -1, jnp.int32)
        before = none
        for c in range(1, grid):
            moved = pltpu.roll(slab[c : c + 1, :], grid - c, 1)
            before = jnp.where((lane % grid == grid - c) & valid, moved, before)
        order = jnp.concatenate([jnp.where(valid, slab[:1, :], none), before], axis=1)
        step = 128
        for r in range(0, chosen.shape[0], step):
            bucket = r + lax.broadcasted_iota(jnp.int32, (step, 4 * seq), 0)
            chosen[r : r + step, :] = jnp.where(bucket == order, 1.0, 0.0).astype(BF16)
        tab[...] = jnp.zeros_like(tab)
        tab[:heads, : tab_ref.shape[1]] = tab_ref[...]
        found = add_thirds(mm(in_thirds(tab[...]), chosen[...]))
        after, before = found[:, : 2 * seq], found[:, 2 * seq :]
        for c in range(grid):
            low = pltpu.roll(after, c, 1) if c else after
            high = pltpu.roll(before, 2 * seq - (grid - c), 1)
            row = jnp.where(lane % grid >= c, low, high)
            for h in range(heads):
                tx_ref[h, c : c + 1, :] = row[h : h + 1, :]

        def expand(h, carry):
            for r in range(grid):
                shift = (2 * seq - grid * (grid - 1 - r)) % (2 * seq)
                bias[h, r * grid : (r + 1) * grid, :] = pltpu.roll(tx_ref[h], shift, 1)[:, :seq]
            return carry

        lax.fori_loop(0, heads, expand, 0)
        loads[0].wait()
        tp_ref[...] = jnp.zeros_like(tp_ref)
        emb = jnp.concatenate([temb_ref[...], jnp.zeros((16 - count, width), BF16)], axis=0)
        for c in range(3):
            tp_ref[c] = mm_nt(emb, partial[0, c * local : (c + 1) * local, :])

    @pl.when(s == 1)
    def _():
        tables()

        def spread_cot(i):
            ag_pass(DMLP, i)
            ag_near(DMLP, i)
            ag_rest(DMLP, i)

        each_image(spread_cot)
        turn(DMLP)
        line_start(1)
        turn_qkv()
        loads[2].wait()
        turn_weight(sums.at[0], wo_ref)
        loads[3].wait()
        turn_weight(partial.at[0], w1_ref)
        loads[4].wait()

        def early(i):
            dh[i] = mm_nt(gath[DMLP, i], w2_ref[...]).astype(BF16)

        each_image(early)
        line_pass(1, 1)

    @pl.when(s == 0)
    def _():
        each_image(take_input)
        tables()
        turn_qkv()
        for n in (2, 3, 4):
            loads[n].wait()

    def project(i, half):
        a = gath[ATT, i, half_of(half), :]
        part = mm(a, partial[1, :, : 2 * wide + local])
        for c in range(3):
            qkv[c, i, half_of(half), :] = (
                part[:, c * wide : c * wide + local] + tp_ref[c, pl.ds(i, 1), :]
            ).astype(BF16)

    def att_first(i):
        @pl.when(s == 1)
        def _():
            take_input(i)

    lead(ATT, att_first, lambda i: project(i, here))

    def att_rest(i):
        project(i, there)
        acc[0] = jnp.zeros_like(acc[0])
        for h, (lo, hi, start, stop) in enumerate(windows):
            q = only(qkv[0, i, :, lo:hi], start, stop)
            scores = mm_nt(q, qkv[1, i, :, lo:hi]) * scale + bias[h]
            top = jnp.max(scores, axis=-1, keepdims=True)
            expo = jnp.exp(scores - top)
            p = expo / jnp.sum(expo, axis=-1, keepdims=True)
            p = p.astype(BF16)
            prob[i, h] = p
            acc[0, :, lo:hi] += mm(p, only(qkv[2, i, :, lo:hi], start, stop))
        att[i] = acc[0, :, :local].astype(BF16)
        far_att[i] = pltpu.roll(acc[0], far_att.shape[-1] - local, 1).astype(BF16)
        rs_give(ATT, i, 0, mm(att[i, half_of(there), :], wo_ref[...]))
        rs_give(ATT, i, 1, mm(att[i, half_of(here), :], wo_ref[...]))

    follow(ATT, att_rest)

    turn(ATT)
    give_factor(0, 3 + full)

    def att_end(i):
        y = xin[i].astype(F32) + rs_take(ATT, i)
        ag_done(ATT, i)
        rs_done(ATT, i)
        ymid[i] = y
        gath[MLP, i, own, :] = norm(y, 1, i)
        ag_start(MLP, i)

    def mlp_half(i, half, which):
        a = gath[MLP, i, half_of(half), :]
        v = mm(a, w1_ref[...])
        value, slope = gelu_parts(v)
        act[i, half_of(half), :] = value.astype(BF16)
        dgel[i, half_of(half), :] = slope.astype(BF16)
        rs_give(MLP, i, which, mm(act[i, half_of(half), :], w2_ref[...]))

    lead(MLP, att_end, lambda i: mlp_half(i, here, 1))
    follow(MLP, lambda i: mlp_half(i, there, 0))
    turn(MLP)
    line_start(0)

    def mlp_end(i):
        mid[i] = (ymid[i] + rs_take(MLP, i)).astype(BF16)
        rs_done(MLP, i)

        @pl.when(s == 0)
        def _():
            mid_copy(i).start()

        @pl.when(s == 1)
        def _():
            out_ref[i] = mid[i]
            out_copy(i).start()

    def take_grad(i):
        mid_copy(i).wait_send()
        grad_copy(i).wait_recv()
        gath[DMLP, i, own, :] = gin[i]
        ag_start(DMLP, i)

    def dmlp_half(i, half, which):
        @pl.when(s == 0)
        def _():
            dh[i, half_of(half), :] = mm(gath[DMLP, i, half_of(half), :], partial[1]).astype(BF16)

        dact = dh[i, half_of(half), :].astype(F32)
        dh[i, half_of(half), :] = (dact * dgel[i, half_of(half), :].astype(F32)).astype(BF16)
        rs_give(DMLP, i, which, mm(dh[i, half_of(half), :], partial[0]))

    @pl.when(s == 0)
    def _():
        each_image(mlp_end)
        turn_weight(partial.at[0], w1_ref)
        turn_weight(partial.at[1], w2_ref)
        turn_weight(sums.at[0], wo_ref)
        for d in range(1, ring):
            line_pass(0, d)
        lead(DMLP, take_grad, lambda i: dmlp_half(i, here, 1))

    def dmlp_rest(i):
        @pl.when(s == 0)
        def _():
            ag_rest(DMLP, i)

            @pl.when(i == count - 1)
            def _():
                turn(DMLP)
                line_start(1)

        dmlp_half(i, there, 0)

        @pl.when(s == 1)
        def _():
            dmlp_half(i, here, 1)

        @pl.when((s == 0) & (i < count - 1))
        def _():
            ag_pass(DMLP, i + 1)

        rs_pass(DMLP, i)

    each_image(dmlp_rest)
    @pl.when(s == 1)
    def _():
        def keep_cot(i):
            gin[i] = cot_ref[i]
            mlp_end(i)

        each_image(keep_cot)

    def dmlp_end(i):
        grad = gin[i].astype(F32) + norm_back(rs_take(DMLP, i), 1, i)
        ymid[i] = grad
        gath[DATT % 3, i, own, :] = grad.astype(BF16)
        ag_start(DATT, i)

    def datt_part(i, half):
        att[i, half_of(half), :] = mm(
            gath[DATT % 3, i, half_of(half), :], sums[0, :, :local]
        ).astype(BF16)

    lead(DATT, dmlp_end, lambda i: datt_part(i, here))

    @pl.when(s == 0)
    def _():
        line_pass(1, 1)

    def datt_rest(i):
        datt_part(i, there)

        turn_image(DATT, i)

        @pl.when(i == t % 2)
        def _():
            give_factor(1)

        acc[...] = jnp.zeros_like(acc)
        for h, (lo, hi, start, stop) in enumerate(windows):
            q = only(qkv[0, i, :, lo:hi], start, stop)
            k = only(qkv[1, i, :, lo:hi], start, stop)
            d = only(att[i, :, lo:hi], start, stop)
            low = prob[i, h]
            p = low.astype(F32)
            dp = mm_nt(d, qkv[2, i, :, lo:hi])
            inner = jnp.sum(p * dp, axis=-1, keepdims=True)
            ds = (p * (dp - inner)).astype(BF16)

            @pl.when(i == 0)
            def _():
                bias[h] = ds.astype(F32)

            @pl.when(i > 0)
            def _():
                bias[h] += ds.astype(F32)

            acc[0, :, lo:hi] += mm(ds, k)
            acc[1, :, lo:hi] += mm_tn(ds, q)
            acc[2, :, lo:hi] += mm_tn(low, d)
        tiles = [None] * (lanes // 128)
        for c, by in enumerate((scale, scale, 1.0)):
            first = c * local // 128
            moved = acc[c] * by
            if c * local > first * 128:
                moved = pltpu.roll(moved, c * local - first * 128, 1)
            for n in range(moved.shape[1] // 128):
                tile = moved[:, n * 128 : (n + 1) * 128]
                tiles[first + n] = tile if tiles[first + n] is None else tiles[first + n] + tile
        per = wide // 128
        over_tokens = []
        for c in range(full + 1):
            part = jnp.concatenate(tiles[c * per : (c + 1) * per], axis=1).astype(BF16)
            if c < full:
                dqkv[c, i] = part
            else:
                dtail[i] = part
            over_tokens.append(jnp.sum(part.astype(F32), axis=0, keepdims=True))
        tok_ref[z, pl.ds(i, 1), :lanes] = jnp.concatenate(over_tokens, axis=1)
        last = 3 * local - full * wide
        for which, half in ((0, there), (1, here)):
            da = mm(dtail[i, half_of(half), :last], wq_ref[full * wide :, :])
            for c in range(full):
                da += mm(dqkv[c, i, half_of(half), :], wq_ref[c * wide : (c + 1) * wide, :])
            rs_give(DATT, i, which, da)

    follow(DATT, datt_rest)

    give_factor(2 + full, *range(2, 2 + full))

    @pl.when(s == 1)
    def _():
        line_pass(0, 1)

    def first_parts():
        mlp_own()
        mlp_of(1, True)
        share_factor(0)
        share_factor(1)
        give_rest(full)

    if chained:
        pl.when(s == 0)(first_parts)
    line_pass(1, 2)

    def datt_end(i):
        grad = ymid[i] + norm_back(rs_take(DATT, i), 0, i)
        ig_ref[i] = grad.astype(BF16)

        @pl.when(s == 1)
        def _():
            grad_copy(i).start()

    each_image(datt_end)

    for j in range(3):
        small_copy(0, j).start()

    def fold(h, carry):
        total = jnp.zeros((grid, 2 * seq), F32)
        for r in range(grid):
            part = wider(bias[h, r * grid : (r + 1) * grid, :], 2 * seq)
            shift = grid * (grid - 1 - r)
            total += part if shift == 0 else pltpu.roll(part, shift, 1)
        after = total[:1, :]
        before = jnp.zeros((1, 2 * seq), F32)
        for c in range(1, grid):
            row = total[c : c + 1, :]
            late = lane % grid >= c
            after += pltpu.roll(jnp.where(late, row, 0.0), 2 * seq - c, 1)
            before += pltpu.roll(jnp.where(late, 0.0, row), grid - c, 1)
        tok_ref[z, pl.ds(count + h, 1), : 4 * seq] = jnp.concatenate([after, before], axis=1)
        return carry

    lax.fori_loop(0, heads, fold, 0)
    for j in range(3):
        small_copy(0, j).wait_recv()
    over_tensor = tiny_s[0] + small_r[0, 0] + small_r[0, 1] + small_r[0, 2]
    row = lax.broadcasted_iota(jnp.int32, over_tensor.shape, 0)
    tok_ref[z, count + heads : count + heads + 1, :] = jnp.sum(
        jnp.where(row == t, over_tensor, 0.0), axis=0, keepdims=True
    )
    over_ring(lambda j: tiny_copy(1, j).start())

    if chained:

        @pl.when(s == 1)
        def _():
            line_pass(0, 2)

            first_parts()

        give_rest(0)
        mlp_of(1, False)
        relay(full)
        for c in range(1, full):
            give_rest(c)
        relay(0)
        mlp_of(2, True)
        mlp_of(2, False)

        @pl.when(s == 1)
        def _():
            line_pass(0, 3)

        line_pass(1, 3)
        for c in range(1, full):
            relay(c)
        mlp_of(3, True)
        mlp_of(3, False)
    else:

        def whole(b, carry):
            at = block(b)
            tot_ref[0, b] = sum(mm(line[1, i, at, :], act[i]) for i in range(count)).astype(BF16)
            tot_ref[1, b] = sum(mm(line[0, i, at, :], dh[i]) for i in range(count)).astype(BF16)
            tot_ref[2, b] = jnp.concatenate(
                [rest_product(c, at, 0) for c in range(full + 1)], axis=1
            ).astype(BF16)
            return carry

        lax.fori_loop(0, blocks, whole, 0)
    over_ring(lambda j: tiny_copy(1, j).wait_recv())

    def add_slot(j, total):
        return total + tok_ref[j]

    total = lax.fori_loop(0, ring, add_slot, jnp.zeros(tok_ref.shape[1:], F32))
    tiny_s[1] = total
    tab[...] = jnp.zeros_like(tab)
    tab[:heads, :] = tiny_s[1, count : count + heads, : 4 * seq]
    found = add_thirds(mm_nt(in_thirds(tab[...]), chosen[...]))
    gtab_ref[...] = found[:heads, : gtab_ref.shape[1]]
    for j in range(3):
        small_copy(1, j).start()
    if chained:
        for c in (full, *range(full)):
            settle(c)
    for j in range(3):
        small_copy(1, j).wait_recv()
    last = count + heads
    small_ref[pl.ds(t, 1), :] = tiny_s[1, last : last + 1, :]
    for j, owner in enumerate((core, far, fcore)):
        small_ref[pl.ds(owner, 1), :] = small_r[1, j, last : last + 1, :]

    def finish(i):
        for k in (MLP, DMLP, DATT):
            ag_done(k, i)
        rs_done(DMLP, i)
        rs_done(DATT, i)

        @pl.when(s == 0)
        def _():
            out_copy(i).wait_recv()

        @pl.when(s == 1)
        def _():
            out_copy(i).wait_send()
            grad_copy(i).wait_send()

    each_image(finish)

    def tiny_left(j):
        tiny_copy(0, j).wait_recv()
        tiny_copy(0, j).wait_send()
        tiny_copy(1, j).wait_send()

    over_ring(tiny_left)
    for j in range(3):
        small_copy(0, j).wait_send()
        small_copy(1, j).wait_send()
    if chained:
        weights_left()


def run_block(x, cot, wq, wt, wo, w1, w2, temb, gain, shift, rel, table, ring):
    count, rows, width = x.shape
    seq = rel.shape[0]
    heads = table.shape[0]
    local = wo.shape[0]
    hidden = w1.shape[1]
    chained = ring == 4 and count == 2 and width % (16 * ring) == 0
    blocks = 4
    pieces = 3 if width // 4 % 48 == 0 else 1
    cut = width // blocks
    padded = -(-local // 128) * 128
    lanes = -(-3 * local // 128) * 128
    dims = (count, rows, seq, heads, ring, chained)
    total = (cut, width) if chained else (3, blocks, cut, width)
    full = 3 * local // padded
    assert pieces == full + 1 and padded * pieces == width
    out_shape = [
        jax.ShapeDtypeStruct((count, rows, width), BF16),
        jax.ShapeDtypeStruct((count, rows, width), BF16),
        jax.ShapeDtypeStruct(total, BF16),
        jax.ShapeDtypeStruct((2, cut, width) if chained else (2, 8, 128), F32),
        jax.ShapeDtypeStruct((ring, 8, width), F32),
        jax.ShapeDtypeStruct((ring, 8, width), F32),
        jax.ShapeDtypeStruct(table.shape, F32),
        jax.ShapeDtypeStruct((4, width), F32),
    ]
    vm = pltpu.VMEM
    dma = pltpu.SemaphoreType.DMA
    scratch = [
        vm(wq.shape, BF16),
        vm(wo.shape, BF16),
        vm(w1.shape, BF16),
        vm(w2.shape, BF16),
        vm((3, 16, local), F32),
        vm((heads, int(round(seq**0.5)), 2 * seq), F32),
        vm((4 * seq, 4 * seq), BF16),
        vm((16, 4 * seq), F32),
        vm((2, width, width), BF16),
        vm((pieces, width, padded), BF16),
        vm((2, pieces, cut, padded) if chained else (16, 128), BF16),
        vm((2, 8, width), F32),
        vm((2, 3, 8, width), F32),
        vm((count, rows, width), BF16),
        vm((count, rows, width), BF16),
        vm((count, rows, width), BF16),
        vm((3, count, seq, width), BF16),
        vm((2, count, 2, rows, width), F32),
        vm((2, count, 2, rows, width), BF16),
        vm((2, count, rows, width), BF16),
        vm((2, count, 2, rows, width), BF16),
        vm((2, count, rows, width), BF16),
        vm((heads, seq, seq), F32),
        vm((count, heads, seq, seq), BF16),
        vm((3, count, seq, local), BF16),
        vm((count, seq, local), BF16),
        vm((count, seq, hidden), BF16),
        vm((count, seq, hidden), BF16),
        vm((2, count, rows, width), F32),
        vm((2, count, rows, 128), F32),
        vm((count, rows, width), F32),
        vm((full, count, seq, padded), BF16),
        vm((count, seq, lanes - full * padded), BF16),
        vm((count, seq, hidden), BF16),
        vm((3, seq, padded), F32),
        vm((2, 2 * count if chained else count, width, seq), BF16),
        vm((2, ring * count if chained else count, width, seq), BF16),
        vm((count, seq, padded), BF16),
        vm((full, count, seq, padded) if chained else (16, 128), BF16),
        vm((count, seq, lanes - full * padded) if chained else (16, 128), BF16),
        vm((count, seq, padded) if chained else (16, 128), BF16),
        dma((5,)),
        dma((4, count, 3)),
        dma((4, count, 3)),
        dma((4, count, 3)),
        dma((4, count, 3)),
        dma((3, count)),
        dma((3, count)),
        dma((3, pieces)),
        dma((2, pieces)),
        dma((6 + full,)),
        dma((6 + full,)),
        dma((2, 3, ring)),
        dma((2, 3, ring)),
        dma((2, ring)),
        dma((2, ring)),
        dma((2, 3)),
        dma((2, 3)),
    ]
    whole = pl.BlockSpec(memory_space=pltpu.VMEM)
    lies = pl.BlockSpec(memory_space=pl.ANY)
    return pl.pallas_call(
        functools.partial(block_kernel, dims),
        out_shape=out_shape,
        in_specs=[whole] * 2 + [lies] * 5 + [whole] * 5,
        out_specs=[whole] * len(out_shape),
        scratch_shapes=scratch,
        compiler_params=pltpu.CompilerParams(
            collective_id=0, has_side_effects=True, vmem_limit_bytes=63 * 2**20
        ),
        name="blocks",
    )(x, cot, wq, wt, wo, w1, w2, temb, gain, shift, rel, table)


def per_device(
    images, timesteps, t_table, rel_index, w_qkv, w_time, w_out, w_fc1, w_fc2, rel_table,
    norm_gain, norm_shift, cotangent,
):
    ring = lax.axis_size("dp")
    count = images.shape[0]
    width = images.shape[-1]
    local = w_out.shape[1]
    cut = width // ring
    embedded = t_table[timesteps]
    wq = jnp.transpose(w_qkv[0], (1, 2, 0)).reshape(3 * local, width)
    wt = jnp.transpose(w_time[0], (1, 2, 0)).reshape(3 * local, width)
    output, in_grad, total, mlp, sums, emb, g_table, small = run_block(
        images, cotangent, wq, wt, w_out[0], w_fc1[0], w_fc2[0], embedded, norm_gain[0], norm_shift[0],
        rel_index, rel_table[0].T, ring,
    )
    if total.ndim == 2:
        g_fc2, g_fc1 = mlp[0].T, mlp[1]
        rest = total.astype(F32)
    else:
        total = lax.psum_scatter(
            total.reshape(3, width, width), "dp", scatter_dimension=1, tiled=True
        ).astype(F32)
        g_fc2, g_fc1, rest = total[0].T, total[1], total[2]
    g_qkv = rest[:, : 3 * local].reshape(cut, 3, local)
    g_out = rest[:, 3 * local :].T
    sums = sums[:, :count, : 3 * local].reshape(ring * count, 3, local)
    emb = emb[:, :count].reshape(ring * count, width)
    emb = lax.dynamic_slice_in_dim(emb, lax.axis_index("dp") * cut, cut, axis=1)
    g_time = jnp.einsum("id,icj->dcj", emb, sums, precision=lax.Precision.HIGHEST)
    return (
        output, in_grad[None], g_qkv[None], g_time[None], g_out[None], g_fc1[None], g_fc2[None],
        g_table.T[None], small[None, :2], small[None, 2:],
    )


def solution(mesh):
    in_specs = (
        P("dp", "tensor", None),
        P("dp"),
        P(),
        P(),
        P("section", None, None, "tensor"),
        P("section", None, None, "tensor"),
        P("section", "tensor", None),
        P("section", None, "tensor"),
        P("section", "tensor", None),
        P("section", None, "tensor"),
        P("section", None, None),
        P("section", None, None),
        P("dp", "tensor", None),
    )
    out_specs = (
        P("dp", "tensor", None),
        P("section", "dp", "tensor", None),
        P("section", "dp", None, "tensor"),
        P("section", "dp", None, "tensor"),
        P("section", "tensor", "dp"),
        P("section", "dp", "tensor"),
        P("section", "tensor", "dp"),
        P("section", None, "tensor"),
        P("section", None, None),
        P("section", None, None),
    )
    return jax.shard_map(
        per_device, mesh=mesh, in_specs=in_specs, out_specs=out_specs, check_vma=False
    )
```

```python
import functools

import jax
import jax.numpy as jnp
from jax import lax
from jax.experimental import pallas as pl
from jax.experimental.pallas import tpu as pltpu
from jax.sharding import PartitionSpec as P

MESH = pl.DeviceIdType.MESH
F32 = jnp.float32
BF16 = jnp.bfloat16
EPS = 1e-06
GELU_A = 0.7978845608028654
GELU_B = 0.044715
ATT, MLP, DMLP, DATT = range(4)
slot_of = (0, 1, 0, 0)


def mm(a, b):
    return lax.dot_general(a, b, (((1,), (0,)), ((), ())), preferred_element_type=F32)


def mm_nt(a, b):
    return lax.dot_general(a, b, (((1,), (1,)), ((), ())), preferred_element_type=F32)


def mm_tn(a, b):
    return lax.dot_general(a, b, (((0,), (0,)), ((), ())), preferred_element_type=F32)


def gelu_parts(v):
    square = v * v
    th = jnp.tanh(v * (GELU_A + (GELU_A * GELU_B) * square))
    up = 0.5 + 0.5 * th
    slope = up + v * (1.0 - th * th) * (0.5 * GELU_A + (1.5 * GELU_A * GELU_B) * square)
    return v * up, slope


def head_windows(heads, local):
    width = local // heads
    found = []
    for h in range(heads):
        lo = h * width // 128 * 128
        hi = min(-(-(h + 1) * width // 128) * 128, local)
        found.append((lo, hi, h * width - lo, (h + 1) * width - lo))
    return found


def only(x, start, stop):
    lane = lax.broadcasted_iota(jnp.int32, x.shape, 1)
    return jnp.where((lane >= start) & (lane < stop), x, jnp.zeros_like(x))


def in_thirds(x):
    high = x.astype(BF16)
    rest = x - high.astype(F32)
    middle = rest.astype(BF16)
    low = (rest - middle.astype(F32)).astype(BF16)
    return jnp.concatenate([high, middle, low], axis=0)


def add_thirds(x):
    rows = x.shape[0] // 3
    return x[:rows] + x[rows : 2 * rows] + x[2 * rows :]


def wider(x, lanes):
    return jnp.concatenate([x, jnp.zeros((x.shape[0], lanes - x.shape[1]), x.dtype)], axis=1)


def block_kernel(
    cfg,
    x_hbm, cot_hbm, wq_hbm, wt_hbm, wo_hbm, w1_hbm, w2_hbm, temb_hbm, gain_hbm, shift_hbm, rel_hbm, tab_hbm,
    out_hbm, ig_hbm, parts_ref, g2_hbm, g1_hbm, gq_hbm, go_hbm, gt_hbm, gtab_hbm, ggain_hbm, gshift_hbm,
    temb_ref, gain_ref, shift_ref, rel_ref, tab_ref, out_ref, ig_ref, tot_ref, mlp_ref, stage, tok_ref, emb_ref,
    gtab_ref, small_ref, ggain_ref, gshift_ref,
    wq_ref, wo_ref, w1_ref, w2_ref, tp_ref, tx_ref, chosen, tab, partial, sums, arrived,
    tiny_s, small_r,
    xin, mid, gath, keep, rcv_c, rcv_y, snd_c, snd_y, bias, prob, qkv, att, act, dgel,
    xhat, inv, ymid, dy1, dqkv, dtail, dh, acc, turned, line, far_att, dqkv2, dtail2, far_att2,
    load_s, store_s, ag_s, ag_r, rs_s, rs_r, sec_s, sec_r, ch_s, ch_r, fac_s, fac_r, li_s, li_r, ti_s, ti_r, sm_s, sm_r,
):
    count, rows, seq, heads, ring, chained = cfg
    half_rows = 2 * rows
    wide = -(-wo_ref.shape[0] // 128) * 128
    width = x_hbm.shape[-1]
    local = wo_ref.shape[0]
    grid = int(round(seq**0.5))
    windows = head_windows(heads, local)
    scale = (local // heads) ** (-0.5)
    blocks = 4
    cut = width // blocks
    pieces = sums.shape[0]
    slim = cut // pieces
    full = dqkv.shape[0]
    lanes = full * dqkv.shape[-1] + dtail.shape[-1]

    s = lax.axis_index("section")
    t = lax.axis_index("tensor")
    z = lax.axis_index("dp")
    core = t + 1 - 2 * (t % 2)
    far = (t + 2) % 4
    fcore = (core + 2) % 4
    here = t // 2
    there = 1 - here
    own = pl.ds(pl.multiple_of(t * rows, rows), rows)

    wt_ref = partial.at[0, : 3 * local, :]

    loads = [
        pltpu.make_async_copy(src, dst, load_s.at[n])
        for n, (src, dst) in enumerate(
            (
                (wt_hbm, wt_ref), (wq_hbm, wq_ref), (wo_hbm, wo_ref), (w1_hbm, w1_ref), (w2_hbm, w2_ref),
                (temb_hbm, temb_ref), (gain_hbm, gain_ref), (shift_hbm, shift_ref), (rel_hbm, rel_ref),
                (tab_hbm, tab_ref),
            )
        )
    ]
    first_rows = pltpu.make_async_copy(x_hbm, xin, load_s.at[10])
    last_rows = pltpu.make_async_copy(cot_hbm, xin, load_s.at[11])

    def cot_rows(i):
        return pltpu.make_async_copy(cot_hbm.at[i], gath.at[DMLP, i, own, :], load_s.at[12 + i])

    @pl.when(s == 0)
    def _():
        first_rows.start()

    @pl.when(s == 1)
    def _():
        for i in range(count):
            cot_rows(i).start()

    for load in loads[5:] + loads[:5]:
        load.start()

    barrier = pltpu.get_barrier_semaphore()
    for peer in ({"tensor": core}, {"tensor": far}, {"tensor": fcore}, {"section": 1 - s}):
        pl.semaphore_signal(barrier, inc=1, device_id=peer, device_id_type=MESH)

    def greet(j, carry):
        pl.semaphore_signal(barrier, inc=1, device_id={"dp": (z + j) % ring}, device_id_type=MESH)
        return carry

    lax.fori_loop(1, ring, greet, 0)
    pl.semaphore_wait(barrier, 3 + ring)

    def rows_of(owner):
        return pl.ds(pl.multiple_of(owner * rows, rows), rows)

    def half_of(half):
        return pl.ds(pl.multiple_of(half * half_rows, half_rows), half_rows)

    def ag_copy(k, i, which):
        owner, to = ((t, core), (t, far), (far, core))[which]
        ref = gath.at[k % 3, i, rows_of(owner), :]
        return pltpu.make_async_remote_copy(
            src_ref=ref, dst_ref=ref, send_sem=ag_s.at[k, i, which], recv_sem=ag_r.at[k, i, which],
            device_id={"tensor": to}, device_id_type=MESH,
        )

    def ag_start(k, i):
        ag_copy(k, i, 1).start()
        ag_copy(k, i, 0).start()

    def ag_near(k, i):
        ag_copy(k, i, 0).wait_recv()

    def ag_pass(k, i):
        ag_copy(k, i, 1).wait_recv()
        ag_copy(k, i, 2).start()

    def ag_rest(k, i):
        ag_copy(k, i, 2).wait_recv()

    def ag_done(k, i):
        for which in range(3):
            ag_copy(k, i, which).wait_send()

    def rs_copy(k, i, which):
        if which < 2:
            src, dst, to = snd_c.at[slot_of[k], i, which], rcv_c.at[slot_of[k], i, which], core
        else:
            src, dst, to = snd_y.at[slot_of[k], i], rcv_y.at[slot_of[k], i], far
        return pltpu.make_async_remote_copy(
            src_ref=src, dst_ref=dst, send_sem=rs_s.at[k, i, which], recv_sem=rs_r.at[k, i, which],
            device_id={"tensor": to}, device_id_type=MESH,
        )

    def rs_give(k, i, which, part):
        odd = t % 2 == 1
        low, high = part[:rows], part[rows:]
        snd_c[slot_of[k], i, which] = jnp.where(odd, low, high).astype(BF16)
        rs_copy(k, i, which).start()
        keep[slot_of[k], i, which] = jnp.where(odd, high, low)

    def rs_pass(k, i):
        rs_copy(k, i, 0).wait_recv()
        snd_y[slot_of[k], i] = (keep[slot_of[k], i, 0] + rcv_c[slot_of[k], i, 0].astype(F32)).astype(BF16)
        rs_copy(k, i, 2).start()

    def rs_take(k, i):
        rs_copy(k, i, 1).wait_recv()
        near = keep[slot_of[k], i, 1] + rcv_c[slot_of[k], i, 1].astype(F32)
        rs_copy(k, i, 2).wait_recv()
        return near + rcv_y[slot_of[k], i].astype(F32)

    def rs_done(k, i):
        for which in range(3):
            rs_copy(k, i, which).wait_send()

    def sec_copy(j, src, dst):
        return lambda i: pltpu.make_async_remote_copy(
            src_ref=src.at[i], dst_ref=dst.at[i], send_sem=sec_s.at[j, i], recv_sem=sec_r.at[j, i],
            device_id={"section": 1 - s}, device_id_type=MESH,
        )

    mid_copy = sec_copy(0, mid, xin)
    grad_copy = sec_copy(1, ig_ref, xin)
    out_copy = sec_copy(2, out_ref, out_ref)

    def tiny_copy(n, j):
        ref = (emb_ref, tok_ref)[n]
        return pltpu.make_async_remote_copy(
            src_ref=ref.at[z], dst_ref=ref.at[z], send_sem=ti_s.at[n, j], recv_sem=ti_r.at[n, j],
            device_id={"dp": (z + j) % ring}, device_id_type=MESH,
        )

    def over_ring(body):
        def run(j, carry):
            body(j)
            return carry

        lax.fori_loop(1, ring, run, 0)

    def small_copy(n, j):
        return pltpu.make_async_remote_copy(
            src_ref=tiny_s.at[n], dst_ref=small_r.at[n, j], send_sem=sm_s.at[n, j], recv_sem=sm_r.at[n, j],
            device_id={"tensor": (core, far, fcore)[j]}, device_id_type=MESH,
        )

    mate = z + 1 - 2 * (z % 2)
    across = 3 - z
    beyond = 3 * (2 - z)
    is_end = (z == 0) | (z == 3)
    is_mate = (z == 1) | (z == 2)
    base = z * count if chained else 0
    place = {ATT: (turned, 0), DATT: (turned, 1), MLP: (line, 0), DMLP: (line, 1)}

    def block(b):
        return pl.ds(pl.multiple_of(b * cut, cut), cut)

    def factor_copy(n):
        if n < 2:
            src, dst = turned.at[n, t % 2], turned.at[n, count + t % 2]
        else:
            pairs = [(dqkv.at[c], dqkv2.at[c]) for c in range(full)] + [(dtail, dtail2), (far_att, far_att2)]
            src, dst = pairs[n - 2]
        return pltpu.make_async_remote_copy(
            src_ref=src, dst_ref=dst, send_sem=fac_s.at[n], recv_sem=fac_r.at[n],
            device_id={"dp": mate}, device_id_type=MESH,
        )

    def share_copy(k):
        ref = turned.at[k, count + t % 2]
        return pltpu.make_async_remote_copy(
            src_ref=ref, dst_ref=ref, send_sem=fac_s.at[4 + full + k], recv_sem=fac_r.at[4 + full + k],
            device_id={"tensor": core}, device_id_type=MESH,
        )

    def give_factor(*which):
        if chained:

            @pl.when(is_end)
            def _():
                for n in which:
                    factor_copy(n).start()

    def share_factor(k):
        if chained:

            @pl.when(is_mate)
            def _():
                factor_copy(k).wait_recv()
                share_copy(k).start()

    def cross_copy(slot, c):
        return pltpu.make_async_remote_copy(
            src_ref=sums.at[c, block((beyond, across)[slot]), :], dst_ref=arrived.at[slot, c],
            send_sem=ch_s.at[slot, c], recv_sem=ch_r.at[slot, c],
            device_id={"dp": across}, device_id_type=MESH,
        )

    def home_copy(c):
        return pltpu.make_async_remote_copy(
            src_ref=sums.at[c, block(mate), :], dst_ref=arrived.at[0, c],
            send_sem=ch_s.at[2, c], recv_sem=ch_r.at[0, c],
            device_id={"dp": mate}, device_id_type=MESH,
        )

    def rest_product(c, at, side):
        def by(n, right):
            return sum(mm(turned[n, side * count + i, at, :], right[i]) for i in range(count))

        if c < full:
            return by(0, (dqkv, dqkv2)[side].at[c])
        return wider(by(0, (dtail, dtail2)[side]), wide) + by(1, (far_att, far_att2)[side])

    def give_rest(c):
        def alone(b):
            sums[c, block(b), :] = rest_product(c, block(b), 0).astype(BF16)

        def both(b):
            both_sides = rest_product(c, block(b), 0) + rest_product(c, block(b), 1)
            sums[c, block(b), :] = both_sides.astype(BF16)

        @pl.when(is_end)
        def _():
            alone(z)

        @pl.when(is_mate)
        def _():
            if c < full:
                factor_copy(2 + c).wait_recv()
            else:
                share_copy(0).wait_recv()
                share_copy(1).wait_recv()
                factor_copy(2 + full).wait_recv()
                factor_copy(3 + full).wait_recv()
            both(beyond)
            cross_copy(0, c).start()
            both(across)
            cross_copy(1, c).start()
            both(z)
            alone(mate)

    def relay(c):
        @pl.when(is_mate)
        def _():
            cross_copy(0, c).wait_recv()
            home = sums[c, block(mate), :].astype(F32) + arrived[0, c].astype(F32)
            sums[c, block(mate), :] = home.astype(BF16)
            home_copy(c).start()

    def settle(c):
        def finish(slot, copy):
            copy.wait_recv()
            whole = sums[c, block(z), :].astype(F32) + arrived[slot, c].astype(F32)
            tot_ref[:, c * wide : (c + 1) * wide] = whole.astype(BF16)

        @pl.when(is_mate)
        def _():
            finish(1, cross_copy(1, c))

        @pl.when(is_end)
        def _():
            finish(0, home_copy(c))

    def weights_left():
        @pl.when(is_end)
        def _():
            for n in range(4 + full):
                factor_copy(n).wait_send()

        @pl.when(is_mate)
        def _():
            for k in range(2):
                share_copy(k).wait_send()
            for c in range(pieces):
                cross_copy(0, c).wait_send()
                cross_copy(1, c).wait_send()
                home_copy(c).wait_send()

        for n in range(2):
            for right in (True, False):

                @pl.when(z < ring - 1 if right else z > 0)
                def _():
                    line_copy(n, z, right).wait_send()

                for d in range(1, ring):
                    zs, there_is = upstream(d, right)

                    @pl.when(there_is)
                    def _():
                        line_share(n, zs).wait_send()

                        @pl.when(z < ring - 1 if right else z > 0)
                        def _():
                            line_copy(n, zs, right).wait_send()

    def line_copy(n, zs, right):
        ref = line.at[n, zs * count + t % 2]
        way = 0 if right else 1
        return pltpu.make_async_remote_copy(
            src_ref=ref, dst_ref=ref, send_sem=li_s.at[n, way, zs], recv_sem=li_r.at[n, way, zs],
            device_id={"dp": (z + 1) % ring if right else (z + ring - 1) % ring}, device_id_type=MESH,
        )

    def line_share(n, zs):
        ref = line.at[n, zs * count + t % 2]
        return pltpu.make_async_remote_copy(
            src_ref=ref, dst_ref=ref, send_sem=li_s.at[n, 2, zs], recv_sem=li_r.at[n, 2, zs],
            device_id={"tensor": core}, device_id_type=MESH,
        )

    def upstream(d, right):
        return (z - d, z >= d) if right else (z + d, z + d < ring)

    def line_start(n):
        if chained:
            for right in (True, False):

                @pl.when(z < ring - 1 if right else z > 0)
                def _():
                    line_copy(n, z, right).start()

    def line_pass(n, d):
        for right in (True, False) if chained else ():
            zs, there_is = upstream(d, right)

            @pl.when(there_is)
            def _():
                line_copy(n, zs, right).wait_recv()

                @pl.when(z < ring - 1 if right else z > 0)
                def _():
                    line_copy(n, zs, right).start()

                line_share(n, zs).start()

    def mlp_own():
        at = pl.ds(pl.multiple_of(z * cut, cut), cut)
        for m, n, right in ((0, 1, act), (1, 0, dh)):
            mlp_ref[m] = sum(mm(line[n, base + i, at, :], right[i]) for i in range(count))

    def mlp_of(d, right):
        at = pl.ds(pl.multiple_of(z * cut, cut), cut)

        def one(zs):
            for n in range(2):
                line_share(n, zs).wait_recv()

            def step(j, carry):
                slot = zs * count + j // pieces
                cols = pl.ds(pl.multiple_of(j % pieces * (width // pieces), 128), width // pieces)
                v = mm(partial[0, cols, :], line[0, slot])
                value, slope = gelu_parts(v)
                back = (mm(w2_ref[cols, :], line[1, slot]) * slope).astype(BF16)
                mlp_ref[0, :, cols] += mm_nt(line[1, slot, at, :], value.astype(BF16))
                mlp_ref[1, :, cols] += mm_nt(line[0, slot, at, :], back)
                return carry

            lax.fori_loop(0, count * pieces, step, 0)

        zs, there_is = upstream(d, right)
        pl.when(there_is)(functools.partial(one, zs))

    def turn_image(k, i):
        ref, n = place[k]
        ref[n, base + i if ref is line else i] = gath[k % 3, i].T

    def turn(k):
        for i in range(count):
            turn_image(k, i)

    def each_image(body):
        def run(i, carry):
            body(i)
            return carry

        lax.fori_loop(0, count, run, 0)

    def norm(x, which, i):
        mean = jnp.mean(x, axis=-1, keepdims=True)
        centre = x - mean
        root = lax.rsqrt(jnp.mean(centre * centre, axis=-1, keepdims=True) + EPS)
        hat = centre * root
        xhat[which, i] = hat
        inv[which, i] = jnp.broadcast_to(root, (rows, 128))
        return (hat * gain_ref[which : which + 1, :] + shift_ref[which : which + 1, :]).astype(BF16)

    def norm_back(da, which, i):
        hat = xhat[which, i]
        tiny_s[0, which : which + 1, :] += jnp.sum(da * hat, axis=0, keepdims=True)
        tiny_s[0, 2 + which : 3 + which, :] += jnp.sum(da, axis=0, keepdims=True)
        dhat = da * gain_ref[which : which + 1, :]
        m1 = jnp.mean(dhat, axis=-1, keepdims=True)
        m2 = jnp.mean(dhat * hat, axis=-1, keepdims=True)
        return inv[which, i][:, :1] * (dhat - m1 - hat * m2)

    def turn_qkv():
        loads[1].wait()
        for r in range(0, width, wide):
            for c in range(3):
                partial[1, r : r + wide, c * wide : c * wide + local] = wq_ref[
                    c * local : (c + 1) * local, r : r + wide
                ].T

    def turn_weight(to, ref):
        for r in range(0, width, wide):
            to[r : r + wide, : ref.shape[0]] = ref[:, r : r + wide].T

    def lead(k, end, near):
        def first(i):
            end(i)

            @pl.when(i == count - 1)
            def _():
                ag_pass(k, 0)

            ag_near(k, i)
            near(i)

        each_image(first)

    def follow(k, rest):
        def second(i):
            ag_rest(k, i)
            rest(i)

            @pl.when(i < count - 1)
            def _():
                ag_pass(k, i + 1)

            rs_pass(k, i)

        each_image(second)

    tiny_s[...] = jnp.zeros_like(tiny_s)
    tok_ref[z] = jnp.zeros_like(tok_ref[z])
    emb_ref[z] = jnp.zeros_like(emb_ref[z])
    for load in loads[5:]:
        load.wait()
    emb_ref[z, :count, :] = temb_ref[...].astype(F32)
    over_ring(lambda j: tiny_copy(0, j).start())

    @pl.when(s == 1)
    def _():
        def begin(i):
            cot_rows(i).wait()
            ag_start(DMLP, i)

        each_image(begin)

    def take_input(i):
        @pl.when((s == 0) & (i == 0))
        def _():
            first_rows.wait()

        @pl.when(s == 1)
        def _():
            mid_copy(i).wait_recv()

        gath[ATT, i, own, :] = norm(xin[i].astype(F32), 0, i)
        ag_start(ATT, i)

    lane = lax.broadcasted_iota(jnp.int32, (1, 2 * seq), 1)

    def tables():
        valid = lane < (2 * grid - 1) * grid
        slab = pltpu.roll(wider(rel_ref[:grid, :], 2 * seq), grid * (grid - 1), 1)
        for k in range(grid - 1):
            r = grid - 1 - k
            block = only(rel_ref[r * grid : (r + 1) * grid, :128], 0, grid)
            slab += pltpu.roll(wider(block, 2 * seq), k * grid, 1)
        none = jnp.full((1, 2 * seq), -1, jnp.int32)
        before = none
        for c in range(1, grid):
            moved = pltpu.roll(slab[c : c + 1, :], grid - c, 1)
            before = jnp.where((lane % grid == grid - c) & valid, moved, before)
        order = jnp.concatenate([jnp.where(valid, slab[:1, :], none), before], axis=1)
        step = 128
        for r in range(0, chosen.shape[0], step):
            bucket = r + lax.broadcasted_iota(jnp.int32, (step, 4 * seq), 0)
            chosen[r : r + step, :] = jnp.where(bucket == order, 1.0, 0.0).astype(BF16)
        tab[...] = jnp.zeros_like(tab)
        tab[:heads, : tab_ref.shape[1]] = tab_ref[...]
        found = add_thirds(mm(in_thirds(tab[...]), chosen[...]))
        after, before = found[:, : 2 * seq], found[:, 2 * seq :]
        for c in range(grid):
            low = pltpu.roll(after, c, 1) if c else after
            high = pltpu.roll(before, 2 * seq - (grid - c), 1)
            row = jnp.where(lane % grid >= c, low, high)
            for h in range(heads):
                tx_ref[h, c : c + 1, :] = row[h : h + 1, :]

        def expand(h, carry):
            for r in range(grid):
                shift = (2 * seq - grid * (grid - 1 - r)) % (2 * seq)
                bias[h, r * grid : (r + 1) * grid, :] = pltpu.roll(tx_ref[h], shift, 1)[:, :seq]
            return carry

        lax.fori_loop(0, heads, expand, 0)
        loads[0].wait()
        tp_ref[...] = jnp.zeros_like(tp_ref)
        emb = jnp.concatenate([temb_ref[...], jnp.zeros((16 - count, width), BF16)], axis=0)
        for c in range(3):
            tp_ref[c] = mm_nt(emb, partial[0, c * local : (c + 1) * local, :])

    @pl.when(s == 1)
    def _():
        tables()

        def spread_cot(i):
            ag_pass(DMLP, i)
            ag_near(DMLP, i)
            ag_rest(DMLP, i)

        each_image(spread_cot)
        turn(DMLP)
        line_start(1)
        turn_qkv()
        loads[2].wait()
        turn_weight(sums.at[0], wo_ref)
        loads[3].wait()
        turn_weight(partial.at[0], w1_ref)
        loads[4].wait()

        def early(i):
            dh[i] = mm_nt(gath[DMLP, i], w2_ref[...]).astype(BF16)

        each_image(early)
        line_pass(1, 1)

    @pl.when(s == 0)
    def _():
        each_image(take_input)
        tables()
        turn_qkv()
        for n in (2, 3, 4):
            loads[n].wait()

    def project(i, half):
        a = gath[ATT, i, half_of(half), :]
        part = mm(a, partial[1, :, : 2 * wide + local])
        for c in range(3):
            qkv[c, i, half_of(half), :] = (
                part[:, c * wide : c * wide + local] + tp_ref[c, pl.ds(i, 1), :]
            ).astype(BF16)

    def att_first(i):
        @pl.when(s == 1)
        def _():
            take_input(i)

    lead(ATT, att_first, lambda i: project(i, here))

    def att_rest(i):
        project(i, there)
        acc[0] = jnp.zeros_like(acc[0])
        for h, (lo, hi, start, stop) in enumerate(windows):
            q = only(qkv[0, i, :, lo:hi], start, stop)
            scores = mm_nt(q, qkv[1, i, :, lo:hi]) * scale + bias[h]
            top = jnp.max(scores, axis=-1, keepdims=True)
            expo = jnp.exp(scores - top)
            p = expo / jnp.sum(expo, axis=-1, keepdims=True)
            p = p.astype(BF16)
            prob[i, h] = p
            acc[0, :, lo:hi] += mm(p, only(qkv[2, i, :, lo:hi], start, stop))
        att[i] = acc[0, :, :local].astype(BF16)
        far_att[i] = pltpu.roll(acc[0], far_att.shape[-1] - local, 1).astype(BF16)
        rs_give(ATT, i, 0, mm(att[i, half_of(there), :], wo_ref[...]))
        rs_give(ATT, i, 1, mm(att[i, half_of(here), :], wo_ref[...]))

    follow(ATT, att_rest)

    turn(ATT)
    give_factor(0, 3 + full)

    def att_end(i):
        y = xin[i].astype(F32) + rs_take(ATT, i)
        ag_done(ATT, i)
        rs_done(ATT, i)
        ymid[i] = y
        gath[MLP, i, own, :] = norm(y, 1, i)
        ag_start(MLP, i)

    def mlp_half(i, half, which):
        a = gath[MLP, i, half_of(half), :]
        v = mm(a, w1_ref[...])
        value, slope = gelu_parts(v)
        act[i, half_of(half), :] = value.astype(BF16)
        dgel[i, half_of(half), :] = slope.astype(BF16)
        rs_give(MLP, i, which, mm(act[i, half_of(half), :], w2_ref[...]))

    def mlp_end(i):
        y = (ymid[i] + rs_take(MLP, i)).astype(BF16)
        rs_done(MLP, i)

        @pl.when(s == 0)
        def _():
            mid[i] = y
            mid_copy(i).start()

        @pl.when(s == 1)
        def _():
            out_ref[i] = y
            out_copy(i).start()

    def take_grad(i):
        mid_copy(i).wait_send()
        grad_copy(i).wait_recv()
        gath[DMLP, i, own, :] = xin[i]
        ag_start(DMLP, i)

    def dmlp_half(i, half, which):
        @pl.when(s == 0)
        def _():
            dh[i, half_of(half), :] = mm(gath[DMLP, i, half_of(half), :], partial[1]).astype(BF16)

        dact = dh[i, half_of(half), :].astype(F32)
        dh[i, half_of(half), :] = (dact * dgel[i, half_of(half), :].astype(F32)).astype(BF16)
        rs_give(DMLP, i, which, mm(dh[i, half_of(half), :], partial[0]))

    def mlp_rest(i):
        ag_rest(MLP, i)
        mlp_half(i, there, 0)

        @pl.when(i < count - 1)
        def _():
            ag_pass(MLP, i + 1)

        @pl.when(s == 0)
        def _():
            rs_pass(MLP, i)

        @pl.when(s == 1)
        def _():
            dmlp_half(i, there, 0)
            dmlp_half(i, here, 1)
            rs_pass(DMLP, i)

    lead(MLP, att_end, lambda i: mlp_half(i, here, 1))
    each_image(mlp_rest)
    turn(MLP)
    line_start(0)

    def dmlp_rest(i):
        @pl.when(i == count - 1)
        def _():
            turn(DMLP)
            line_start(1)

        dmlp_half(i, there, 0)

    @pl.when(s == 0)
    def _():
        each_image(mlp_end)
        turn_weight(partial.at[0], w1_ref)
        turn_weight(partial.at[1], w2_ref)
        turn_weight(sums.at[0], wo_ref)
        for d in range(1, ring):
            line_pass(0, d)
        lead(DMLP, take_grad, lambda i: dmlp_half(i, here, 1))
        follow(DMLP, dmlp_rest)

    @pl.when(s == 1)
    def _():
        last_rows.start()
        last_rows.wait()

    def dmlp_end(i):
        grad = xin[i].astype(F32) + norm_back(rs_take(DMLP, i), 1, i)
        rs_done(DMLP, i)
        dy1[i] = grad
        gath[DATT % 3, i, own, :] = grad.astype(BF16)
        ag_start(DATT, i)

    def datt_part(i, half):
        att[i, half_of(half), :] = mm(
            gath[DATT % 3, i, half_of(half), :], sums[0, :, :local]
        ).astype(BF16)

    lead(DATT, dmlp_end, lambda i: datt_part(i, here))

    @pl.when(s == 0)
    def _():
        line_pass(1, 1)

    def datt_rest(i):
        datt_part(i, there)

        turn_image(DATT, i)

        @pl.when(i == t % 2)
        def _():
            give_factor(1)

        acc[...] = jnp.zeros_like(acc)
        for h, (lo, hi, start, stop) in enumerate(windows):
            q = only(qkv[0, i, :, lo:hi], start, stop)
            k = only(qkv[1, i, :, lo:hi], start, stop)
            d = only(att[i, :, lo:hi], start, stop)
            low = prob[i, h]
            p = low.astype(F32)
            dp = mm_nt(d, qkv[2, i, :, lo:hi])
            inner = jnp.sum(p * dp, axis=-1, keepdims=True)
            ds = (p * (dp - inner)).astype(BF16)

            @pl.when(i == 0)
            def _():
                bias[h] = ds.astype(F32)

            @pl.when(i > 0)
            def _():
                bias[h] += ds.astype(F32)

            acc[0, :, lo:hi] += mm(ds, k)
            acc[1, :, lo:hi] += mm_tn(ds, q)
            acc[2, :, lo:hi] += mm_tn(low, d)
        tiles = [None] * (lanes // 128)
        for c, by in enumerate((scale, scale, 1.0)):
            first = c * local // 128
            moved = acc[c] * by
            if c * local > first * 128:
                moved = pltpu.roll(moved, c * local - first * 128, 1)
            for n in range(moved.shape[1] // 128):
                tile = moved[:, n * 128 : (n + 1) * 128]
                tiles[first + n] = tile if tiles[first + n] is None else tiles[first + n] + tile
        per = wide // 128
        over_tokens = []
        for c in range(full + 1):
            part = jnp.concatenate(tiles[c * per : (c + 1) * per], axis=1).astype(BF16)
            if c < full:
                dqkv[c, i] = part
            else:
                dtail[i] = part
            over_tokens.append(jnp.sum(part.astype(F32), axis=0, keepdims=True))
        tok_ref[z, pl.ds(i, 1), :lanes] = jnp.concatenate(over_tokens, axis=1)
        last = 3 * local - full * wide
        for which, half in ((0, there), (1, here)):
            da = mm(dtail[i, half_of(half), :last], wq_ref[full * wide :, :])
            for c in range(full):
                da += mm(dqkv[c, i, half_of(half), :], wq_ref[c * wide : (c + 1) * wide, :])
            rs_give(DATT, i, which, da)

    follow(DATT, datt_rest)

    give_factor(2 + full, *range(2, 2 + full))

    @pl.when(s == 1)
    def _():
        line_pass(0, 1)

    def first_parts():
        mlp_own()
        mlp_of(1, True)
        share_factor(0)
        share_factor(1)
        give_rest(full)

    if chained:
        pl.when(s == 0)(first_parts)
    line_pass(1, 2)

    def datt_end(i):
        grad = dy1[i] + norm_back(rs_take(DATT, i), 0, i)
        ig_ref[i] = grad.astype(BF16)

        @pl.when(s == 1)
        def _():
            grad_copy(i).start()

    each_image(datt_end)

    @pl.when(s == 1)
    def _():
        each_image(lambda i: rs_pass(MLP, i))

    for j in range(3):
        small_copy(0, j).start()

    def fold(h, carry):
        total = jnp.zeros((grid, 2 * seq), F32)
        for r in range(grid):
            part = wider(bias[h, r * grid : (r + 1) * grid, :], 2 * seq)
            shift = grid * (grid - 1 - r)
            total += part if shift == 0 else pltpu.roll(part, shift, 1)
        after = total[:1, :]
        before = jnp.zeros((1, 2 * seq), F32)
        for c in range(1, grid):
            row = total[c : c + 1, :]
            late = lane % grid >= c
            after += pltpu.roll(jnp.where(late, row, 0.0), 2 * seq - c, 1)
            before += pltpu.roll(jnp.where(late, 0.0, row), grid - c, 1)
        tok_ref[z, pl.ds(count + h, 1), : 4 * seq] = jnp.concatenate([after, before], axis=1)
        return carry

    lax.fori_loop(0, heads, fold, 0)
    for j in range(3):
        small_copy(0, j).wait_recv()
    over_tensor = tiny_s[0] + small_r[0, 0] + small_r[0, 1] + small_r[0, 2]
    row = lax.broadcasted_iota(jnp.int32, over_tensor.shape, 0)
    tok_ref[z, count + heads : count + heads + 1, :] = jnp.sum(
        jnp.where(row == t, over_tensor, 0.0), axis=0, keepdims=True
    )
    over_ring(lambda j: tiny_copy(1, j).start())

    @pl.when(s == 1)
    def _():
        each_image(mlp_end)

    if chained:

        @pl.when(s == 1)
        def _():
            line_pass(0, 2)

            first_parts()

        give_rest(0)
        mlp_of(1, False)
        relay(full)
        for c in range(1, full):
            give_rest(c)
        relay(0)
        mlp_of(2, True)
        mlp_of(2, False)

        @pl.when(s == 1)
        def _():
            line_pass(0, 3)

        line_pass(1, 3)
        for c in range(1, full):
            relay(c)
        mlp_of(3, True)
        mlp_of(3, False)
    else:

        def whole(b, carry):
            at = block(b)
            parts_ref[0, b] = sum(mm(line[1, i, at, :], act[i]) for i in range(count)).astype(BF16)
            parts_ref[1, b] = sum(mm(line[0, i, at, :], dh[i]) for i in range(count)).astype(BF16)
            parts_ref[2, b] = jnp.concatenate(
                [rest_product(c, at, 0) for c in range(full + 1)], axis=1
            ).astype(BF16)
            return carry

        lax.fori_loop(0, blocks, whole, 0)
    stores = []

    def store(src, dst):
        copy = pltpu.make_async_copy(src, dst, store_s.at[len(stores)])
        copy.start()
        stores.append(copy)
        return copy

    mlp_stores = []
    if chained:
        mlp_stores = [store(mlp_ref.at[0], g2_hbm), store(mlp_ref.at[1], g1_hbm)]
    over_ring(lambda j: tiny_copy(1, j).wait_recv())

    def add_slot(j, total):
        return total + tok_ref[j]

    total = lax.fori_loop(0, ring, add_slot, jnp.zeros(tok_ref.shape[1:], F32))
    tiny_s[1] = total
    for j in range(3):
        small_copy(1, j).start()
    tab[...] = jnp.zeros_like(tab)
    tab[:heads, :] = tiny_s[1, count : count + heads, : 4 * seq]
    found = add_thirds(mm_nt(in_thirds(tab[...]), chosen[...]))
    gtab_ref[...] = found[:heads, : gtab_ref.shape[1]]
    store(gtab_ref, gtab_hbm)

    over_ring(lambda j: tiny_copy(0, j).wait_recv())
    mine = width // ring
    tall = gt_hbm.shape[1]
    rows_of_emb = emb_ref[...].reshape(ring * 8, width)
    rows_of_emb = pltpu.roll(rows_of_emb, (width - z * mine) % width, 1)[:, :mine].astype(BF16)
    right = in_thirds(tok_ref[...].reshape(ring * 8, width)[:, :lanes])
    over_images = mm_tn(jnp.concatenate([rows_of_emb] * 3, axis=0), right)
    for copy in mlp_stores:
        copy.wait()
    room = mlp_ref.at[0] if chained else stage
    time_stores = []
    for c in range(3):
        first = c * local // 128 * 128
        window = over_images[:, first : first + wide]
        if c * local > first:
            window = pltpu.roll(window, wide - (c * local - first), 1)
        room[:mine, c * wide : (c + 1) * wide] = window
        time_stores.append(store(room.at[pl.ds(0, tall), pl.ds(c * wide, wide)], gt_hbm.at[c]))
    if chained:
        for c in (full, *range(full)):
            settle(c)
        for c in range(3):
            first = c * local // 128 * 128
            window = tot_ref[:, first : first + wide].astype(F32)
            if c * local > first:
                window = pltpu.roll(window, wide - (c * local - first), 1)
            mlp_ref[1, :, c * wide : (c + 1) * wide] = window
            store(mlp_ref.at[1, :, pl.ds(c * wide, wide)], gq_hbm.at[c])
        window = tot_ref[:, width - wide :].astype(F32)
        window = pltpu.roll(window, wide - (3 * local - (width - wide)), 1)
        for copy in time_stores:
            copy.wait()
        mlp_ref[0, :, :wide] = wider(window.T[:local], wide)
        store(mlp_ref.at[0, :, pl.ds(0, wide)], go_hbm)
    for j in range(3):
        small_copy(1, j).wait_recv()
    last = count + heads
    small_ref[pl.ds(t, 1), :] = tiny_s[1, last : last + 1, :]
    for j, owner in enumerate((core, far, fcore)):
        small_ref[pl.ds(owner, 1), :] = small_r[1, j, last : last + 1, :]
    ggain_ref[...] = small_ref[:2, :]
    gshift_ref[...] = small_ref[2:, :]
    store(ggain_ref, ggain_hbm)
    store(gshift_ref, gshift_hbm)
    store(ig_ref, ig_hbm)

    def finish(i):
        for k in (MLP, DMLP, DATT):
            ag_done(k, i)
        rs_done(DATT, i)

        @pl.when(s == 0)
        def _():
            out_copy(i).wait_recv()

        @pl.when(s == 1)
        def _():
            out_copy(i).wait_send()
            grad_copy(i).wait_send()

    each_image(finish)
    store(out_ref, out_hbm)

    def tiny_left(j):
        tiny_copy(0, j).wait_send()
        tiny_copy(1, j).wait_send()

    over_ring(tiny_left)
    for j in range(3):
        small_copy(0, j).wait_send()
        small_copy(1, j).wait_send()
    if chained:
        weights_left()
    waited = mlp_stores + (time_stores if chained else [])
    for copy in stores:
        if all(copy is not done for done in waited):
            copy.wait()


def run_block(x, cot, wq, wt, wo, w1, w2, temb, gain, shift, rel, table, ring):
    count, rows, width = x.shape
    seq = rel.shape[0]
    heads = table.shape[0]
    local = wo.shape[0]
    hidden = w1.shape[1]
    chained = ring == 4 and count == 2 and width % (16 * ring) == 0
    blocks = 4
    pieces = 3 if width // 4 % 48 == 0 else 1
    cut = width // blocks
    padded = -(-local // 128) * 128
    lanes = -(-3 * local // 128) * 128
    dims = (count, rows, seq, heads, ring, chained)
    full = 3 * local // padded
    assert pieces == full + 1 and padded * pieces == width
    mine = width // ring
    small = (8, 128)
    out_shape = [
        jax.ShapeDtypeStruct((count, rows, width), BF16),
        jax.ShapeDtypeStruct((count, rows, width), BF16),
        jax.ShapeDtypeStruct((16, 128) if chained else (3, blocks, cut, width), BF16),
        jax.ShapeDtypeStruct((cut, width) if chained else small, F32),
        jax.ShapeDtypeStruct((cut, width) if chained else small, F32),
        jax.ShapeDtypeStruct((3, cut, padded) if chained else small, F32),
        jax.ShapeDtypeStruct((local, padded) if chained else small, F32),
        jax.ShapeDtypeStruct((3, -(-mine // 8) * 8, padded), F32),
        jax.ShapeDtypeStruct(table.shape, F32),
        jax.ShapeDtypeStruct((2, width), F32),
        jax.ShapeDtypeStruct((2, width), F32),
    ]
    vm = pltpu.VMEM
    dma = pltpu.SemaphoreType.DMA
    scratch = [
        vm(temb.shape, BF16),
        vm(gain.shape, F32),
        vm(shift.shape, F32),
        vm(rel.shape, jnp.int32),
        vm(table.shape, F32),
        vm((count, rows, width), BF16),
        vm((count, rows, width), BF16),
        vm((cut, width) if chained else (16, 128), BF16),
        vm((2, cut, width) if chained else (2, 8, 128), F32),
        vm(small if chained else (-(-mine // 8) * 8, 3 * padded), F32),
        vm((ring, 8, width), F32),
        vm((ring, 8, width), F32),
        vm(table.shape, F32),
        vm((4, width), F32),
        vm((2, width), F32),
        vm((2, width), F32),
        vm(wq.shape, BF16),
        vm(wo.shape, BF16),
        vm(w1.shape, BF16),
        vm(w2.shape, BF16),
        vm((3, 16, local), F32),
        vm((heads, int(round(seq**0.5)), 2 * seq), F32),
        vm((4 * seq, 4 * seq), BF16),
        vm((16, 4 * seq), F32),
        vm((2, width, width), BF16),
        vm((pieces, width, padded), BF16),
        vm((2, pieces, cut, padded) if chained else (16, 128), BF16),
        vm((2, 8, width), F32),
        vm((2, 3, 8, width), F32),
        vm((count, rows, width), BF16),
        vm((count, rows, width), BF16),
        vm((3, count, seq, width), BF16),
        vm((2, count, 2, rows, width), F32),
        vm((2, count, 2, rows, width), BF16),
        vm((2, count, rows, width), BF16),
        vm((2, count, 2, rows, width), BF16),
        vm((2, count, rows, width), BF16),
        vm((heads, seq, seq), F32),
        vm((count, heads, seq, seq), BF16),
        vm((3, count, seq, local), BF16),
        vm((count, seq, local), BF16),
        vm((count, seq, hidden), BF16),
        vm((count, seq, hidden), BF16),
        vm((2, count, rows, width), F32),
        vm((2, count, rows, 128), F32),
        vm((count, rows, width), F32),
        vm((count, rows, width), F32),
        vm((full, count, seq, padded), BF16),
        vm((count, seq, lanes - full * padded), BF16),
        vm((count, seq, hidden), BF16),
        vm((3, seq, padded), F32),
        vm((2, 2 * count if chained else count, width, seq), BF16),
        vm((2, ring * count if chained else count, width, seq), BF16),
        vm((count, seq, padded), BF16),
        vm((full, count, seq, padded) if chained else (16, 128), BF16),
        vm((count, seq, lanes - full * padded) if chained else (16, 128), BF16),
        vm((count, seq, padded) if chained else (16, 128), BF16),
        dma((12 + count,)),
        dma((20,)),
        dma((4, count, 3)),
        dma((4, count, 3)),
        dma((4, count, 3)),
        dma((4, count, 3)),
        dma((3, count)),
        dma((3, count)),
        dma((3, pieces)),
        dma((2, pieces)),
        dma((6 + full,)),
        dma((6 + full,)),
        dma((2, 3, ring)),
        dma((2, 3, ring)),
        dma((2, ring)),
        dma((2, ring)),
        dma((2, 3)),
        dma((2, 3)),
    ]
    whole = pl.BlockSpec(memory_space=pltpu.VMEM)
    lies = pl.BlockSpec(memory_space=pl.ANY)
    return pl.pallas_call(
        functools.partial(block_kernel, dims),
        out_shape=out_shape,
        in_specs=[lies] * 12,
        out_specs=[lies] * 2 + [lies if chained else whole] + [lies] * 8,
        scratch_shapes=scratch,
        compiler_params=pltpu.CompilerParams(
            collective_id=0, has_side_effects=True, vmem_limit_bytes=63 * 2**20
        ),
        name="blocks",
    )(x, cot, wq, wt, wo, w1, w2, temb, gain, shift, rel, table)


def per_device(
    images, timesteps, t_table, rel_index, w_qkv, w_time, w_out, w_fc1, w_fc2, rel_table,
    norm_gain, norm_shift, cotangent,
):
    ring = lax.axis_size("dp")
    count = images.shape[0]
    width = images.shape[-1]
    local = w_out.shape[1]
    cut = width // ring
    embedded = jnp.concatenate(
        [lax.dynamic_slice_in_dim(t_table, timesteps[i], 1, axis=0) for i in range(count)], axis=0
    )
    wq = jnp.transpose(w_qkv[0], (1, 2, 0)).reshape(3 * local, width)
    wt = jnp.transpose(w_time[0], (1, 2, 0)).reshape(3 * local, width)
    output, in_grad, parts, g_fc2, g_fc1, g_qkv, g_out, g_time, g_table, g_gain, g_shift = run_block(
        images, cotangent, wq, wt, w_out[0], w_fc1[0], w_fc2[0], embedded, norm_gain[0], norm_shift[0],
        rel_index, rel_table[0].T, ring,
    )
    if parts.ndim == 4:
        parts = lax.psum_scatter(
            parts.reshape(3, width, width), "dp", scatter_dimension=1, tiled=True
        ).astype(F32)
        g_fc2, g_fc1, rest = parts
        g_qkv = jnp.transpose(rest[:, : 3 * local].reshape(cut, 3, local), (1, 0, 2))
        g_out = rest[:, 3 * local :].T
    else:
        g_qkv, g_out = g_qkv[:, :, :local], g_out[:, :cut]
    g_time = g_time[:, : width // ring, :local]
    return (
        output, in_grad[None], jnp.transpose(g_qkv, (1, 0, 2))[None], jnp.transpose(g_time, (1, 0, 2))[None],
        g_out[None], g_fc1[None], g_fc2.T[None], g_table.T[None], g_gain[None], g_shift[None],
    )


def solution(mesh):
    in_specs = (
        P("dp", "tensor", None),
        P("dp"),
        P(),
        P(),
        P("section", None, None, "tensor"),
        P("section", None, None, "tensor"),
        P("section", "tensor", None),
        P("section", None, "tensor"),
        P("section", "tensor", None),
        P("section", None, "tensor"),
        P("section", None, None),
        P("section", None, None),
        P("dp", "tensor", None),
    )
    out_specs = (
        P("dp", "tensor", None),
        P("section", "dp", "tensor", None),
        P("section", "dp", None, "tensor"),
        P("section", "dp", None, "tensor"),
        P("section", "tensor", "dp"),
        P("section", "dp", "tensor"),
        P("section", "tensor", "dp"),
        P("section", None, "tensor"),
        P("section", None, None),
        P("section", None, None),
    )
    return jax.shard_map(
        per_device, mesh=mesh, in_specs=in_specs, out_specs=out_specs, check_vma=False
    )
```

```python
import functools

import jax
import jax.numpy as jnp
from jax import lax
from jax.experimental import pallas as pl
from jax.experimental.pallas import tpu as pltpu
from jax.sharding import PartitionSpec as P

MESH = pl.DeviceIdType.MESH
F32 = jnp.float32
BF16 = jnp.bfloat16
EPS = 1e-06
GELU_A = 0.7978845608028654
GELU_B = 0.044715
ATT, MLP, DMLP, DATT = range(4)
slot_of = (0, 1, 0, 0)


def mm(a, b):
    return lax.dot_general(a, b, (((1,), (0,)), ((), ())), preferred_element_type=F32)


def mm_nt(a, b):
    return lax.dot_general(a, b, (((1,), (1,)), ((), ())), preferred_element_type=F32)


def mm_tn(a, b):
    return lax.dot_general(a, b, (((0,), (0,)), ((), ())), preferred_element_type=F32)


def gelu_parts(v):
    square = v * v
    th = jnp.tanh(v * (GELU_A + (GELU_A * GELU_B) * square))
    up = 0.5 + 0.5 * th
    slope = up + v * (1.0 - th * th) * (0.5 * GELU_A + (1.5 * GELU_A * GELU_B) * square)
    return v * up, slope


def head_windows(heads, local):
    width = local // heads
    found = []
    for h in range(heads):
        lo = h * width // 128 * 128
        hi = min(-(-(h + 1) * width // 128) * 128, local)
        found.append((lo, hi, h * width - lo, (h + 1) * width - lo))
    return found


def only(x, start, stop):
    lane = lax.broadcasted_iota(jnp.int32, x.shape, 1)
    return jnp.where((lane >= start) & (lane < stop), x, jnp.zeros_like(x))


def in_thirds(x):
    high = x.astype(BF16)
    rest = x - high.astype(F32)
    middle = rest.astype(BF16)
    low = (rest - middle.astype(F32)).astype(BF16)
    return jnp.concatenate([high, middle, low], axis=0)


def add_thirds(x):
    rows = x.shape[0] // 3
    return x[:rows] + x[rows : 2 * rows] + x[2 * rows :]


def wider(x, lanes):
    return jnp.concatenate([x, jnp.zeros((x.shape[0], lanes - x.shape[1]), x.dtype)], axis=1)


def block_kernel(
    cfg,
    x_hbm, cot_hbm, wq_hbm, wt_hbm, wo_hbm, w1_hbm, w2_hbm, temb_hbm, gain_hbm, shift_hbm, rel_hbm, tab_hbm,
    out_hbm, ig_hbm, parts_ref, g2_hbm, g1_hbm, gq_hbm, go_hbm, gt_hbm, gtab_hbm, ggain_hbm, gshift_hbm,
    temb_ref, gain_ref, shift_ref, rel_ref, tab_ref, out_ref, ig_ref, tot_ref, mlp_ref, stage, tok_ref, emb_ref,
    gtab_ref, small_ref, ggain_ref, gshift_ref,
    wq_ref, wo_ref, w1_ref, w2_ref, tp_ref, tx_ref, chosen, tab, partial, sums, arrived,
    tiny_s, small_r,
    xin, mid, gath, keep, rcv_c, rcv_y, snd_c, snd_y, bias, prob, qkv, att, act, dgel,
    xhat, inv, ymid, dy1, dqkv, dtail, dh, acc, turned, line, far_att, dqkv2, dtail2, far_att2,
    load_s, store_s, ag_s, ag_r, rs_s, rs_r, sec_s, sec_r, ch_s, ch_r, fac_s, fac_r, li_s, li_r, ti_s, ti_r, sm_s, sm_r,
):
    count, rows, seq, heads, ring, chained = cfg
    half_rows = 2 * rows
    wide = -(-wo_ref.shape[0] // 128) * 128
    width = x_hbm.shape[-1]
    local = wo_ref.shape[0]
    grid = int(round(seq**0.5))
    windows = head_windows(heads, local)
    scale = (local // heads) ** (-0.5)
    blocks = 4
    cut = width // blocks
    pieces = sums.shape[0]
    slim = cut // pieces
    full = dqkv.shape[0]
    lanes = full * dqkv.shape[-1] + dtail.shape[-1]

    s = lax.axis_index("section")
    t = lax.axis_index("tensor")
    z = lax.axis_index("dp")
    core = t + 1 - 2 * (t % 2)
    far = (t + 2) % 4
    fcore = (core + 2) % 4
    here = t // 2
    there = 1 - here
    own = pl.ds(pl.multiple_of(t * rows, rows), rows)

    wt_ref = partial.at[0, : 3 * local, :]

    loads = [
        pltpu.make_async_copy(src, dst, load_s.at[n])
        for n, (src, dst) in enumerate(
            (
                (wt_hbm, wt_ref), (wq_hbm, wq_ref), (wo_hbm, wo_ref), (w1_hbm, w1_ref), (w2_hbm, w2_ref),
                (temb_hbm, temb_ref), (gain_hbm, gain_ref), (shift_hbm, shift_ref), (rel_hbm, rel_ref),
                (tab_hbm, tab_ref),
            )
        )
    ]
    first_rows = pltpu.make_async_copy(x_hbm, xin, load_s.at[10])
    last_rows = pltpu.make_async_copy(cot_hbm, xin, load_s.at[11])

    def cot_rows(i):
        return pltpu.make_async_copy(cot_hbm.at[i], gath.at[DMLP, i, own, :], load_s.at[12 + i])

    @pl.when(s == 0)
    def _():
        first_rows.start()

    @pl.when(s == 1)
    def _():
        for i in range(count):
            cot_rows(i).start()

    for load in loads[5:] + loads[:5]:
        load.start()

    barrier = pltpu.get_barrier_semaphore()
    for peer in ({"tensor": core}, {"tensor": far}, {"tensor": fcore}, {"section": 1 - s}):
        pl.semaphore_signal(barrier, inc=1, device_id=peer, device_id_type=MESH)

    def greet(j, carry):
        pl.semaphore_signal(barrier, inc=1, device_id={"dp": (z + j) % ring}, device_id_type=MESH)
        return carry

    lax.fori_loop(1, ring, greet, 0)

    def rows_of(owner):
        return pl.ds(pl.multiple_of(owner * rows, rows), rows)

    def half_of(half):
        return pl.ds(pl.multiple_of(half * half_rows, half_rows), half_rows)

    def ag_copy(k, i, which):
        owner, to = ((t, core), (t, far), (far, core))[which]
        ref = gath.at[k % 3, i, rows_of(owner), :]
        return pltpu.make_async_remote_copy(
            src_ref=ref, dst_ref=ref, send_sem=ag_s.at[k, i, which], recv_sem=ag_r.at[k, i, which],
            device_id={"tensor": to}, device_id_type=MESH,
        )

    def ag_start(k, i):
        ag_copy(k, i, 1).start()
        ag_copy(k, i, 0).start()

    def ag_near(k, i):
        ag_copy(k, i, 0).wait_recv()

    def ag_pass(k, i):
        ag_copy(k, i, 1).wait_recv()
        ag_copy(k, i, 2).start()

    def ag_rest(k, i):
        ag_copy(k, i, 2).wait_recv()

    def ag_done(k, i):
        for which in range(3):
            ag_copy(k, i, which).wait_send()

    def rs_copy(k, i, which):
        if which < 2:
            src, dst, to = snd_c.at[slot_of[k], i, which], rcv_c.at[slot_of[k], i, which], core
        else:
            src, dst, to = snd_y.at[slot_of[k], i], rcv_y.at[slot_of[k], i], far
        return pltpu.make_async_remote_copy(
            src_ref=src, dst_ref=dst, send_sem=rs_s.at[k, i, which], recv_sem=rs_r.at[k, i, which],
            device_id={"tensor": to}, device_id_type=MESH,
        )

    def rs_give(k, i, which, part):
        odd = t % 2 == 1
        low, high = part[:rows], part[rows:]
        snd_c[slot_of[k], i, which] = jnp.where(odd, low, high).astype(BF16)
        rs_copy(k, i, which).start()
        keep[slot_of[k], i, which] = jnp.where(odd, high, low)

    def rs_pass(k, i):
        rs_copy(k, i, 0).wait_recv()
        snd_y[slot_of[k], i] = (keep[slot_of[k], i, 0] + rcv_c[slot_of[k], i, 0].astype(F32)).astype(BF16)
        rs_copy(k, i, 2).start()

    def rs_take(k, i):
        rs_copy(k, i, 1).wait_recv()
        near = keep[slot_of[k], i, 1] + rcv_c[slot_of[k], i, 1].astype(F32)
        rs_copy(k, i, 2).wait_recv()
        return near + rcv_y[slot_of[k], i].astype(F32)

    def rs_done(k, i):
        for which in range(3):
            rs_copy(k, i, which).wait_send()

    def sec_copy(j, src, dst):
        return lambda i: pltpu.make_async_remote_copy(
            src_ref=src.at[i], dst_ref=dst.at[i], send_sem=sec_s.at[j, i], recv_sem=sec_r.at[j, i],
            device_id={"section": 1 - s}, device_id_type=MESH,
        )

    mid_copy = sec_copy(0, mid, xin)
    grad_copy = sec_copy(1, ig_ref, xin)
    out_copy = sec_copy(2, out_ref, out_ref)

    def tiny_copy(n, j):
        ref = (emb_ref, tok_ref)[n]
        return pltpu.make_async_remote_copy(
            src_ref=ref.at[z], dst_ref=ref.at[z], send_sem=ti_s.at[n, j], recv_sem=ti_r.at[n, j],
            device_id={"dp": (z + j) % ring}, device_id_type=MESH,
        )

    def over_ring(body):
        def run(j, carry):
            body(j)
            return carry

        lax.fori_loop(1, ring, run, 0)

    def small_copy(n, j):
        return pltpu.make_async_remote_copy(
            src_ref=tiny_s.at[n], dst_ref=small_r.at[n, j], send_sem=sm_s.at[n, j], recv_sem=sm_r.at[n, j],
            device_id={"tensor": (core, far, fcore)[j]}, device_id_type=MESH,
        )

    mate = z + 1 - 2 * (z % 2)
    across = 3 - z
    beyond = 3 * (2 - z)
    is_end = (z == 0) | (z == 3)
    is_mate = (z == 1) | (z == 2)
    base = z * count if chained else 0
    place = {ATT: (turned, 0), DATT: (turned, 1), MLP: (line, 0), DMLP: (line, 1)}

    def block(b):
        return pl.ds(pl.multiple_of(b * cut, cut), cut)

    def factor_copy(n):
        if n < 2:
            src, dst = turned.at[n, t % 2], turned.at[n, count + t % 2]
        else:
            pairs = [(dqkv.at[c], dqkv2.at[c]) for c in range(full)] + [(dtail, dtail2), (far_att, far_att2)]
            src, dst = pairs[n - 2]
        return pltpu.make_async_remote_copy(
            src_ref=src, dst_ref=dst, send_sem=fac_s.at[n], recv_sem=fac_r.at[n],
            device_id={"dp": mate}, device_id_type=MESH,
        )

    def share_copy(k):
        ref = turned.at[k, count + t % 2]
        return pltpu.make_async_remote_copy(
            src_ref=ref, dst_ref=ref, send_sem=fac_s.at[4 + full + k], recv_sem=fac_r.at[4 + full + k],
            device_id={"tensor": core}, device_id_type=MESH,
        )

    def give_factor(*which):
        if chained:

            @pl.when(is_end)
            def _():
                for n in which:
                    factor_copy(n).start()

    def share_factor(k):
        if chained:

            @pl.when(is_mate)
            def _():
                factor_copy(k).wait_recv()
                share_copy(k).start()

    def cross_copy(slot, c):
        return pltpu.make_async_remote_copy(
            src_ref=sums.at[c, block((beyond, across)[slot]), :], dst_ref=arrived.at[slot, c],
            send_sem=ch_s.at[slot, c], recv_sem=ch_r.at[slot, c],
            device_id={"dp": across}, device_id_type=MESH,
        )

    def home_copy(c):
        return pltpu.make_async_remote_copy(
            src_ref=sums.at[c, block(mate), :], dst_ref=arrived.at[0, c],
            send_sem=ch_s.at[2, c], recv_sem=ch_r.at[0, c],
            device_id={"dp": mate}, device_id_type=MESH,
        )

    def rest_product(c, at, side):
        def by(n, right):
            return sum(mm(turned[n, side * count + i, at, :], right[i]) for i in range(count))

        if c < full:
            return by(0, (dqkv, dqkv2)[side].at[c])
        return wider(by(0, (dtail, dtail2)[side]), wide) + by(1, (far_att, far_att2)[side])

    def own_rest():
        @pl.when(is_end)
        def _():
            for c in range(full + 1):
                sums[c, block(z), :] = rest_product(c, block(z), 0).astype(BF16)

        @pl.when(is_mate)
        def _():
            def half(h, carry):
                at = pl.ds(pl.multiple_of(h * 2 * cut, 2 * cut), 2 * cut)
                for c in range(full + 1):
                    sums[c, at, :] = rest_product(c, at, 0).astype(BF16)
                return carry

            lax.fori_loop(0, 2, half, 0)

    def give_rest(c):
        def add(b):
            both_sides = sums[c, block(b), :].astype(F32) + rest_product(c, block(b), 1)
            sums[c, block(b), :] = both_sides.astype(BF16)

        @pl.when(is_mate)
        def _():
            if c < full:
                factor_copy(2 + c).wait_recv()
            else:
                share_copy(0).wait_recv()
                share_copy(1).wait_recv()
                factor_copy(2 + full).wait_recv()
                factor_copy(3 + full).wait_recv()
            add(beyond)
            cross_copy(0, c).start()
            if c < full:
                cross_copy(1, full if c == 0 else c - 1).start()
            add(across)
            if c == full - 1:
                cross_copy(1, c).start()
            add(z)

    def relay(c):
        @pl.when(is_mate)
        def _():
            cross_copy(0, c).wait_recv()
            home = sums[c, block(mate), :].astype(F32) + arrived[0, c].astype(F32)
            sums[c, block(mate), :] = home.astype(BF16)
            home_copy(c).start()

    def settle(c):
        def finish(slot, copy):
            copy.wait_recv()
            whole = sums[c, block(z), :].astype(F32) + arrived[slot, c].astype(F32)
            tot_ref[:, c * wide : (c + 1) * wide] = whole.astype(BF16)

        @pl.when(is_mate)
        def _():
            finish(1, cross_copy(1, c))

        @pl.when(is_end)
        def _():
            finish(0, home_copy(c))

    def weights_left():
        @pl.when(is_end)
        def _():
            for n in range(4 + full):
                factor_copy(n).wait_send()

        @pl.when(is_mate)
        def _():
            for k in range(2):
                share_copy(k).wait_send()
            for c in range(pieces):
                cross_copy(0, c).wait_send()
                cross_copy(1, c).wait_send()
                home_copy(c).wait_send()

        for n in range(2):
            for right in (True, False):

                @pl.when(z < ring - 1 if right else z > 0)
                def _():
                    line_copy(n, z, right).wait_send()

                for d in range(1, ring):
                    zs, there_is = upstream(d, right)

                    @pl.when(there_is)
                    def _():
                        line_share(n, zs).wait_send()

                        @pl.when(z < ring - 1 if right else z > 0)
                        def _():
                            line_copy(n, zs, right).wait_send()

    def line_copy(n, zs, right):
        ref = line.at[n, zs * count + t % 2]
        way = 0 if right else 1
        return pltpu.make_async_remote_copy(
            src_ref=ref, dst_ref=ref, send_sem=li_s.at[n, way, zs], recv_sem=li_r.at[n, way, zs],
            device_id={"dp": (z + 1) % ring if right else (z + ring - 1) % ring}, device_id_type=MESH,
        )

    def line_share(n, zs):
        ref = line.at[n, zs * count + t % 2]
        return pltpu.make_async_remote_copy(
            src_ref=ref, dst_ref=ref, send_sem=li_s.at[n, 2, zs], recv_sem=li_r.at[n, 2, zs],
            device_id={"tensor": core}, device_id_type=MESH,
        )

    def upstream(d, right):
        return (z - d, z >= d) if right else (z + d, z + d < ring)

    def line_start(n):
        if chained:
            for right in (True, False):

                @pl.when(z < ring - 1 if right else z > 0)
                def _():
                    line_copy(n, z, right).start()

    def line_pass(n, d):
        for right in (True, False) if chained else ():
            zs, there_is = upstream(d, right)

            @pl.when(there_is)
            def _():
                line_copy(n, zs, right).wait_recv()

                @pl.when(z < ring - 1 if right else z > 0)
                def _():
                    line_copy(n, zs, right).start()

                line_share(n, zs).start()

    def mlp_own():
        at = pl.ds(pl.multiple_of(z * cut, cut), cut)
        for m, n, right in ((0, 1, act), (1, 0, dh)):
            mlp_ref[m] = sum(mm(line[n, base + i, at, :], right[i]) for i in range(count))

    def mlp_of(zs):
        at = pl.ds(pl.multiple_of(z * cut, cut), cut)
        for n in range(2):
            line_share(n, zs).wait_recv()

        def step(j, carry):
            slot = zs * count + j // pieces
            cols = pl.ds(pl.multiple_of(j % pieces * (width // pieces), 128), width // pieces)
            v = mm(partial[0, cols, :], line[0, slot])
            value, slope = gelu_parts(v)
            back = (mm(w2_ref[cols, :], line[1, slot]) * slope).astype(BF16)
            mlp_ref[0, :, cols] += mm_nt(line[1, slot, at, :], value.astype(BF16))
            mlp_ref[1, :, cols] += mm_nt(line[0, slot, at, :], back)
            return carry

        lax.fori_loop(0, count * pieces, step, 0)

    def turn_image(k, i):
        ref, n = place[k]
        ref[n, base + i if ref is line else i] = gath[k % 3, i].T

    def turn(k):
        for i in range(count):
            turn_image(k, i)

    def each_image(body):
        def run(i, carry):
            body(i)
            return carry

        lax.fori_loop(0, count, run, 0)

    def norm(x, which, i):
        mean = jnp.mean(x, axis=-1, keepdims=True)
        centre = x - mean
        root = lax.rsqrt(jnp.mean(centre * centre, axis=-1, keepdims=True) + EPS)
        hat = centre * root
        xhat[which, i] = hat
        inv[which, i] = jnp.broadcast_to(root, (rows, 128))
        return (hat * gain_ref[which : which + 1, :] + shift_ref[which : which + 1, :]).astype(BF16)

    def norm_back(da, which, i):
        hat = xhat[which, i]
        tiny_s[0, which : which + 1, :] += jnp.sum(da * hat, axis=0, keepdims=True)
        tiny_s[0, 2 + which : 3 + which, :] += jnp.sum(da, axis=0, keepdims=True)
        dhat = da * gain_ref[which : which + 1, :]
        m1 = jnp.mean(dhat, axis=-1, keepdims=True)
        m2 = jnp.mean(dhat * hat, axis=-1, keepdims=True)
        return inv[which, i][:, :1] * (dhat - m1 - hat * m2)

    def turn_qkv():
        loads[1].wait()
        for r in range(0, width, wide):
            for c in range(3):
                partial[1, r : r + wide, c * wide : c * wide + local] = wq_ref[
                    c * local : (c + 1) * local, r : r + wide
                ].T

    def turn_weight(to, ref):
        for r in range(0, width, wide):
            to[r : r + wide, : ref.shape[0]] = ref[:, r : r + wide].T

    def lead(k, end, near):
        def first(i):
            end(i)

            @pl.when(i == count - 1)
            def _():
                ag_pass(k, 0)

            ag_near(k, i)
            near(i)

        each_image(first)

    def follow(k, rest):
        def second(i):
            ag_rest(k, i)
            rest(i)

            @pl.when(i < count - 1)
            def _():
                ag_pass(k, i + 1)

            rs_pass(k, i)

        each_image(second)

    tiny_s[...] = jnp.zeros_like(tiny_s)
    tok_ref[z] = jnp.zeros_like(tok_ref[z])
    emb_ref[z] = jnp.zeros_like(emb_ref[z])
    for load in loads[5:]:
        load.wait()
    emb_ref[z, :count, :] = temb_ref[...].astype(F32)

    def norm_input(i):
        gath[ATT, i, own, :] = norm(xin[i].astype(F32), 0, i)

    @pl.when(s == 0)
    def _():
        first_rows.wait()
        each_image(norm_input)

    pl.semaphore_wait(barrier, 3 + ring)
    over_ring(lambda j: tiny_copy(0, j).start())

    @pl.when(s == 1)
    def _():
        def begin(i):
            cot_rows(i).wait()
            ag_start(DMLP, i)

        each_image(begin)

    def take_input(i):
        mid_copy(i).wait_recv()
        norm_input(i)
        ag_start(ATT, i)

    lane = lax.broadcasted_iota(jnp.int32, (1, 2 * seq), 1)

    def tables():
        valid = lane < (2 * grid - 1) * grid
        slab = pltpu.roll(wider(rel_ref[:grid, :], 2 * seq), grid * (grid - 1), 1)
        for k in range(grid - 1):
            r = grid - 1 - k
            block = only(rel_ref[r * grid : (r + 1) * grid, :128], 0, grid)
            slab += pltpu.roll(wider(block, 2 * seq), k * grid, 1)
        none = jnp.full((1, 2 * seq), -1, jnp.int32)
        before = none
        for c in range(1, grid):
            moved = pltpu.roll(slab[c : c + 1, :], grid - c, 1)
            before = jnp.where((lane % grid == grid - c) & valid, moved, before)
        order = jnp.concatenate([jnp.where(valid, slab[:1, :], none), before], axis=1)
        step = 128
        for r in range(0, chosen.shape[0], step):
            bucket = r + lax.broadcasted_iota(jnp.int32, (step, 4 * seq), 0)
            chosen[r : r + step, :] = jnp.where(bucket == order, 1.0, 0.0).astype(BF16)
        tab[...] = jnp.zeros_like(tab)
        tab[:heads, : tab_ref.shape[1]] = tab_ref[...]
        found = add_thirds(mm(in_thirds(tab[...]), chosen[...]))
        after, before = found[:, : 2 * seq], found[:, 2 * seq :]
        for c in range(grid):
            low = pltpu.roll(after, c, 1) if c else after
            high = pltpu.roll(before, 2 * seq - (grid - c), 1)
            row = jnp.where(lane % grid >= c, low, high)
            for h in range(heads):
                tx_ref[h, c : c + 1, :] = row[h : h + 1, :]

        def expand(h, carry):
            for r in range(grid):
                shift = (2 * seq - grid * (grid - 1 - r)) % (2 * seq)
                bias[h, r * grid : (r + 1) * grid, :] = pltpu.roll(tx_ref[h], shift, 1)[:, :seq]
            return carry

        lax.fori_loop(0, heads, expand, 0)
        loads[0].wait()
        tp_ref[...] = jnp.zeros_like(tp_ref)
        emb = jnp.concatenate([temb_ref[...], jnp.zeros((16 - count, width), BF16)], axis=0)
        for c in range(3):
            tp_ref[c] = mm_nt(emb, partial[0, c * local : (c + 1) * local, :])

    @pl.when(s == 1)
    def _():
        tables()

        def spread_cot(i):
            ag_pass(DMLP, i)
            ag_near(DMLP, i)
            ag_rest(DMLP, i)

        each_image(spread_cot)
        turn(DMLP)
        line_start(1)
        turn_qkv()
        loads[2].wait()
        turn_weight(sums.at[0], wo_ref)
        loads[3].wait()
        turn_weight(partial.at[0], w1_ref)
        loads[4].wait()

        def early(i):
            dh[i] = mm_nt(gath[DMLP, i], w2_ref[...]).astype(BF16)

        each_image(early)
        line_pass(1, 1)

    @pl.when(s == 0)
    def _():
        each_image(lambda i: ag_start(ATT, i))
        tables()
        turn_qkv()
        for n in (2, 3, 4):
            loads[n].wait()

    def project(i, half):
        a = gath[ATT, i, half_of(half), :]
        part = mm(a, partial[1, :, : 2 * wide + local])
        for c in range(3):
            qkv[c, i, half_of(half), :] = (
                part[:, c * wide : c * wide + local] + tp_ref[c, pl.ds(i, 1), :]
            ).astype(BF16)

    def att_first(i):
        @pl.when(s == 1)
        def _():
            take_input(i)

    lead(ATT, att_first, lambda i: project(i, here))

    def att_rest(i):
        project(i, there)
        acc[0] = jnp.zeros_like(acc[0])
        for h, (lo, hi, start, stop) in enumerate(windows):
            q = only(qkv[0, i, :, lo:hi], start, stop)
            scores = mm_nt(q, qkv[1, i, :, lo:hi]) * scale + bias[h]
            top = jnp.max(scores, axis=-1, keepdims=True)
            expo = jnp.exp(scores - top)
            p = expo * (1.0 / jnp.sum(expo, axis=-1, keepdims=True))
            p = p.astype(BF16)
            prob[i, h] = p
            acc[0, :, lo:hi] += mm(p, only(qkv[2, i, :, lo:hi], start, stop))
        att[i] = acc[0, :, :local].astype(BF16)
        far_att[i] = pltpu.roll(acc[0], far_att.shape[-1] - local, 1).astype(BF16)
        rs_give(ATT, i, 0, mm(att[i, half_of(there), :], wo_ref[...]))
        rs_give(ATT, i, 1, mm(att[i, half_of(here), :], wo_ref[...]))

    follow(ATT, att_rest)

    turn(ATT)
    give_factor(0, 3 + full)

    def att_end(i):
        y = xin[i].astype(F32) + rs_take(ATT, i)
        ag_done(ATT, i)
        rs_done(ATT, i)
        ymid[i] = y
        gath[MLP, i, own, :] = norm(y, 1, i)
        ag_start(MLP, i)

    def mlp_half(i, half, which):
        a = gath[MLP, i, half_of(half), :]
        v = mm(a, w1_ref[...])
        value, slope = gelu_parts(v)
        act[i, half_of(half), :] = value.astype(BF16)
        dgel[i, half_of(half), :] = slope.astype(BF16)
        rs_give(MLP, i, which, mm(act[i, half_of(half), :], w2_ref[...]))

    def mlp_end(i):
        y = (ymid[i] + rs_take(MLP, i)).astype(BF16)
        rs_done(MLP, i)

        @pl.when(s == 0)
        def _():
            mid[i] = y
            mid_copy(i).start()

        @pl.when(s == 1)
        def _():
            out_ref[i] = y
            out_copy(i).start()

    def take_grad(i):
        mid_copy(i).wait_send()
        grad_copy(i).wait_recv()
        gath[DMLP, i, own, :] = xin[i]
        ag_start(DMLP, i)

    def dmlp_half(i, half, which):
        @pl.when(s == 0)
        def _():
            dh[i, half_of(half), :] = mm(gath[DMLP, i, half_of(half), :], partial[1]).astype(BF16)

        dact = dh[i, half_of(half), :].astype(F32)
        dh[i, half_of(half), :] = (dact * dgel[i, half_of(half), :].astype(F32)).astype(BF16)
        rs_give(DMLP, i, which, mm(dh[i, half_of(half), :], partial[0]))

    def mlp_rest(i):
        ag_rest(MLP, i)
        mlp_half(i, there, 0)

        @pl.when(i < count - 1)
        def _():
            ag_pass(MLP, i + 1)

        @pl.when(s == 0)
        def _():
            rs_pass(MLP, i)

        @pl.when(s == 1)
        def _():
            dmlp_half(i, there, 0)
            dmlp_half(i, here, 1)
            rs_pass(DMLP, i)

    lead(MLP, att_end, lambda i: mlp_half(i, here, 1))
    each_image(mlp_rest)
    turn(MLP)
    line_start(0)

    def dmlp_rest(i):
        @pl.when(i == count - 1)
        def _():
            turn(DMLP)
            line_start(1)

        dmlp_half(i, there, 0)

    @pl.when(s == 0)
    def _():
        each_image(mlp_end)
        turn_weight(partial.at[0], w1_ref)
        turn_weight(partial.at[1], w2_ref)
        turn_weight(sums.at[0], wo_ref)
        for d in range(1, ring):
            line_pass(0, d)
        lead(DMLP, take_grad, lambda i: dmlp_half(i, here, 1))
        follow(DMLP, dmlp_rest)

    @pl.when(s == 1)
    def _():
        last_rows.start()
        last_rows.wait()

    def dmlp_end(i):
        grad = xin[i].astype(F32) + norm_back(rs_take(DMLP, i), 1, i)
        rs_done(DMLP, i)
        dy1[i] = grad
        gath[DATT % 3, i, own, :] = grad.astype(BF16)
        ag_start(DATT, i)

    def datt_part(i, half):
        att[i, half_of(half), :] = mm(
            gath[DATT % 3, i, half_of(half), :], sums[0, :, :local]
        ).astype(BF16)

    def turn_factor(i):
        turn_image(DATT, i)

        @pl.when(i == t % 2)
        def _():
            give_factor(1)

    lead(DATT, dmlp_end, lambda i: datt_part(i, here))

    @pl.when(s == 0)
    def _():
        line_pass(1, 1)

        def gathered(i):
            ag_rest(DATT, i)
            turn_factor(i)

            @pl.when(i < count - 1)
            def _():
                ag_pass(DATT, i + 1)

        each_image(gathered)

    def datt_rest(i):
        @pl.when(s == 1)
        def _():
            ag_rest(DATT, i)

        datt_part(i, there)

        @pl.when(s == 1)
        def _():
            turn_factor(i)

        acc[...] = jnp.zeros_like(acc)
        for h, (lo, hi, start, stop) in enumerate(windows):
            q = only(qkv[0, i, :, lo:hi], start, stop)
            k = only(qkv[1, i, :, lo:hi], start, stop)
            d = only(att[i, :, lo:hi], start, stop)
            low = prob[i, h]
            p = low.astype(F32)
            dp = mm_nt(d, qkv[2, i, :, lo:hi])
            inner = jnp.sum(p * dp, axis=-1, keepdims=True)
            ds = (p * (dp - inner)).astype(BF16)

            @pl.when(i == 0)
            def _():
                bias[h] = ds.astype(F32)

            @pl.when(i > 0)
            def _():
                bias[h] += ds.astype(F32)

            acc[0, :, lo:hi] += mm(ds, k)
            acc[1, :, lo:hi] += mm_tn(ds, q)
            acc[2, :, lo:hi] += mm_tn(low, d)
        tiles = [None] * (lanes // 128)
        for c, by in enumerate((scale, scale, 1.0)):
            first = c * local // 128
            moved = acc[c] * by
            if c * local > first * 128:
                moved = pltpu.roll(moved, c * local - first * 128, 1)
            for n in range(moved.shape[1] // 128):
                tile = moved[:, n * 128 : (n + 1) * 128]
                tiles[first + n] = tile if tiles[first + n] is None else tiles[first + n] + tile
        per = wide // 128
        over_tokens = []
        for c in range(full + 1):
            part = jnp.concatenate(tiles[c * per : (c + 1) * per], axis=1).astype(BF16)
            if c < full:
                dqkv[c, i] = part
            else:
                dtail[i] = part
            over_tokens.append(jnp.sum(part.astype(F32), axis=0, keepdims=True))
        tok_ref[z, pl.ds(i, 1), :lanes] = jnp.concatenate(over_tokens, axis=1)
        last = 3 * local - full * wide
        for which, half in ((0, there), (1, here)):
            da = mm(dtail[i, half_of(half), :last], wq_ref[full * wide :, :])
            for c in range(full):
                da += mm(dqkv[c, i, half_of(half), :], wq_ref[c * wide : (c + 1) * wide, :])
            rs_give(DATT, i, which, da)

        @pl.when((s == 1) & (i < count - 1))
        def _():
            ag_pass(DATT, i + 1)

        rs_pass(DATT, i)

    each_image(datt_rest)

    give_factor(2 + full, *range(2, 2 + full))

    @pl.when(s == 1)
    def _():
        line_pass(0, 1)

    def first_parts():
        own_rest()
        mlp_own()
        share_factor(0)
        share_factor(1)

    ig_store = pltpu.make_async_copy(ig_ref, ig_hbm, store_s.at[18])
    out_store = pltpu.make_async_copy(out_ref, out_hbm, store_s.at[19])

    def end_of_chain(r, carry):
        if chained:
            pl.when(r == s)(first_parts)

        @pl.when(r == 0)
        def _():
            line_pass(1, 2)

        @pl.when(r == 1)
        def _():
            line_pass(0, 2)

        if chained:

            @pl.when(r == s)
            def _():
                give_rest(full)

        @pl.when(r == 0)
        def _():

            def datt_end(i):
                grad = dy1[i] + norm_back(rs_take(DATT, i), 0, i)
                ig_ref[i] = grad.astype(BF16)

                @pl.when(s == 1)
                def _():
                    grad_copy(i).start()

            each_image(datt_end)

            ig_store.start()

            @pl.when(s == 0)
            def _():
                each_image(lambda i: out_copy(i).wait_recv())
                out_store.start()

            @pl.when(s == 1)
            def _():
                each_image(lambda i: rs_pass(MLP, i))

            for j in range(3):
                small_copy(0, j).start()

            def fold(h, carry):
                total = jnp.zeros((grid, 2 * seq), F32)
                for r in range(grid):
                    part = wider(bias[h, r * grid : (r + 1) * grid, :], 2 * seq)
                    shift = grid * (grid - 1 - r)
                    total += part if shift == 0 else pltpu.roll(part, shift, 1)
                after = total[:1, :]
                before = jnp.zeros((1, 2 * seq), F32)
                for c in range(1, grid):
                    row = total[c : c + 1, :]
                    late = lane % grid >= c
                    after += pltpu.roll(jnp.where(late, row, 0.0), 2 * seq - c, 1)
                    before += pltpu.roll(jnp.where(late, 0.0, row), grid - c, 1)
                tok_ref[z, pl.ds(count + h, 1), : 4 * seq] = jnp.concatenate([after, before], axis=1)
                return carry

            lax.fori_loop(0, heads, fold, 0)
            for j in range(3):
                small_copy(0, j).wait_recv()
            over_tensor = tiny_s[0] + small_r[0, 0] + small_r[0, 1] + small_r[0, 2]
            row = lax.broadcasted_iota(jnp.int32, over_tensor.shape, 0)
            tok_ref[z, count + heads : count + heads + 1, :] = jnp.sum(
                jnp.where(row == t, over_tensor, 0.0), axis=0, keepdims=True
            )
            over_ring(lambda j: tiny_copy(1, j).start())

            @pl.when(s == 1)
            def _():
                each_image(mlp_end)
                out_store.start()

        return carry

    lax.fori_loop(0, 1 + s, end_of_chain, 0)

    if chained:
        give_rest(0)

        def others(j, carry):
            d = 1 + j // 2
            zs = z - d + 2 * d * (j % 2)

            @pl.when((zs >= 0) & (zs < ring))
            def _():
                mlp_of(zs)

            @pl.when(j == 0)
            def _():
                for c in range(1, full):
                    give_rest(c)
                relay(full)
                relay(0)

            @pl.when(j == 1)
            def _():
                for c in range(1, full):
                    relay(c)

            @pl.when((j == 3) & (s == 1))
            def _():
                line_pass(0, 3)

            @pl.when(j == 3)
            def _():
                line_pass(1, 3)

            return carry

        lax.fori_loop(0, 2 * (ring - 1), others, 0)
    else:

        def whole(b, carry):
            at = block(b)
            parts_ref[0, b] = sum(mm(line[1, i, at, :], act[i]) for i in range(count)).astype(BF16)
            parts_ref[1, b] = sum(mm(line[0, i, at, :], dh[i]) for i in range(count)).astype(BF16)
            parts_ref[2, b] = jnp.concatenate(
                [rest_product(c, at, 0) for c in range(full + 1)], axis=1
            ).astype(BF16)
            return carry

        lax.fori_loop(0, blocks, whole, 0)
    stores = []

    def store(src, dst):
        copy = pltpu.make_async_copy(src, dst, store_s.at[len(stores)])
        copy.start()
        stores.append(copy)
        return copy

    mlp_stores = []
    if chained:
        mlp_stores = [store(mlp_ref.at[0], g2_hbm), store(mlp_ref.at[1], g1_hbm)]
    over_ring(lambda j: tiny_copy(1, j).wait_recv())

    def add_slot(j, total):
        return total + tok_ref[j]

    total = lax.fori_loop(0, ring, add_slot, jnp.zeros(tok_ref.shape[1:], F32))
    tiny_s[1] = total
    for j in range(3):
        small_copy(1, j).start()
    tab[...] = jnp.zeros_like(tab)
    tab[:heads, :] = tiny_s[1, count : count + heads, : 4 * seq]
    found = add_thirds(mm_nt(in_thirds(tab[...]), chosen[...]))
    gtab_ref[...] = found[:heads, : gtab_ref.shape[1]]
    store(gtab_ref, gtab_hbm)

    over_ring(lambda j: tiny_copy(0, j).wait_recv())
    mine = width // ring
    tall = gt_hbm.shape[1]
    rows_of_emb = emb_ref[...].reshape(ring * 8, width)
    rows_of_emb = pltpu.roll(rows_of_emb, (width - z * mine) % width, 1)[:, :mine].astype(BF16)
    right = in_thirds(tok_ref[...].reshape(ring * 8, width)[:, :lanes])
    over_images = mm_tn(jnp.concatenate([rows_of_emb] * 3, axis=0), right)
    for copy in mlp_stores:
        copy.wait()
    room = mlp_ref.at[0] if chained else stage
    time_stores = []
    for c in range(3):
        first = c * local // 128 * 128
        window = over_images[:, first : first + wide]
        if c * local > first:
            window = pltpu.roll(window, wide - (c * local - first), 1)
        room[:mine, c * wide : (c + 1) * wide] = window
        time_stores.append(store(room.at[pl.ds(0, tall), pl.ds(c * wide, wide)], gt_hbm.at[c]))
    if chained:
        for c in (full, *range(full)):
            settle(c)
        for c in range(3):
            first = c * local // 128 * 128
            window = tot_ref[:, first : first + wide].astype(F32)
            if c * local > first:
                window = pltpu.roll(window, wide - (c * local - first), 1)
            mlp_ref[1, :, c * wide : (c + 1) * wide] = window
            store(mlp_ref.at[1, :, pl.ds(c * wide, wide)], gq_hbm.at[c])
        window = tot_ref[:, width - wide :].astype(F32)
        window = pltpu.roll(window, wide - (3 * local - (width - wide)), 1)
        for copy in time_stores:
            copy.wait()
        mlp_ref[0, :, :wide] = wider(window.T[:local], wide)
        store(mlp_ref.at[0, :, pl.ds(0, wide)], go_hbm)
    for j in range(3):
        small_copy(1, j).wait_recv()
    last = count + heads
    small_ref[pl.ds(t, 1), :] = tiny_s[1, last : last + 1, :]
    for j, owner in enumerate((core, far, fcore)):
        small_ref[pl.ds(owner, 1), :] = small_r[1, j, last : last + 1, :]
    ggain_ref[...] = small_ref[:2, :]
    gshift_ref[...] = small_ref[2:, :]
    store(ggain_ref, ggain_hbm)
    store(gshift_ref, gshift_hbm)

    def finish(i):
        for k in (MLP, DMLP, DATT):
            ag_done(k, i)
        rs_done(DATT, i)

        @pl.when(s == 1)
        def _():
            out_copy(i).wait_send()
            grad_copy(i).wait_send()

    each_image(finish)
    ig_store.wait()
    out_store.wait()

    def tiny_left(j):
        tiny_copy(0, j).wait_send()
        tiny_copy(1, j).wait_send()

    over_ring(tiny_left)
    for j in range(3):
        small_copy(0, j).wait_send()
        small_copy(1, j).wait_send()
    if chained:
        weights_left()
    waited = mlp_stores + (time_stores if chained else [])
    for copy in stores:
        if all(copy is not done for done in waited):
            copy.wait()


def run_block(x, cot, wq, wt, wo, w1, w2, temb, gain, shift, rel, table, ring):
    count, rows, width = x.shape
    seq = rel.shape[0]
    heads = table.shape[0]
    local = wo.shape[0]
    hidden = w1.shape[1]
    chained = ring == 4 and count == 2 and width % (16 * ring) == 0
    blocks = 4
    pieces = 3 if width // 4 % 48 == 0 else 1
    cut = width // blocks
    padded = -(-local // 128) * 128
    lanes = -(-3 * local // 128) * 128
    dims = (count, rows, seq, heads, ring, chained)
    full = 3 * local // padded
    assert pieces == full + 1 and padded * pieces == width
    mine = width // ring
    small = (8, 128)
    out_shape = [
        jax.ShapeDtypeStruct((count, rows, width), BF16),
        jax.ShapeDtypeStruct((count, rows, width), BF16),
        jax.ShapeDtypeStruct((16, 128) if chained else (3, blocks, cut, width), BF16),
        jax.ShapeDtypeStruct((cut, width) if chained else small, F32),
        jax.ShapeDtypeStruct((cut, width) if chained else small, F32),
        jax.ShapeDtypeStruct((3, cut, padded) if chained else small, F32),
        jax.ShapeDtypeStruct((local, padded) if chained else small, F32),
        jax.ShapeDtypeStruct((3, -(-mine // 8) * 8, padded), F32),
        jax.ShapeDtypeStruct(table.shape, F32),
        jax.ShapeDtypeStruct((2, width), F32),
        jax.ShapeDtypeStruct((2, width), F32),
    ]
    vm = pltpu.VMEM
    dma = pltpu.SemaphoreType.DMA
    scratch = [
        vm(temb.shape, BF16),
        vm(gain.shape, F32),
        vm(shift.shape, F32),
        vm(rel.shape, jnp.int32),
        vm(table.shape, F32),
        vm((count, rows, width), BF16),
        vm((count, rows, width), BF16),
        vm((cut, width) if chained else (16, 128), BF16),
        vm((2, cut, width) if chained else (2, 8, 128), F32),
        vm(small if chained else (-(-mine // 8) * 8, 3 * padded), F32),
        vm((ring, 8, width), F32),
        vm((ring, 8, width), F32),
        vm(table.shape, F32),
        vm((4, width), F32),
        vm((2, width), F32),
        vm((2, width), F32),
        vm(wq.shape, BF16),
        vm(wo.shape, BF16),
        vm(w1.shape, BF16),
        vm(w2.shape, BF16),
        vm((3, 16, local), F32),
        vm((heads, int(round(seq**0.5)), 2 * seq), F32),
        vm((4 * seq, 4 * seq), BF16),
        vm((16, 4 * seq), F32),
        vm((2, width, width), BF16),
        vm((pieces, width, padded), BF16),
        vm((2, pieces, cut, padded) if chained else (16, 128), BF16),
        vm((2, 8, width), F32),
        vm((2, 3, 8, width), F32),
        vm((count, rows, width), BF16),
        vm((count, rows, width), BF16),
        vm((3, count, seq, width), BF16),
        vm((2, count, 2, rows, width), F32),
        vm((2, count, 2, rows, width), BF16),
        vm((2, count, rows, width), BF16),
        vm((2, count, 2, rows, width), BF16),
        vm((2, count, rows, width), BF16),
        vm((heads, seq, seq), F32),
        vm((count, heads, seq, seq), BF16),
        vm((3, count, seq, local), BF16),
        vm((count, seq, local), BF16),
        vm((count, seq, hidden), BF16),
        vm((count, seq, hidden), BF16),
        vm((2, count, rows, width), F32),
        vm((2, count, rows, 128), F32),
        vm((count, rows, width), F32),
        vm((count, rows, width), F32),
        vm((full, count, seq, padded), BF16),
        vm((count, seq, lanes - full * padded), BF16),
        vm((count, seq, hidden), BF16),
        vm((3, seq, padded), F32),
        vm((2, 2 * count if chained else count, width, seq), BF16),
        vm((2, ring * count if chained else count, width, seq), BF16),
        vm((count, seq, padded), BF16),
        vm((full, count, seq, padded) if chained else (16, 128), BF16),
        vm((count, seq, lanes - full * padded) if chained else (16, 128), BF16),
        vm((count, seq, padded) if chained else (16, 128), BF16),
        dma((12 + count,)),
        dma((20,)),
        dma((4, count, 3)),
        dma((4, count, 3)),
        dma((4, count, 3)),
        dma((4, count, 3)),
        dma((3, count)),
        dma((3, count)),
        dma((3, pieces)),
        dma((2, pieces)),
        dma((6 + full,)),
        dma((6 + full,)),
        dma((2, 3, ring)),
        dma((2, 3, ring)),
        dma((2, ring)),
        dma((2, ring)),
        dma((2, 3)),
        dma((2, 3)),
    ]
    whole = pl.BlockSpec(memory_space=pltpu.VMEM)
    lies = pl.BlockSpec(memory_space=pl.ANY)
    return pl.pallas_call(
        functools.partial(block_kernel, dims),
        out_shape=out_shape,
        in_specs=[lies] * 12,
        out_specs=[lies] * 2 + [lies if chained else whole] + [lies] * 8,
        scratch_shapes=scratch,
        compiler_params=pltpu.CompilerParams(
            collective_id=0, has_side_effects=True, vmem_limit_bytes=63 * 2**20
        ),
        name="blocks",
    )(x, cot, wq, wt, wo, w1, w2, temb, gain, shift, rel, table)


def per_device(
    images, timesteps, t_table, rel_index, w_qkv, w_time, w_out, w_fc1, w_fc2, rel_table,
    norm_gain, norm_shift, cotangent,
):
    ring = lax.axis_size("dp")
    count = images.shape[0]
    width = images.shape[-1]
    local = w_out.shape[1]
    cut = width // ring
    embedded = jnp.concatenate(
        [lax.dynamic_slice_in_dim(t_table, timesteps[i], 1, axis=0) for i in range(count)], axis=0
    )
    wq = jnp.transpose(w_qkv[0], (1, 2, 0)).reshape(3 * local, width)
    wt = jnp.transpose(w_time[0], (1, 2, 0)).reshape(3 * local, width)
    output, in_grad, parts, g_fc2, g_fc1, g_qkv, g_out, g_time, g_table, g_gain, g_shift = run_block(
        images, cotangent, wq, wt, w_out[0], w_fc1[0], w_fc2[0], embedded, norm_gain[0], norm_shift[0],
        rel_index, rel_table[0].T, ring,
    )
    if parts.ndim == 4:
        parts = lax.psum_scatter(
            parts.reshape(3, width, width), "dp", scatter_dimension=1, tiled=True
        ).astype(F32)
        g_fc2, g_fc1, rest = parts
        g_qkv = jnp.transpose(rest[:, : 3 * local].reshape(cut, 3, local), (1, 0, 2))
        g_out = rest[:, 3 * local :].T
    else:
        g_qkv, g_out = g_qkv[:, :, :local], g_out[:, :cut]
    g_time = g_time[:, : width // ring, :local]
    return (
        output, in_grad[None], jnp.transpose(g_qkv, (1, 0, 2))[None], jnp.transpose(g_time, (1, 0, 2))[None],
        g_out[None], g_fc1[None], g_fc2.T[None], g_table.T[None], g_gain[None], g_shift[None],
    )


def solution(mesh):
    in_specs = (
        P("dp", "tensor", None),
        P("dp"),
        P(),
        P(),
        P("section", None, None, "tensor"),
        P("section", None, None, "tensor"),
        P("section", "tensor", None),
        P("section", None, "tensor"),
        P("section", "tensor", None),
        P("section", None, "tensor"),
        P("section", None, None),
        P("section", None, None),
        P("dp", "tensor", None),
    )
    out_specs = (
        P("dp", "tensor", None),
        P("section", "dp", "tensor", None),
        P("section", "dp", None, "tensor"),
        P("section", "dp", None, "tensor"),
        P("section", "tensor", "dp"),
        P("section", "dp", "tensor"),
        P("section", "tensor", "dp"),
        P("section", None, "tensor"),
        P("section", None, None),
        P("section", None, None),
    )
    return jax.shard_map(
        per_device, mesh=mesh, in_specs=in_specs, out_specs=out_specs, check_vma=False
    )
```

```python
import functools

import jax
import jax.numpy as jnp
from jax import lax
from jax.experimental import pallas as pl
from jax.experimental.pallas import tpu as pltpu
from jax.sharding import PartitionSpec as P

MESH = pl.DeviceIdType.MESH
F32 = jnp.float32
BF16 = jnp.bfloat16
EPS = 1e-06
GELU_A = 0.7978845608028654
GELU_B = 0.044715
ATT, MLP, DMLP, DATT = range(4)
slot_of = (0, 1, 0, 0)


def mm(a, b):
    return lax.dot_general(a, b, (((1,), (0,)), ((), ())), preferred_element_type=F32)


def mm_nt(a, b):
    return lax.dot_general(a, b, (((1,), (1,)), ((), ())), preferred_element_type=F32)


def mm_tn(a, b):
    return lax.dot_general(a, b, (((0,), (0,)), ((), ())), preferred_element_type=F32)


def gelu_parts(v):
    square = v * v
    th = jnp.tanh(v * (GELU_A + (GELU_A * GELU_B) * square))
    up = 0.5 + 0.5 * th
    slope = up + v * (1.0 - th * th) * (0.5 * GELU_A + (1.5 * GELU_A * GELU_B) * square)
    return v * up, slope


def head_windows(heads, local):
    width = local // heads
    found = []
    for h in range(heads):
        lo = h * width // 128 * 128
        hi = min(-(-(h + 1) * width // 128) * 128, local)
        found.append((lo, hi, h * width - lo, (h + 1) * width - lo))
    return found


def only(x, start, stop):
    lane = lax.broadcasted_iota(jnp.int32, x.shape, 1)
    return jnp.where((lane >= start) & (lane < stop), x, jnp.zeros_like(x))


def in_thirds(x):
    high = x.astype(BF16)
    rest = x - high.astype(F32)
    middle = rest.astype(BF16)
    low = (rest - middle.astype(F32)).astype(BF16)
    return jnp.concatenate([high, middle, low], axis=0)


def add_thirds(x):
    rows = x.shape[0] // 3
    return x[:rows] + x[rows : 2 * rows] + x[2 * rows :]


def wider(x, lanes):
    return jnp.concatenate([x, jnp.zeros((x.shape[0], lanes - x.shape[1]), x.dtype)], axis=1)


def block_kernel(
    cfg,
    x_hbm, cot_hbm, wq_hbm, wt_hbm, wo_hbm, w1_hbm, w2_hbm, temb_hbm, gain_hbm, shift_hbm, rel_hbm, tab_hbm,
    out_hbm, ig_hbm, parts_ref, mlp_hbm, gq_hbm, go_hbm, gt_hbm, gtab_hbm, ggain_hbm, gshift_hbm,
    temb_ref, gain_ref, shift_ref, rel_ref, tab_ref, out_ref, ig_ref, mlp_ref, exact, tok_ref, emb_ref,
    gtab_ref, small_ref, ggain_ref, gshift_ref,
    wq_ref, wo_ref, w1_ref, w2_ref, tp_ref, tx_ref, order_ref, tab, partial, sums, arrived,
    tiny_s, small_r,
    xin, gath, keep, rcv_c, rcv_y, snd_c, snd_y, bias, prob, qkv, att, act, dgel,
    xhat, inv, ymid, dy1, dqkv, dtail, dh, acc, turned, line, far_att, dqkv2, dtail2, far_att2,
    load_s, store_s, ag_s, ag_r, rs_s, rs_r, sec_s, sec_r, ch_s, ch_r, fac_s, fac_r, li_s, li_r, ti_s, ti_r, sm_s, sm_r,
):
    count, rows, seq, heads, ring, chained = cfg
    half_rows = 2 * rows
    wide = -(-wo_ref.shape[0] // 128) * 128
    width = x_hbm.shape[-1]
    local = wo_ref.shape[0]
    grid = int(round(seq**0.5))
    windows = head_windows(heads, local)
    scale = (local // heads) ** (-0.5)
    blocks = 4
    cut = width // blocks
    pieces = sums.shape[0]
    slim = cut // pieces
    full = dqkv.shape[0]
    lanes = full * dqkv.shape[-1] + dtail.shape[-1]

    s = lax.axis_index("section")
    t = lax.axis_index("tensor")
    z = lax.axis_index("dp")
    core = t + 1 - 2 * (t % 2)
    far = (t + 2) % 4
    fcore = (core + 2) % 4
    here = t // 2
    there = 1 - here
    own = pl.ds(pl.multiple_of(t * rows, rows), rows)

    wt_ref = partial.at[0, : 3 * local, :]

    loads = [
        pltpu.make_async_copy(src, dst, load_s.at[n])
        for n, (src, dst) in enumerate(
            (
                (wt_hbm, wt_ref), (wq_hbm, wq_ref), (wo_hbm, wo_ref), (w1_hbm, w1_ref), (w2_hbm, w2_ref),
                (temb_hbm, temb_ref), (gain_hbm, gain_ref), (shift_hbm, shift_ref), (rel_hbm, rel_ref),
                (tab_hbm, tab_ref),
            )
        )
    ]
    first_rows = pltpu.make_async_copy(x_hbm, xin, load_s.at[10])
    last_rows = pltpu.make_async_copy(cot_hbm, xin, load_s.at[11])

    def cot_rows(i):
        return pltpu.make_async_copy(cot_hbm.at[i], gath.at[DMLP, i, own, :], load_s.at[12 + i])

    @pl.when(s == 0)
    def _():
        first_rows.start()

    @pl.when(s == 1)
    def _():
        for i in range(count):
            cot_rows(i).start()

    for load in loads[5:] + loads[:5]:
        load.start()

    barrier = pltpu.get_barrier_semaphore()
    for peer in ({"tensor": core}, {"tensor": far}, {"tensor": fcore}, {"section": 1 - s}):
        pl.semaphore_signal(barrier, inc=1, device_id=peer, device_id_type=MESH)

    def greet(j, carry):
        pl.semaphore_signal(barrier, inc=1, device_id={"dp": (z + j) % ring}, device_id_type=MESH)
        return carry

    lax.fori_loop(1, ring, greet, 0)

    def rows_of(owner):
        return pl.ds(pl.multiple_of(owner * rows, rows), rows)

    def half_of(half):
        return pl.ds(pl.multiple_of(half * half_rows, half_rows), half_rows)

    def ag_copy(k, i, which):
        owner, to = ((t, core), (t, far), (far, core))[which]
        ref = gath.at[k % 3, i, rows_of(owner), :]
        return pltpu.make_async_remote_copy(
            src_ref=ref, dst_ref=ref, send_sem=ag_s.at[k, i, which], recv_sem=ag_r.at[k, i, which],
            device_id={"tensor": to}, device_id_type=MESH,
        )

    def ag_start(k, i):
        ag_copy(k, i, 1).start()
        ag_copy(k, i, 0).start()

    def ag_near(k, i):
        ag_copy(k, i, 0).wait_recv()

    def ag_pass(k, i):
        ag_copy(k, i, 1).wait_recv()
        ag_copy(k, i, 2).start()

    def ag_rest(k, i):
        ag_copy(k, i, 2).wait_recv()

    def ag_done(k, i):
        for which in range(3):
            ag_copy(k, i, which).wait_send()

    def rs_copy(k, i, which):
        if which < 2:
            src, dst, to = snd_c.at[slot_of[k], i, which], rcv_c.at[slot_of[k], i, which], core
        else:
            src, dst, to = snd_y.at[slot_of[k], i], rcv_y.at[slot_of[k], i], far
        return pltpu.make_async_remote_copy(
            src_ref=src, dst_ref=dst, send_sem=rs_s.at[k, i, which], recv_sem=rs_r.at[k, i, which],
            device_id={"tensor": to}, device_id_type=MESH,
        )

    def rs_give(k, i, which, part):
        odd = t % 2 == 1
        low, high = part[:rows], part[rows:]
        snd_c[slot_of[k], i, which] = jnp.where(odd, low, high).astype(BF16)
        rs_copy(k, i, which).start()
        keep[slot_of[k], i, which] = jnp.where(odd, high, low)

    def rs_pass(k, i):
        rs_copy(k, i, 0).wait_recv()
        snd_y[slot_of[k], i] = (keep[slot_of[k], i, 0] + rcv_c[slot_of[k], i, 0].astype(F32)).astype(BF16)
        rs_copy(k, i, 2).start()

    def rs_take(k, i):
        rs_copy(k, i, 1).wait_recv()
        near = keep[slot_of[k], i, 1] + rcv_c[slot_of[k], i, 1].astype(F32)
        rs_copy(k, i, 2).wait_recv()
        return near + rcv_y[slot_of[k], i].astype(F32)

    def rs_done(k, i):
        for which in range(3):
            rs_copy(k, i, which).wait_send()

    def sec_copy(j, src, dst):
        return lambda i: pltpu.make_async_remote_copy(
            src_ref=src.at[i], dst_ref=dst.at[i], send_sem=sec_s.at[j, i], recv_sem=sec_r.at[j, i],
            device_id={"section": 1 - s}, device_id_type=MESH,
        )

    mid_copy = sec_copy(0, ig_ref, xin)
    grad_copy = sec_copy(1, ig_ref, xin)
    out_copy = sec_copy(2, out_ref, out_ref)

    def tiny_copy(n, j):
        ref = (emb_ref, tok_ref)[n]
        return pltpu.make_async_remote_copy(
            src_ref=ref.at[z], dst_ref=ref.at[z], send_sem=ti_s.at[n, j], recv_sem=ti_r.at[n, j],
            device_id={"dp": (z + j) % ring}, device_id_type=MESH,
        )

    def over_ring(body):
        def run(j, carry):
            body(j)
            return carry

        lax.fori_loop(1, ring, run, 0)

    def small_copy(n, j):
        return pltpu.make_async_remote_copy(
            src_ref=tiny_s.at[n], dst_ref=small_r.at[n, j], send_sem=sm_s.at[n, j], recv_sem=sm_r.at[n, j],
            device_id={"tensor": (core, far, fcore)[j]}, device_id_type=MESH,
        )

    mate = z + 1 - 2 * (z % 2)
    across = 3 - z
    beyond = 3 * (2 - z)
    is_end = (z == 0) | (z == 3)
    is_mate = (z == 1) | (z == 2)
    base = z * count if chained else 0
    place = {ATT: (turned, 0), DATT: (turned, 1), MLP: (line, 0), DMLP: (line, 1)}

    def block(b):
        return pl.ds(pl.multiple_of(b * cut, cut), cut)

    def factor_copy(n):
        if n < 2:
            src, dst = turned.at[n, t % 2], turned.at[n, count + t % 2]
        else:
            pairs = [(dqkv.at[c], dqkv2.at[c]) for c in range(full)] + [(dtail, dtail2), (far_att, far_att2)]
            src, dst = pairs[n - 2]
        return pltpu.make_async_remote_copy(
            src_ref=src, dst_ref=dst, send_sem=fac_s.at[n], recv_sem=fac_r.at[n],
            device_id={"dp": mate}, device_id_type=MESH,
        )

    def share_copy(k):
        ref = turned.at[k, count + t % 2]
        return pltpu.make_async_remote_copy(
            src_ref=ref, dst_ref=ref, send_sem=fac_s.at[4 + full + k], recv_sem=fac_r.at[4 + full + k],
            device_id={"tensor": core}, device_id_type=MESH,
        )

    def give_factor(*which):
        if chained:

            @pl.when(is_end)
            def _():
                for n in which:
                    factor_copy(n).start()

    def share_factor(k):
        if chained:

            @pl.when(is_mate)
            def _():
                factor_copy(k).wait_recv()
                share_copy(k).start()

    def cross_copy(slot, c):
        return pltpu.make_async_remote_copy(
            src_ref=sums.at[c, block((beyond, across)[slot]), :], dst_ref=arrived.at[slot, c],
            send_sem=ch_s.at[slot, c], recv_sem=ch_r.at[slot, c],
            device_id={"dp": across}, device_id_type=MESH,
        )

    def home_copy(c):
        return pltpu.make_async_remote_copy(
            src_ref=sums.at[c, block(mate), :], dst_ref=arrived.at[0, c],
            send_sem=ch_s.at[2, c], recv_sem=ch_r.at[0, c],
            device_id={"dp": mate}, device_id_type=MESH,
        )

    def rest_product(c, at, side):
        def by(n, right):
            return sum(mm(turned[n, side * count + i, at, :], right[i]) for i in range(count))

        if c < full:
            return by(0, (dqkv, dqkv2)[side].at[c])
        return wider(by(0, (dtail, dtail2)[side]), wide) + by(1, (far_att, far_att2)[side])

    def own_rest():
        @pl.when(is_end)
        def _():
            for c in range(full + 1):
                sums[c, block(z), :] = rest_product(c, block(z), 0).astype(BF16)

        @pl.when(is_mate)
        def _():
            def half(h, carry):
                at = pl.ds(pl.multiple_of(h * 2 * cut, 2 * cut), 2 * cut)
                for c in range(full + 1):
                    sums[c, at, :] = rest_product(c, at, 0).astype(BF16)
                return carry

            lax.fori_loop(0, 2, half, 0)

    def give_rest(c):
        def add(b):
            both_sides = sums[c, block(b), :].astype(F32) + rest_product(c, block(b), 1)
            sums[c, block(b), :] = both_sides.astype(BF16)

        @pl.when(is_mate)
        def _():
            if c < full:
                factor_copy(2 + c).wait_recv()
            else:
                share_copy(0).wait_recv()
                share_copy(1).wait_recv()
                factor_copy(2 + full).wait_recv()
                factor_copy(3 + full).wait_recv()
            add(beyond)
            cross_copy(0, c).start()
            if c < full:
                cross_copy(1, full if c == 0 else c - 1).start()
            add(across)
            if c == full - 1:
                cross_copy(1, c).start()
            add(z)

    def relay(c):
        @pl.when(is_mate)
        def _():
            cross_copy(0, c).wait_recv()
            home = sums[c, block(mate), :].astype(F32) + arrived[0, c].astype(F32)
            sums[c, block(mate), :] = home.astype(BF16)
            home_copy(c).start()

    def settle(c):
        def finish(slot, copy):
            copy.wait_recv()
            whole = sums[c, block(z), :].astype(F32) + arrived[slot, c].astype(F32)
            sums[c, block(z), :] = whole.astype(BF16)

        @pl.when(is_mate)
        def _():
            finish(1, cross_copy(1, c))

        @pl.when(is_end)
        def _():
            finish(0, home_copy(c))

    def weights_left():
        @pl.when(is_end)
        def _():
            for n in range(4 + full):
                factor_copy(n).wait_send()

        @pl.when(is_mate)
        def _():
            for k in range(2):
                share_copy(k).wait_send()
            for c in range(pieces):
                cross_copy(0, c).wait_send()
                cross_copy(1, c).wait_send()
                home_copy(c).wait_send()

        for n in range(2):
            for right in (True, False):

                @pl.when(z < ring - 1 if right else z > 0)
                def _():
                    line_copy(n, z, right).wait_send()

                for d in range(1, ring):
                    zs, there_is = upstream(d, right)

                    @pl.when(there_is)
                    def _():
                        line_share(n, zs).wait_send()

                        @pl.when(z < ring - 1 if right else z > 0)
                        def _():
                            line_copy(n, zs, right).wait_send()

    def line_copy(n, zs, right):
        ref = line.at[n, zs * count + t % 2]
        way = 0 if right else 1
        return pltpu.make_async_remote_copy(
            src_ref=ref, dst_ref=ref, send_sem=li_s.at[n, way, zs], recv_sem=li_r.at[n, way, zs],
            device_id={"dp": (z + 1) % ring if right else (z + ring - 1) % ring}, device_id_type=MESH,
        )

    def line_share(n, zs):
        ref = line.at[n, zs * count + t % 2]
        return pltpu.make_async_remote_copy(
            src_ref=ref, dst_ref=ref, send_sem=li_s.at[n, 2, zs], recv_sem=li_r.at[n, 2, zs],
            device_id={"tensor": core}, device_id_type=MESH,
        )

    def upstream(d, right):
        return (z - d, z >= d) if right else (z + d, z + d < ring)

    def line_start(n):
        if chained:
            for right in (True, False):

                @pl.when(z < ring - 1 if right else z > 0)
                def _():
                    line_copy(n, z, right).start()

    def line_pass(n, d):
        for right in (True, False) if chained else ():
            zs, there_is = upstream(d, right)

            @pl.when(there_is)
            def _():
                line_copy(n, zs, right).wait_recv()

                @pl.when(z < ring - 1 if right else z > 0)
                def _():
                    line_copy(n, zs, right).start()

                line_share(n, zs).start()

    def mlp_own():
        at = pl.ds(pl.multiple_of(z * cut, cut), cut)
        for m, n, right in ((0, 1, act), (1, 0, dh)):
            mlp_ref[m] = sum(mm(line[n, base + i, at, :], right[i]) for i in range(count))

    def mlp_of(zs):
        at = pl.ds(pl.multiple_of(z * cut, cut), cut)
        for n in range(2):
            line_share(n, zs).wait_recv()

        def step(j, carry):
            slot = zs * count + j // pieces
            cols = pl.ds(pl.multiple_of(j % pieces * (width // pieces), 128), width // pieces)
            v = mm(partial[0, cols, :], line[0, slot])
            value, slope = gelu_parts(v)
            back = (mm(w2_ref[cols, :], line[1, slot]) * slope).astype(BF16)
            mlp_ref[0, :, cols] += mm_nt(line[1, slot, at, :], value.astype(BF16))
            mlp_ref[1, :, cols] += mm_nt(line[0, slot, at, :], back)
            return carry

        lax.fori_loop(0, count * pieces, step, 0)

    def turn_image(k, i):
        ref, n = place[k]
        ref[n, base + i if ref is line else i] = gath[k % 3, i].T

    def turn(k):
        for i in range(count):
            turn_image(k, i)

    def each_image(body):
        def run(i, carry):
            body(i)
            return carry

        lax.fori_loop(0, count, run, 0)

    def norm(x, which, i):
        mean = jnp.mean(x, axis=-1, keepdims=True)
        centre = x - mean
        root = lax.rsqrt(jnp.mean(centre * centre, axis=-1, keepdims=True) + EPS)
        hat = centre * root
        xhat[which, i] = hat
        inv[which, i] = jnp.broadcast_to(root, (rows, 128))
        return (hat * gain_ref[which : which + 1, :] + shift_ref[which : which + 1, :]).astype(BF16)

    def norm_back(da, which, i):
        hat = xhat[which, i]
        tiny_s[0, which : which + 1, :] += jnp.sum(da * hat, axis=0, keepdims=True)
        tiny_s[0, 2 + which : 3 + which, :] += jnp.sum(da, axis=0, keepdims=True)
        dhat = da * gain_ref[which : which + 1, :]
        m1 = jnp.mean(dhat, axis=-1, keepdims=True)
        m2 = jnp.mean(dhat * hat, axis=-1, keepdims=True)
        return inv[which, i][:, :1] * (dhat - m1 - hat * m2)

    def turn_qkv():
        loads[1].wait()
        for r in range(0, width, wide):
            for c in range(3):
                partial[1, r : r + wide, c * wide : c * wide + local] = wq_ref[
                    c * local : (c + 1) * local, r : r + wide
                ].T

    def turn_weight(to, ref):
        for r in range(0, width, wide):
            to[r : r + wide, : ref.shape[0]] = ref[:, r : r + wide].T

    def lead(k, end, near):
        def first(i):
            end(i)

            @pl.when(i == count - 1)
            def _():
                ag_pass(k, 0)

            ag_near(k, i)
            near(i)

        each_image(first)

    def follow(k, rest):
        def second(i):
            ag_rest(k, i)
            rest(i)

            @pl.when(i < count - 1)
            def _():
                ag_pass(k, i + 1)

            rs_pass(k, i)

        each_image(second)

    tiny_s[...] = jnp.zeros_like(tiny_s)
    tok_ref[z] = jnp.zeros_like(tok_ref[z])
    emb_ref[z] = jnp.zeros_like(emb_ref[z])
    for load in loads[5:]:
        load.wait()
    emb_ref[z, :count, :] = temb_ref[...].astype(F32)

    def norm_input(i):
        gath[ATT, i, own, :] = norm(xin[i].astype(F32), 0, i)

    @pl.when(s == 0)
    def _():
        first_rows.wait()
        each_image(norm_input)

    pl.semaphore_wait(barrier, 3 + ring)
    over_ring(lambda j: tiny_copy(0, j).start())

    @pl.when(s == 1)
    def _():
        def begin(i):
            cot_rows(i).wait()
            ag_start(DMLP, i)

        each_image(begin)

    def take_input(i):
        mid_copy(i).wait_recv()
        norm_input(i)
        ag_start(ATT, i)

    lane = lax.broadcasted_iota(jnp.int32, (1, 2 * seq), 1)

    def choose():
        step = 128
        for r in range(0, 4 * seq, step):
            bucket = r + lax.broadcasted_iota(jnp.int32, (step, 4 * seq), 0)
            partial[1, r : r + step, : 4 * seq] = jnp.where(
                bucket == order_ref[:1, :], 1.0, 0.0
            ).astype(BF16)

    def tables():
        valid = lane < (2 * grid - 1) * grid
        slab = pltpu.roll(wider(rel_ref[:grid, :], 2 * seq), grid * (grid - 1), 1)
        for k in range(grid - 1):
            r = grid - 1 - k
            block = only(rel_ref[r * grid : (r + 1) * grid, :128], 0, grid)
            slab += pltpu.roll(wider(block, 2 * seq), k * grid, 1)
        none = jnp.full((1, 2 * seq), -1, jnp.int32)
        before = none
        for c in range(1, grid):
            moved = pltpu.roll(slab[c : c + 1, :], grid - c, 1)
            before = jnp.where((lane % grid == grid - c) & valid, moved, before)
        order = jnp.concatenate([jnp.where(valid, slab[:1, :], none), before], axis=1)
        order_ref[...] = jnp.broadcast_to(order, order_ref.shape)
        choose()
        tab[...] = jnp.zeros_like(tab)
        tab[:heads, : tab_ref.shape[1]] = tab_ref[...]
        found = add_thirds(mm(in_thirds(tab[...]), partial[1, : 4 * seq, : 4 * seq]))
        after, before = found[:, : 2 * seq], found[:, 2 * seq :]
        for c in range(grid):
            low = pltpu.roll(after, c, 1) if c else after
            high = pltpu.roll(before, 2 * seq - (grid - c), 1)
            row = jnp.where(lane % grid >= c, low, high)
            for h in range(heads):
                tx_ref[h, c : c + 1, :] = row[h : h + 1, :]

        def expand(h, carry):
            for r in range(grid):
                shift = (2 * seq - grid * (grid - 1 - r)) % (2 * seq)
                bias[h, r * grid : (r + 1) * grid, :] = pltpu.roll(tx_ref[h], shift, 1)[:, :seq]
            return carry

        lax.fori_loop(0, heads, expand, 0)
        loads[0].wait()
        tp_ref[...] = jnp.zeros_like(tp_ref)
        emb = jnp.concatenate([temb_ref[...], jnp.zeros((16 - count, width), BF16)], axis=0)
        for c in range(3):
            tp_ref[c] = mm_nt(emb, partial[0, c * local : (c + 1) * local, :])

    @pl.when(s == 1)
    def _():
        tables()

        def spread_cot(i):
            ag_pass(DMLP, i)
            ag_near(DMLP, i)
            ag_rest(DMLP, i)

        each_image(spread_cot)
        turn(DMLP)
        line_start(1)
        turn_qkv()
        loads[2].wait()
        turn_weight(sums.at[0], wo_ref)
        loads[3].wait()
        turn_weight(partial.at[0], w1_ref)
        loads[4].wait()

        def early(i):
            dh[i] = mm_nt(gath[DMLP, i], w2_ref[...]).astype(BF16)

        each_image(early)
        line_pass(1, 1)

    @pl.when(s == 0)
    def _():
        each_image(lambda i: ag_start(ATT, i))
        tables()
        turn_qkv()
        for n in (2, 3, 4):
            loads[n].wait()

    def project(i, half):
        a = gath[ATT, i, half_of(half), :]
        part = mm(a, partial[1, :, : 2 * wide + local])
        for c in range(3):
            qkv[c, i, half_of(half), :] = (
                part[:, c * wide : c * wide + local] + tp_ref[c, pl.ds(i, 1), :]
            ).astype(BF16)

    def att_first(i):
        @pl.when(s == 1)
        def _():
            take_input(i)

    lead(ATT, att_first, lambda i: project(i, here))

    def att_rest(i):
        project(i, there)
        acc[0] = jnp.zeros_like(acc[0])
        for h, (lo, hi, start, stop) in enumerate(windows):
            q = only(qkv[0, i, :, lo:hi], start, stop)
            scores = mm_nt(q, qkv[1, i, :, lo:hi]) * scale + bias[h]
            top = jnp.max(scores, axis=-1, keepdims=True)
            expo = jnp.exp(scores - top)
            p = expo * (1.0 / jnp.sum(expo, axis=-1, keepdims=True))
            p = p.astype(BF16)
            prob[i, h] = p
            acc[0, :, lo:hi] += mm(p, only(qkv[2, i, :, lo:hi], start, stop))
        att[i] = acc[0, :, :local].astype(BF16)
        far_att[i] = pltpu.roll(acc[0], far_att.shape[-1] - local, 1).astype(BF16)
        rs_give(ATT, i, 0, mm(att[i, half_of(there), :], wo_ref[...]))
        rs_give(ATT, i, 1, mm(att[i, half_of(here), :], wo_ref[...]))

    follow(ATT, att_rest)

    turn(ATT)
    give_factor(0, 3 + full)

    def att_end(i):
        y = xin[i].astype(F32) + rs_take(ATT, i)
        ag_done(ATT, i)
        rs_done(ATT, i)
        ymid[i] = y
        gath[MLP, i, own, :] = norm(y, 1, i)
        ag_start(MLP, i)

    def mlp_half(i, half, which):
        a = gath[MLP, i, half_of(half), :]
        v = mm(a, w1_ref[...])
        value, slope = gelu_parts(v)
        act[i, half_of(half), :] = value.astype(BF16)
        dgel[i, half_of(half), :] = slope.astype(BF16)
        rs_give(MLP, i, which, mm(act[i, half_of(half), :], w2_ref[...]))

    def mlp_end(i):
        y = (ymid[i] + rs_take(MLP, i)).astype(BF16)
        rs_done(MLP, i)

        @pl.when(s == 0)
        def _():
            ig_ref[i] = y
            mid_copy(i).start()

        @pl.when(s == 1)
        def _():
            out_ref[i] = y
            out_copy(i).start()

    def take_grad(i):
        mid_copy(i).wait_send()
        grad_copy(i).wait_recv()
        gath[DMLP, i, own, :] = xin[i]
        ag_start(DMLP, i)

    def dmlp_half(i, half, which):
        @pl.when(s == 0)
        def _():
            dh[i, half_of(half), :] = mm(gath[DMLP, i, half_of(half), :], partial[1]).astype(BF16)

        dact = dh[i, half_of(half), :].astype(F32)
        dh[i, half_of(half), :] = (dact * dgel[i, half_of(half), :].astype(F32)).astype(BF16)
        rs_give(DMLP, i, which, mm(dh[i, half_of(half), :], partial[0]))

    def mlp_rest(i):
        ag_rest(MLP, i)
        mlp_half(i, there, 0)

        @pl.when(i < count - 1)
        def _():
            ag_pass(MLP, i + 1)

        @pl.when(s == 0)
        def _():
            rs_pass(MLP, i)

        @pl.when(s == 1)
        def _():
            dmlp_half(i, there, 0)
            dmlp_half(i, here, 1)
            rs_pass(DMLP, i)

    lead(MLP, att_end, lambda i: mlp_half(i, here, 1))
    each_image(mlp_rest)
    turn(MLP)
    line_start(0)

    def dmlp_rest(i):
        @pl.when(i == count - 1)
        def _():
            turn(DMLP)
            line_start(1)

        dmlp_half(i, there, 0)

    @pl.when(s == 0)
    def _():
        each_image(mlp_end)
        turn_weight(partial.at[0], w1_ref)
        turn_weight(partial.at[1], w2_ref)
        turn_weight(sums.at[0], wo_ref)
        for d in range(1, ring):
            line_pass(0, d)
        lead(DMLP, take_grad, lambda i: dmlp_half(i, here, 1))
        follow(DMLP, dmlp_rest)

    @pl.when(s == 1)
    def _():
        last_rows.start()
        last_rows.wait()

    def dmlp_end(i):
        grad = xin[i].astype(F32) + norm_back(rs_take(DMLP, i), 1, i)
        rs_done(DMLP, i)
        dy1[i] = grad
        gath[DATT % 3, i, own, :] = grad.astype(BF16)
        ag_start(DATT, i)

    def datt_part(i, half):
        att[i, half_of(half), :] = mm(
            gath[DATT % 3, i, half_of(half), :], sums[0, :, :local]
        ).astype(BF16)

    def turn_factor(i):
        turn_image(DATT, i)

        @pl.when(i == t % 2)
        def _():
            give_factor(1)

    lead(DATT, dmlp_end, lambda i: datt_part(i, here))

    @pl.when(s == 0)
    def _():
        line_pass(1, 1)

        def gathered(i):
            ag_rest(DATT, i)
            turn_factor(i)

            @pl.when(i < count - 1)
            def _():
                ag_pass(DATT, i + 1)

        each_image(gathered)

    def datt_rest(i):
        @pl.when(s == 1)
        def _():
            ag_rest(DATT, i)

        datt_part(i, there)

        @pl.when(s == 1)
        def _():
            turn_factor(i)

        acc[...] = jnp.zeros_like(acc)
        for h, (lo, hi, start, stop) in enumerate(windows):
            q = only(qkv[0, i, :, lo:hi], start, stop)
            k = only(qkv[1, i, :, lo:hi], start, stop)
            d = only(att[i, :, lo:hi], start, stop)
            low = prob[i, h]
            p = low.astype(F32)
            dp = mm_nt(d, qkv[2, i, :, lo:hi])
            inner = jnp.sum(p * dp, axis=-1, keepdims=True)
            ds = (p * (dp - inner)).astype(BF16)

            @pl.when(i == 0)
            def _():
                bias[h] = ds.astype(F32)

            @pl.when(i > 0)
            def _():
                bias[h] += ds.astype(F32)

            acc[0, :, lo:hi] += mm(ds, k)
            acc[1, :, lo:hi] += mm_tn(ds, q)
            acc[2, :, lo:hi] += mm_tn(low, d)
        tiles = [None] * (lanes // 128)
        for c, by in enumerate((scale, scale, 1.0)):
            first = c * local // 128
            moved = acc[c] * by
            if c * local > first * 128:
                moved = pltpu.roll(moved, c * local - first * 128, 1)
            for n in range(moved.shape[1] // 128):
                tile = moved[:, n * 128 : (n + 1) * 128]
                tiles[first + n] = tile if tiles[first + n] is None else tiles[first + n] + tile
        per = wide // 128
        over_tokens = []
        for c in range(full + 1):
            part = jnp.concatenate(tiles[c * per : (c + 1) * per], axis=1).astype(BF16)
            if c < full:
                dqkv[c, i] = part
            else:
                dtail[i] = part
            over_tokens.append(jnp.sum(part.astype(F32), axis=0, keepdims=True))
        tok_ref[z, pl.ds(i, 1), :lanes] = jnp.concatenate(over_tokens, axis=1)
        last = 3 * local - full * wide
        for which, half in ((0, there), (1, here)):
            da = mm(dtail[i, half_of(half), :last], wq_ref[full * wide :, :])
            for c in range(full):
                da += mm(dqkv[c, i, half_of(half), :], wq_ref[c * wide : (c + 1) * wide, :])
            rs_give(DATT, i, which, da)

        @pl.when((s == 1) & (i < count - 1))
        def _():
            ag_pass(DATT, i + 1)

        rs_pass(DATT, i)

    each_image(datt_rest)

    give_factor(2 + full, *range(2, 2 + full))

    @pl.when(s == 1)
    def _():
        line_pass(0, 1)

    def first_parts():
        own_rest()
        mlp_own()
        share_factor(0)
        share_factor(1)
        choose()

    ig_store = pltpu.make_async_copy(ig_ref, ig_hbm, store_s.at[18])
    out_store = pltpu.make_async_copy(out_ref, out_hbm, store_s.at[19])

    def end_of_chain(r, carry):
        if chained:
            pl.when(r == s)(first_parts)

        @pl.when(r == 0)
        def _():
            line_pass(1, 2)

        @pl.when(r == 1)
        def _():
            line_pass(0, 2)

        if chained:

            @pl.when(r == s)
            def _():
                give_rest(full)

        @pl.when(r == 0)
        def _():

            def datt_end(i):
                grad = dy1[i] + norm_back(rs_take(DATT, i), 0, i)
                ig_ref[i] = grad.astype(BF16)

                @pl.when(s == 1)
                def _():
                    grad_copy(i).start()

            each_image(datt_end)

            ig_store.start()

            @pl.when(s == 0)
            def _():
                each_image(lambda i: out_copy(i).wait_recv())
                out_store.start()

            @pl.when(s == 1)
            def _():
                each_image(lambda i: rs_pass(MLP, i))

            for j in range(3):
                small_copy(0, j).start()

            def fold(h, carry):
                total = jnp.zeros((grid, 2 * seq), F32)
                for r in range(grid):
                    part = wider(bias[h, r * grid : (r + 1) * grid, :], 2 * seq)
                    shift = grid * (grid - 1 - r)
                    total += part if shift == 0 else pltpu.roll(part, shift, 1)
                after = total[:1, :]
                before = jnp.zeros((1, 2 * seq), F32)
                for c in range(1, grid):
                    row = total[c : c + 1, :]
                    late = lane % grid >= c
                    after += pltpu.roll(jnp.where(late, row, 0.0), 2 * seq - c, 1)
                    before += pltpu.roll(jnp.where(late, 0.0, row), grid - c, 1)
                tok_ref[z, pl.ds(count + h, 1), : 4 * seq] = jnp.concatenate([after, before], axis=1)
                return carry

            lax.fori_loop(0, heads, fold, 0)
            for j in range(3):
                small_copy(0, j).wait_recv()
            over_tensor = tiny_s[0] + small_r[0, 0] + small_r[0, 1] + small_r[0, 2]
            row = lax.broadcasted_iota(jnp.int32, over_tensor.shape, 0)
            tok_ref[z, count + heads : count + heads + 1, :] = jnp.sum(
                jnp.where(row == t, over_tensor, 0.0), axis=0, keepdims=True
            )
            over_ring(lambda j: tiny_copy(1, j).start())

            @pl.when(s == 1)
            def _():
                each_image(mlp_end)
                out_store.start()

        return carry

    lax.fori_loop(0, 1 + s, end_of_chain, 0)

    if chained:
        give_rest(0)

        def others(j, carry):
            d = 1 + j // 2
            zs = z - d + 2 * d * (j % 2)

            @pl.when((zs >= 0) & (zs < ring))
            def _():
                mlp_of(zs)

            @pl.when(j == 0)
            def _():
                for c in range(1, full):
                    give_rest(c)
                relay(full)
                relay(0)

            @pl.when(j == 1)
            def _():
                for c in range(1, full):
                    relay(c)

            @pl.when((j == 3) & (s == 1))
            def _():
                line_pass(0, 3)

            @pl.when(j == 3)
            def _():
                line_pass(1, 3)

            return carry

        lax.fori_loop(0, 2 * (ring - 1), others, 0)
    else:

        def whole(b, carry):
            at = block(b)
            parts_ref[0, b] = sum(mm(line[1, i, at, :], act[i]) for i in range(count)).astype(BF16)
            parts_ref[1, b] = sum(mm(line[0, i, at, :], dh[i]) for i in range(count)).astype(BF16)
            parts_ref[2, b] = jnp.concatenate(
                [rest_product(c, at, 0) for c in range(full + 1)], axis=1
            ).astype(BF16)
            return carry

        lax.fori_loop(0, blocks, whole, 0)
        choose()
    stores = []

    def store(src, dst):
        copy = pltpu.make_async_copy(src, dst, store_s.at[len(stores)])
        copy.start()
        stores.append(copy)
        return copy

    if chained:
        store(mlp_ref, mlp_hbm)
    over_ring(lambda j: tiny_copy(1, j).wait_recv())

    def add_slot(j, total):
        return total + tok_ref[j]

    total = lax.fori_loop(0, ring, add_slot, jnp.zeros(tok_ref.shape[1:], F32))
    tiny_s[1] = total
    for j in range(3):
        small_copy(1, j).start()
    tab[...] = jnp.zeros_like(tab)
    tab[:heads, :] = tiny_s[1, count : count + heads, : 4 * seq]
    found = add_thirds(mm_nt(in_thirds(tab[...]), partial[1, : 4 * seq, : 4 * seq]))
    gtab_ref[...] = found[:heads, : gtab_ref.shape[1]]
    store(gtab_ref, gtab_hbm)

    over_ring(lambda j: tiny_copy(0, j).wait_recv())
    mine = width // ring
    rows_of_emb = emb_ref[...].reshape(ring * 8, width)
    rows_of_emb = pltpu.roll(rows_of_emb, (width - z * mine) % width, 1)[:, :mine].astype(BF16)
    right = in_thirds(tok_ref[...].reshape(ring * 8, width)[:, :lanes])
    over_images = mm_tn(jnp.concatenate([rows_of_emb] * 3, axis=0), right)
    time_stores = []
    for c in range(3):
        first = c * local // 128 * 128
        window = over_images[:, first : first + wide]
        if c * local > first:
            window = pltpu.roll(window, wide - (c * local - first), 1)
        exact[c, :mine, :] = window[:, :local]
        time_stores.append(store(exact.at[c], gt_hbm.at[c]))
    if chained:
        settle(full)
        window = sums[full, block(z), :].astype(F32)
        window = pltpu.roll(window, wide - (3 * local - (width - wide)), 1)
        for copy in time_stores:
            copy.wait()
        exact[0] = window.T[:local]
        out_grad_store = store(exact.at[0], go_hbm)
    for j in range(3):
        small_copy(1, j).wait_recv()
    last = count + heads
    small_ref[pl.ds(t, 1), :] = tiny_s[1, last : last + 1, :]
    for j, owner in enumerate((core, far, fcore)):
        small_ref[pl.ds(owner, 1), :] = small_r[1, j, last : last + 1, :]
    ggain_ref[...] = small_ref[:2, :]
    gshift_ref[...] = small_ref[2:, :]
    store(ggain_ref, ggain_hbm)
    store(gshift_ref, gshift_hbm)
    if chained:
        settled = 0
        for c in range(3):
            first = c * local // 128 * 128
            while settled < full and settled * wide < first + wide:
                settle(settled)
                settled += 1
            n, offset = first // wide, first % wide
            window = sums[n, block(z), offset:]
            if offset:
                window = jnp.concatenate([window, sums[n + 1, block(z), :offset]], axis=1)
            window = window.astype(F32)
            if c * local > first:
                window = pltpu.roll(window, wide - (c * local - first), 1)
            if c == 0:
                out_grad_store.wait()
            exact[c] = window[:, :local]
            store(exact.at[c], gq_hbm.at[c])

    def finish(i):
        for k in (MLP, DMLP, DATT):
            ag_done(k, i)
        rs_done(DATT, i)

        @pl.when(s == 1)
        def _():
            out_copy(i).wait_send()
            grad_copy(i).wait_send()

    each_image(finish)
    ig_store.wait()
    out_store.wait()

    def tiny_left(j):
        tiny_copy(0, j).wait_send()
        tiny_copy(1, j).wait_send()

    over_ring(tiny_left)
    for j in range(3):
        small_copy(0, j).wait_send()
        small_copy(1, j).wait_send()
    if chained:
        weights_left()
    waited = time_stores + [out_grad_store] if chained else []
    for copy in stores:
        if all(copy is not done for done in waited):
            copy.wait()


def run_block(x, cot, wq, wt, wo, w1, w2, temb, gain, shift, rel, table, ring):
    count, rows, width = x.shape
    seq = rel.shape[0]
    heads = table.shape[0]
    local = wo.shape[0]
    hidden = w1.shape[1]
    chained = ring == 4 and count == 2 and width % (16 * ring) == 0 and local == width // ring
    blocks = 4
    pieces = 3 if width // 4 % 48 == 0 else 1
    cut = width // blocks
    padded = -(-local // 128) * 128
    lanes = -(-3 * local // 128) * 128
    dims = (count, rows, seq, heads, ring, chained)
    full = 3 * local // padded
    assert pieces == full + 1 and padded * pieces == width
    mine = width // ring
    small = (8, 128)
    out_shape = [
        jax.ShapeDtypeStruct((count, rows, width), BF16),
        jax.ShapeDtypeStruct((count, rows, width), BF16),
        jax.ShapeDtypeStruct((16, 128) if chained else (3, blocks, cut, width), BF16),
        jax.ShapeDtypeStruct((2, cut, width) if chained else small, F32),
        jax.ShapeDtypeStruct((3, cut, local) if chained else small, F32),
        jax.ShapeDtypeStruct((local, cut) if chained else small, F32),
        jax.ShapeDtypeStruct((3, -(-mine // 8) * 8, local), F32),
        jax.ShapeDtypeStruct(table.shape, F32),
        jax.ShapeDtypeStruct((2, width), F32),
        jax.ShapeDtypeStruct((2, width), F32),
    ]
    vm = pltpu.VMEM
    dma = pltpu.SemaphoreType.DMA
    scratch = [
        vm(temb.shape, BF16),
        vm(gain.shape, F32),
        vm(shift.shape, F32),
        vm(rel.shape, jnp.int32),
        vm(table.shape, F32),
        vm((count, rows, width), BF16),
        vm((count, rows, width), BF16),
        vm((2, cut, width) if chained else (2, 8, 128), F32),
        vm((3, -(-mine // 8) * 8, local), F32),
        vm((ring, 8, width), F32),
        vm((ring, 8, width), F32),
        vm(table.shape, F32),
        vm((4, width), F32),
        vm((2, width), F32),
        vm((2, width), F32),
        vm(wq.shape, BF16),
        vm(wo.shape, BF16),
        vm(w1.shape, BF16),
        vm(w2.shape, BF16),
        vm((3, 16, local), F32),
        vm((heads, int(round(seq**0.5)), 2 * seq), F32),
        vm((8, 4 * seq), jnp.int32),
        vm((16, 4 * seq), F32),
        vm((2, width, width), BF16),
        vm((pieces, width, padded), BF16),
        vm((2, pieces, cut, padded) if chained else (16, 128), BF16),
        vm((2, 8, width), F32),
        vm((2, 3, 8, width), F32),
        vm((count, rows, width), BF16),
        vm((3, count, seq, width), BF16),
        vm((2, count, 2, rows, width), F32),
        vm((2, count, 2, rows, width), BF16),
        vm((2, count, rows, width), BF16),
        vm((2, count, 2, rows, width), BF16),
        vm((2, count, rows, width), BF16),
        vm((heads, seq, seq), F32),
        vm((count, heads, seq, seq), BF16),
        vm((3, count, seq, local), BF16),
        vm((count, seq, local), BF16),
        vm((count, seq, hidden), BF16),
        vm((count, seq, hidden), BF16),
        vm((2, count, rows, width), F32),
        vm((2, count, rows, 128), F32),
        vm((count, rows, width), F32),
        vm((count, rows, width), F32),
        vm((full, count, seq, padded), BF16),
        vm((count, seq, lanes - full * padded), BF16),
        vm((count, seq, hidden), BF16),
        vm((3, seq, padded), F32),
        vm((2, 2 * count if chained else count, width, seq), BF16),
        vm((2, ring * count if chained else count, width, seq), BF16),
        vm((count, seq, padded), BF16),
        vm((full, count, seq, padded) if chained else (16, 128), BF16),
        vm((count, seq, lanes - full * padded) if chained else (16, 128), BF16),
        vm((count, seq, padded) if chained else (16, 128), BF16),
        dma((12 + count,)),
        dma((20,)),
        dma((4, count, 3)),
        dma((4, count, 3)),
        dma((4, count, 3)),
        dma((4, count, 3)),
        dma((3, count)),
        dma((3, count)),
        dma((3, pieces)),
        dma((2, pieces)),
        dma((6 + full,)),
        dma((6 + full,)),
        dma((2, 3, ring)),
        dma((2, 3, ring)),
        dma((2, ring)),
        dma((2, ring)),
        dma((2, 3)),
        dma((2, 3)),
    ]
    whole = pl.BlockSpec(memory_space=pltpu.VMEM)
    lies = pl.BlockSpec(memory_space=pl.ANY)
    return pl.pallas_call(
        functools.partial(block_kernel, dims),
        out_shape=out_shape,
        in_specs=[lies] * 12,
        out_specs=[lies] * 2 + [lies if chained else whole] + [lies] * 7,
        scratch_shapes=scratch,
        compiler_params=pltpu.CompilerParams(
            collective_id=0, has_side_effects=True, vmem_limit_bytes=63 * 2**20
        ),
        name="blocks",
    )(x, cot, wq, wt, wo, w1, w2, temb, gain, shift, rel, table)


def per_device(
    images, timesteps, t_table, rel_index, w_qkv, w_time, w_out, w_fc1, w_fc2, rel_table,
    norm_gain, norm_shift, cotangent,
):
    ring = lax.axis_size("dp")
    count = images.shape[0]
    width = images.shape[-1]
    local = w_out.shape[1]
    cut = width // ring
    steps = lax.broadcasted_iota(jnp.int32, (count, t_table.shape[0]), 1)
    embedded = jnp.dot(
        (steps == timesteps[:, None]).astype(BF16), t_table, preferred_element_type=F32
    ).astype(BF16)
    wq = jnp.transpose(w_qkv[0], (1, 2, 0)).reshape(3 * local, width)
    wt = jnp.transpose(w_time[0], (1, 2, 0)).reshape(3 * local, width)
    output, in_grad, parts, mlp, g_qkv, g_out, g_time, g_table, g_gain, g_shift = run_block(
        images, cotangent, wq, wt, w_out[0], w_fc1[0], w_fc2[0], embedded, norm_gain[0], norm_shift[0],
        rel_index, rel_table[0].T, ring,
    )
    if parts.ndim == 4:
        parts = lax.psum_scatter(
            parts.reshape(3, width, width), "dp", scatter_dimension=1, tiled=True
        ).astype(F32)
        g_fc2, g_fc1, rest = parts
        g_qkv = jnp.transpose(rest[:, : 3 * local].reshape(cut, 3, local), (1, 0, 2))
        g_out = rest[:, 3 * local :].T
    else:
        g_fc2, g_fc1 = mlp
    g_time = g_time[:, : width // ring]
    return (
        output, in_grad[None], jnp.transpose(g_qkv, (1, 0, 2))[None],
        jnp.transpose(g_time, (1, 0, 2))[None], g_out[None], g_fc1[None], g_fc2.T[None],
        g_table.T[None], g_gain[None], g_shift[None],
    )


def solution(mesh):
    in_specs = (
        P("dp", "tensor", None),
        P("dp"),
        P(),
        P(),
        P("section", None, None, "tensor"),
        P("section", None, None, "tensor"),
        P("section", "tensor", None),
        P("section", None, "tensor"),
        P("section", "tensor", None),
        P("section", None, "tensor"),
        P("section", None, None),
        P("section", None, None),
        P("dp", "tensor", None),
    )
    out_specs = (
        P("dp", "tensor", None),
        P("section", "dp", "tensor", None),
        P("section", "dp", None, "tensor"),
        P("section", "dp", None, "tensor"),
        P("section", "tensor", "dp"),
        P("section", "dp", "tensor"),
        P("section", "tensor", "dp"),
        P("section", None, "tensor"),
        P("section", None, None),
        P("section", None, None),
    )
    return jax.shard_map(
        per_device, mesh=mesh, in_specs=in_specs, out_specs=out_specs, check_vma=False
    )
```

```python
import functools

import jax
import jax.numpy as jnp
from jax import lax
from jax.experimental import pallas as pl
from jax.experimental.pallas import tpu as pltpu
from jax.sharding import PartitionSpec as P

MESH = pl.DeviceIdType.MESH
F32 = jnp.float32
BF16 = jnp.bfloat16
EPS = 1e-06
GELU_A = 0.7978845608028654
GELU_B = 0.044715
ATT, MLP, DMLP, DATT = range(4)
slot_of = (0, 1, 0, 0)


def mm(a, b):
    return lax.dot_general(a, b, (((1,), (0,)), ((), ())), preferred_element_type=F32)


def mm_nt(a, b):
    return lax.dot_general(a, b, (((1,), (1,)), ((), ())), preferred_element_type=F32)


def mm_tn(a, b):
    return lax.dot_general(a, b, (((0,), (0,)), ((), ())), preferred_element_type=F32)


def gelu_parts(v):
    square = v * v
    th = jnp.tanh(v * (GELU_A + (GELU_A * GELU_B) * square))
    up = 0.5 + 0.5 * th
    slope = up + v * (1.0 - th * th) * (0.5 * GELU_A + (1.5 * GELU_A * GELU_B) * square)
    return v * up, slope


def head_windows(heads, local):
    width = local // heads
    found = []
    for h in range(heads):
        lo = h * width // 128 * 128
        hi = min(-(-(h + 1) * width // 128) * 128, local)
        found.append((lo, hi, h * width - lo, (h + 1) * width - lo))
    return found


def only(x, start, stop):
    lane = lax.broadcasted_iota(jnp.int32, x.shape, 1)
    return jnp.where((lane >= start) & (lane < stop), x, jnp.zeros_like(x))


def in_thirds(x):
    high = x.astype(BF16)
    rest = x - high.astype(F32)
    middle = rest.astype(BF16)
    low = (rest - middle.astype(F32)).astype(BF16)
    return jnp.concatenate([high, middle, low], axis=0)


def add_thirds(x):
    rows = x.shape[0] // 3
    return x[:rows] + x[rows : 2 * rows] + x[2 * rows :]


def wider(x, lanes):
    return jnp.concatenate([x, jnp.zeros((x.shape[0], lanes - x.shape[1]), x.dtype)], axis=1)


def block_kernel(
    cfg,
    x_hbm, cot_hbm, wq_hbm, wt_hbm, wo_hbm, w1_hbm, w2_hbm, temb_hbm, gain_hbm, shift_hbm, rel_hbm, tab_hbm,
    out_hbm, ig_hbm, parts_ref, mlp_hbm, gq_hbm, go_hbm, gt_hbm, gtab_hbm, ggain_hbm, gshift_hbm,
    temb_ref, gain_ref, shift_ref, rel_ref, tab_ref, out_ref, ig_ref, mlp_ref, exact, tok_ref, emb_ref,
    gtab_ref, small_ref, ggain_ref, gshift_ref,
    wq_ref, wo_ref, w1_ref, w2_ref, tp_ref, tx_ref, order_ref, tab, partial, sums, arrived,
    tiny_s, small_r,
    xin, gath, keep, rcv_c, rcv_y, snd_c, snd_y, bias, prob, qkv, att, act, dgel,
    xhat, inv, ymid, dy1, dqkv, dtail, dh, acc, turned, line, far_att, dqkv2, dtail2, far_att2,
    load_s, store_s, ag_s, ag_r, rs_s, rs_r, sec_s, sec_r, ch_s, ch_r, fac_s, fac_r, li_s, li_r, ti_s, ti_r, sm_s, sm_r,
):
    count, rows, seq, heads, ring, chained = cfg
    half_rows = 2 * rows
    wide = -(-wo_ref.shape[0] // 128) * 128
    width = x_hbm.shape[-1]
    local = wo_ref.shape[0]
    grid = int(round(seq**0.5))
    windows = head_windows(heads, local)
    scale = (local // heads) ** (-0.5)
    blocks = 4
    cut = width // blocks
    pieces = sums.shape[0]
    slim = cut // pieces
    full = dqkv.shape[0]
    lanes = full * dqkv.shape[-1] + dtail.shape[-1]

    s = lax.axis_index("section")
    t = lax.axis_index("tensor")
    z = lax.axis_index("dp")
    core = t + 1 - 2 * (t % 2)
    far = (t + 2) % 4
    fcore = (core + 2) % 4
    here = t // 2
    there = 1 - here
    own = pl.ds(pl.multiple_of(t * rows, rows), rows)

    wt_ref = partial.at[0, : 3 * local, :]

    loads = [
        pltpu.make_async_copy(src, dst, load_s.at[n])
        for n, (src, dst) in enumerate(
            (
                (wt_hbm, wt_ref), (wq_hbm, wq_ref), (wo_hbm, wo_ref), (w1_hbm, w1_ref), (w2_hbm, w2_ref),
                (temb_hbm, temb_ref), (gain_hbm, gain_ref), (shift_hbm, shift_ref), (rel_hbm, rel_ref),
                (tab_hbm, tab_ref),
            )
        )
    ]
    first_rows = pltpu.make_async_copy(x_hbm, xin, load_s.at[10])
    last_rows = pltpu.make_async_copy(cot_hbm, xin, load_s.at[11])

    def cot_rows(i):
        return pltpu.make_async_copy(cot_hbm.at[i], gath.at[DMLP, i, own, :], load_s.at[12 + i])

    @pl.when(s == 0)
    def _():
        first_rows.start()

    @pl.when(s == 1)
    def _():
        for i in range(count):
            cot_rows(i).start()

    for load in loads[5:] + loads[:5]:
        load.start()

    barrier = pltpu.get_barrier_semaphore()
    for peer in ({"tensor": core}, {"tensor": far}, {"tensor": fcore}, {"section": 1 - s}):
        pl.semaphore_signal(barrier, inc=1, device_id=peer, device_id_type=MESH)

    def greet(j, carry):
        pl.semaphore_signal(barrier, inc=1, device_id={"dp": (z + j) % ring}, device_id_type=MESH)
        return carry

    lax.fori_loop(1, ring, greet, 0)

    def rows_of(owner):
        return pl.ds(pl.multiple_of(owner * rows, rows), rows)

    def half_of(half):
        return pl.ds(pl.multiple_of(half * half_rows, half_rows), half_rows)

    def ag_copy(k, i, which):
        owner, to = ((t, core), (t, far), (far, core))[which]
        ref = gath.at[k % 3, i, rows_of(owner), :]
        return pltpu.make_async_remote_copy(
            src_ref=ref, dst_ref=ref, send_sem=ag_s.at[k, i, which], recv_sem=ag_r.at[k, i, which],
            device_id={"tensor": to}, device_id_type=MESH,
        )

    def ag_start(k, i):
        ag_copy(k, i, 1).start()
        ag_copy(k, i, 0).start()

    def ag_near(k, i):
        ag_copy(k, i, 0).wait_recv()

    def ag_pass(k, i):
        ag_copy(k, i, 1).wait_recv()
        ag_copy(k, i, 2).start()

    def ag_rest(k, i):
        ag_copy(k, i, 2).wait_recv()

    def ag_done(k, i):
        for which in range(3):
            ag_copy(k, i, which).wait_send()

    def rs_copy(k, i, which):
        if which < 2:
            src, dst, to = snd_c.at[slot_of[k], i, which], rcv_c.at[slot_of[k], i, which], core
        else:
            src, dst, to = snd_y.at[slot_of[k], i], rcv_y.at[slot_of[k], i], far
        return pltpu.make_async_remote_copy(
            src_ref=src, dst_ref=dst, send_sem=rs_s.at[k, i, which], recv_sem=rs_r.at[k, i, which],
            device_id={"tensor": to}, device_id_type=MESH,
        )

    def rs_give(k, i, which, part):
        odd = t % 2 == 1
        low, high = part[:rows], part[rows:]
        snd_c[slot_of[k], i, which] = jnp.where(odd, low, high).astype(BF16)
        rs_copy(k, i, which).start()
        keep[slot_of[k], i, which] = jnp.where(odd, high, low)

    def rs_pass(k, i):
        rs_copy(k, i, 0).wait_recv()
        snd_y[slot_of[k], i] = (keep[slot_of[k], i, 0] + rcv_c[slot_of[k], i, 0].astype(F32)).astype(BF16)
        rs_copy(k, i, 2).start()

    def rs_take(k, i):
        rs_copy(k, i, 1).wait_recv()
        near = keep[slot_of[k], i, 1] + rcv_c[slot_of[k], i, 1].astype(F32)
        rs_copy(k, i, 2).wait_recv()
        return near + rcv_y[slot_of[k], i].astype(F32)

    def rs_done(k, i):
        for which in range(3):
            rs_copy(k, i, which).wait_send()

    def sec_copy(j, src, dst):
        return lambda i: pltpu.make_async_remote_copy(
            src_ref=src.at[i], dst_ref=dst.at[i], send_sem=sec_s.at[j, i], recv_sem=sec_r.at[j, i],
            device_id={"section": 1 - s}, device_id_type=MESH,
        )

    mid_copy = sec_copy(0, ig_ref, xin)
    grad_copy = sec_copy(1, ig_ref, xin)
    out_copy = sec_copy(2, out_ref, out_ref)

    def tiny_copy(n, j):
        ref = (emb_ref, tok_ref)[n]
        return pltpu.make_async_remote_copy(
            src_ref=ref.at[z], dst_ref=ref.at[z], send_sem=ti_s.at[n, j], recv_sem=ti_r.at[n, j],
            device_id={"dp": (z + j) % ring}, device_id_type=MESH,
        )

    def over_ring(body):
        def run(j, carry):
            body(j)
            return carry

        lax.fori_loop(1, ring, run, 0)

    def small_copy(n, j):
        return pltpu.make_async_remote_copy(
            src_ref=tiny_s.at[n], dst_ref=small_r.at[n, j], send_sem=sm_s.at[n, j], recv_sem=sm_r.at[n, j],
            device_id={"tensor": (core, far, fcore)[j]}, device_id_type=MESH,
        )

    mate = z + 1 - 2 * (z % 2)
    across = 3 - z
    beyond = 3 * (2 - z)
    is_end = (z == 0) | (z == 3)
    is_mate = (z == 1) | (z == 2)
    base = z * count if chained else 0
    place = {ATT: (turned, 0), DATT: (turned, 1), MLP: (line, 0), DMLP: (line, 1)}

    def block(b):
        return pl.ds(pl.multiple_of(b * cut, cut), cut)

    mate_rows = pl.ds(pl.multiple_of((1 - z // 2) * cut, cut), 3 * cut)

    def factor_copy(n):
        if n < 2:
            src, dst = turned.at[n, t % 2, mate_rows, :], turned.at[n, count + t % 2, mate_rows, :]
        else:
            pairs = [(dqkv.at[c], dqkv2.at[c]) for c in range(full)] + [(dtail, dtail2), (far_att, far_att2)]
            src, dst = pairs[n - 2]
        return pltpu.make_async_remote_copy(
            src_ref=src, dst_ref=dst, send_sem=fac_s.at[n], recv_sem=fac_r.at[n],
            device_id={"dp": mate}, device_id_type=MESH,
        )

    def share_copy(k):
        ref = turned.at[k, count + t % 2, mate_rows, :]
        return pltpu.make_async_remote_copy(
            src_ref=ref, dst_ref=ref, send_sem=fac_s.at[4 + full + k], recv_sem=fac_r.at[4 + full + k],
            device_id={"tensor": core}, device_id_type=MESH,
        )

    def give_factor(*which):
        if chained:

            @pl.when(is_end)
            def _():
                for n in which:
                    factor_copy(n).start()

    def share_factor(k):
        if chained:

            @pl.when(is_mate)
            def _():
                factor_copy(k).wait_recv()
                share_copy(k).start()

    def cross_copy(slot, c):
        return pltpu.make_async_remote_copy(
            src_ref=sums.at[c, block((beyond, across)[slot]), :], dst_ref=arrived.at[slot, c],
            send_sem=ch_s.at[slot, c], recv_sem=ch_r.at[slot, c],
            device_id={"dp": across}, device_id_type=MESH,
        )

    def home_copy(c):
        return pltpu.make_async_remote_copy(
            src_ref=sums.at[c, block(mate), :], dst_ref=arrived.at[0, c],
            send_sem=ch_s.at[2, c], recv_sem=ch_r.at[0, c],
            device_id={"dp": mate}, device_id_type=MESH,
        )

    def rest_product(c, at, side):
        def by(n, right):
            return sum(mm(turned[n, side * count + i, at, :], right[i]) for i in range(count))

        if c < full:
            return by(0, (dqkv, dqkv2)[side].at[c])
        return wider(by(0, (dtail, dtail2)[side]), wide) + by(1, (far_att, far_att2)[side])

    def own_rest():
        @pl.when(is_end)
        def _():
            for c in range(full + 1):
                sums[c, block(z), :] = rest_product(c, block(z), 0).astype(BF16)

        @pl.when(is_mate)
        def _():
            def half(h, carry):
                at = pl.ds(pl.multiple_of(h * 2 * cut, 2 * cut), 2 * cut)
                for c in range(full + 1):
                    sums[c, at, :] = rest_product(c, at, 0).astype(BF16)
                return carry

            lax.fori_loop(0, 2, half, 0)

    def give_rest(c):
        def add(b):
            both_sides = sums[c, block(b), :].astype(F32) + rest_product(c, block(b), 1)
            sums[c, block(b), :] = both_sides.astype(BF16)

        @pl.when(is_mate)
        def _():
            if c < full:
                factor_copy(2 + c).wait_recv()
            else:
                share_copy(0).wait_recv()
                share_copy(1).wait_recv()
                factor_copy(2 + full).wait_recv()
                factor_copy(3 + full).wait_recv()
            add(beyond)
            cross_copy(0, c).start()
            if c < full:
                cross_copy(1, full if c == 0 else c - 1).start()
            add(across)
            if c == full - 1:
                cross_copy(1, c).start()
            add(z)

    def relay(c):
        @pl.when(is_mate)
        def _():
            cross_copy(0, c).wait_recv()
            home = sums[c, block(mate), :].astype(F32) + arrived[0, c].astype(F32)
            sums[c, block(mate), :] = home.astype(BF16)
            home_copy(c).start()

    def settle(c):
        def finish(slot, copy):
            copy.wait_recv()
            whole = sums[c, block(z), :].astype(F32) + arrived[slot, c].astype(F32)
            sums[c, block(z), :] = whole.astype(BF16)

        @pl.when(is_mate)
        def _():
            finish(1, cross_copy(1, c))

        @pl.when(is_end)
        def _():
            finish(0, home_copy(c))

    def weights_left():
        @pl.when(is_end)
        def _():
            for n in range(4 + full):
                factor_copy(n).wait_send()

        @pl.when(is_mate)
        def _():
            for k in range(2):
                share_copy(k).wait_send()
            for c in range(pieces):
                cross_copy(0, c).wait_send()
                cross_copy(1, c).wait_send()
                home_copy(c).wait_send()

        for n in range(2):
            for right in (True, False):

                @pl.when(z < ring - 1 if right else z > 0)
                def _():
                    line_copy(n, z, right).wait_send()

                for d in range(1, ring):
                    zs, there_is = upstream(d, right)

                    @pl.when(there_is)
                    def _():
                        line_share(n, zs).wait_send()

                        @pl.when(z < ring - 1 if right else z > 0)
                        def _():
                            line_copy(n, zs, right).wait_send()

    def line_copy(n, zs, right):
        ref = line.at[n, zs * count + t % 2]
        way = 0 if right else 1
        return pltpu.make_async_remote_copy(
            src_ref=ref, dst_ref=ref, send_sem=li_s.at[n, way, zs], recv_sem=li_r.at[n, way, zs],
            device_id={"dp": (z + 1) % ring if right else (z + ring - 1) % ring}, device_id_type=MESH,
        )

    def line_share(n, zs):
        ref = line.at[n, zs * count + t % 2]
        return pltpu.make_async_remote_copy(
            src_ref=ref, dst_ref=ref, send_sem=li_s.at[n, 2, zs], recv_sem=li_r.at[n, 2, zs],
            device_id={"tensor": core}, device_id_type=MESH,
        )

    def upstream(d, right):
        return (z - d, z >= d) if right else (z + d, z + d < ring)

    def line_start(n):
        if chained:
            for right in (True, False):

                @pl.when(z < ring - 1 if right else z > 0)
                def _():
                    line_copy(n, z, right).start()

    def line_pass(n, d):
        for right in (True, False) if chained else ():
            zs, there_is = upstream(d, right)

            @pl.when(there_is)
            def _():
                line_copy(n, zs, right).wait_recv()

                @pl.when(z < ring - 1 if right else z > 0)
                def _():
                    line_copy(n, zs, right).start()

                line_share(n, zs).start()

    def mlp_own():
        at = pl.ds(pl.multiple_of(z * cut, cut), cut)
        for m, n, right in ((0, 1, act), (1, 0, dh)):
            mlp_ref[m] = sum(mm(line[n, base + i, at, :], right[i]) for i in range(count))

    def mlp_of(zs):
        at = pl.ds(pl.multiple_of(z * cut, cut), cut)
        for n in range(2):
            line_share(n, zs).wait_recv()

        def step(j, carry):
            slot = zs * count + j // pieces
            cols = pl.ds(pl.multiple_of(j % pieces * (width // pieces), 128), width // pieces)
            v = mm(partial[0, cols, :], line[0, slot])
            value, slope = gelu_parts(v)
            back = (mm(w2_ref[cols, :], line[1, slot]) * slope).astype(BF16)
            mlp_ref[0, :, cols] += mm_nt(line[1, slot, at, :], value.astype(BF16))
            mlp_ref[1, :, cols] += mm_nt(line[0, slot, at, :], back)
            return carry

        lax.fori_loop(0, count * pieces, step, 0)

    def turn_image(k, i):
        ref, n = place[k]
        ref[n, base + i if ref is line else i] = gath[k % 3, i].T

    def turn(k):
        for i in range(count):
            turn_image(k, i)

    def each_image(body):
        def run(i, carry):
            body(i)
            return carry

        lax.fori_loop(0, count, run, 0)

    def norm(x, which, i):
        mean = jnp.mean(x, axis=-1, keepdims=True)
        centre = x - mean
        root = lax.rsqrt(jnp.mean(centre * centre, axis=-1, keepdims=True) + EPS)
        hat = centre * root
        xhat[which, i] = hat
        inv[which, i] = jnp.broadcast_to(root, (rows, 128))
        return (hat * gain_ref[which : which + 1, :] + shift_ref[which : which + 1, :]).astype(BF16)

    def norm_back(da, which, i):
        hat = xhat[which, i]
        tiny_s[0, which : which + 1, :] += jnp.sum(da * hat, axis=0, keepdims=True)
        tiny_s[0, 2 + which : 3 + which, :] += jnp.sum(da, axis=0, keepdims=True)
        dhat = da * gain_ref[which : which + 1, :]
        m1 = jnp.mean(dhat, axis=-1, keepdims=True)
        m2 = jnp.mean(dhat * hat, axis=-1, keepdims=True)
        return inv[which, i][:, :1] * (dhat - m1 - hat * m2)

    def turn_qkv():
        loads[1].wait()
        for r in range(0, width, wide):
            for c in range(3):
                partial[1, r : r + wide, c * wide : c * wide + local] = wq_ref[
                    c * local : (c + 1) * local, r : r + wide
                ].T

    def turn_weight(to, ref):
        for r in range(0, width, wide):
            to[r : r + wide, : ref.shape[0]] = ref[:, r : r + wide].T

    def lead(k, end, near):
        def first(i):
            end(i)

            @pl.when(i == count - 1)
            def _():
                ag_pass(k, 0)

            ag_near(k, i)
            near(i)

        each_image(first)

    def follow(k, rest):
        def second(i):
            ag_rest(k, i)
            rest(i)

            @pl.when(i < count - 1)
            def _():
                ag_pass(k, i + 1)

            rs_pass(k, i)

        each_image(second)

    tiny_s[...] = jnp.zeros_like(tiny_s)
    tok_ref[z] = jnp.zeros_like(tok_ref[z])
    emb_ref[z] = jnp.zeros_like(emb_ref[z])
    for load in loads[5:]:
        load.wait()
    emb_ref[z, :count, :] = temb_ref[...].astype(F32)

    def norm_input(i):
        gath[ATT, i, own, :] = norm(xin[i].astype(F32), 0, i)

    @pl.when(s == 0)
    def _():
        first_rows.wait()
        each_image(norm_input)

    pl.semaphore_wait(barrier, 3 + ring)
    over_ring(lambda j: tiny_copy(0, j).start())

    @pl.when(s == 1)
    def _():
        def begin(i):
            cot_rows(i).wait()
            ag_start(DMLP, i)

        each_image(begin)

    def take_input(i):
        mid_copy(i).wait_recv()
        norm_input(i)
        ag_start(ATT, i)

    lane = lax.broadcasted_iota(jnp.int32, (1, 2 * seq), 1)

    def choose():
        step = 128
        for r in range(0, 4 * seq, step):
            bucket = r + lax.broadcasted_iota(jnp.int32, (step, 4 * seq), 0)
            partial[1, r : r + step, : 4 * seq] = jnp.where(
                bucket == order_ref[:1, :], 1.0, 0.0
            ).astype(BF16)

    def tables():
        valid = lane < (2 * grid - 1) * grid
        slab = pltpu.roll(wider(rel_ref[:grid, :], 2 * seq), grid * (grid - 1), 1)
        for k in range(grid - 1):
            r = grid - 1 - k
            block = only(rel_ref[r * grid : (r + 1) * grid, :128], 0, grid)
            slab += pltpu.roll(wider(block, 2 * seq), k * grid, 1)
        none = jnp.full((1, 2 * seq), -1, jnp.int32)
        before = none
        for c in range(1, grid):
            moved = pltpu.roll(slab[c : c + 1, :], grid - c, 1)
            before = jnp.where((lane % grid == grid - c) & valid, moved, before)
        order = jnp.concatenate([jnp.where(valid, slab[:1, :], none), before], axis=1)
        order_ref[...] = jnp.broadcast_to(order, order_ref.shape)
        choose()
        tab[...] = jnp.zeros_like(tab)
        tab[:heads, : tab_ref.shape[1]] = tab_ref[...]
        found = add_thirds(mm(in_thirds(tab[...]), partial[1, : 4 * seq, : 4 * seq]))
        after, before = found[:, : 2 * seq], found[:, 2 * seq :]
        for c in range(grid):
            low = pltpu.roll(after, c, 1) if c else after
            high = pltpu.roll(before, 2 * seq - (grid - c), 1)
            row = jnp.where(lane % grid >= c, low, high)
            for h in range(heads):
                tx_ref[h, c : c + 1, :] = row[h : h + 1, :]

        def expand(h, carry):
            for r in range(grid):
                shift = (2 * seq - grid * (grid - 1 - r)) % (2 * seq)
                bias[h, r * grid : (r + 1) * grid, :] = pltpu.roll(tx_ref[h], shift, 1)[:, :seq]
            return carry

        lax.fori_loop(0, heads, expand, 0)
        loads[0].wait()
        tp_ref[...] = jnp.zeros_like(tp_ref)
        emb = jnp.concatenate([temb_ref[...], jnp.zeros((16 - count, width), BF16)], axis=0)
        for c in range(3):
            tp_ref[c] = mm_nt(emb, partial[0, c * local : (c + 1) * local, :])

    @pl.when(s == 1)
    def _():
        tables()

        def spread_cot(i):
            ag_pass(DMLP, i)
            ag_near(DMLP, i)
            ag_rest(DMLP, i)

        each_image(spread_cot)
        turn(DMLP)
        line_start(1)
        turn_qkv()
        loads[2].wait()
        turn_weight(sums.at[0], wo_ref)
        loads[3].wait()
        turn_weight(partial.at[0], w1_ref)
        loads[4].wait()

        def early(i):
            dh[i] = mm_nt(gath[DMLP, i], w2_ref[...]).astype(BF16)

        each_image(early)
        line_pass(1, 1)

    @pl.when(s == 0)
    def _():
        each_image(lambda i: ag_start(ATT, i))
        tables()
        turn_qkv()
        for n in (2, 3, 4):
            loads[n].wait()

    def project(i, half):
        a = gath[ATT, i, half_of(half), :]
        part = mm(a, partial[1, :, : 2 * wide + local])
        for c in range(3):
            qkv[c, i, half_of(half), :] = (
                part[:, c * wide : c * wide + local] + tp_ref[c, pl.ds(i, 1), :]
            ).astype(BF16)

    def att_first(i):
        @pl.when(s == 1)
        def _():
            take_input(i)

    lead(ATT, att_first, lambda i: project(i, here))

    def att_rest(i):
        project(i, there)
        acc[0] = jnp.zeros_like(acc[0])
        for h, (lo, hi, start, stop) in enumerate(windows):
            q = only(qkv[0, i, :, lo:hi], start, stop)
            scores = mm_nt(q, qkv[1, i, :, lo:hi]) * scale + bias[h]
            top = jnp.max(scores, axis=-1, keepdims=True)
            expo = jnp.exp(scores - top)
            p = expo * (1.0 / jnp.sum(expo, axis=-1, keepdims=True))
            p = p.astype(BF16)
            prob[i, h] = p
            acc[0, :, lo:hi] += mm(p, only(qkv[2, i, :, lo:hi], start, stop))
        att[i] = acc[0, :, :local].astype(BF16)
        far_att[i] = pltpu.roll(acc[0], far_att.shape[-1] - local, 1).astype(BF16)
        rs_give(ATT, i, 0, mm(att[i, half_of(there), :], wo_ref[...]))
        rs_give(ATT, i, 1, mm(att[i, half_of(here), :], wo_ref[...]))

    follow(ATT, att_rest)

    turn(ATT)
    give_factor(0, 3 + full)

    def att_end(i):
        y = xin[i].astype(F32) + rs_take(ATT, i)
        ag_done(ATT, i)
        rs_done(ATT, i)
        ymid[i] = y
        gath[MLP, i, own, :] = norm(y, 1, i)
        ag_start(MLP, i)

    def mlp_half(i, half, which):
        a = gath[MLP, i, half_of(half), :]
        v = mm(a, w1_ref[...])
        value, slope = gelu_parts(v)
        act[i, half_of(half), :] = value.astype(BF16)
        dgel[i, half_of(half), :] = slope.astype(BF16)
        rs_give(MLP, i, which, mm(act[i, half_of(half), :], w2_ref[...]))

    def mlp_end(i):
        y = (ymid[i] + rs_take(MLP, i)).astype(BF16)
        rs_done(MLP, i)

        @pl.when(s == 0)
        def _():
            ig_ref[i] = y
            mid_copy(i).start()

        @pl.when(s == 1)
        def _():
            out_ref[i] = y
            out_copy(i).start()

    def take_grad(i):
        mid_copy(i).wait_send()
        grad_copy(i).wait_recv()
        gath[DMLP, i, own, :] = xin[i]
        ag_start(DMLP, i)

    def dmlp_half(i, half, which):
        @pl.when(s == 0)
        def _():
            dh[i, half_of(half), :] = mm(gath[DMLP, i, half_of(half), :], partial[1]).astype(BF16)

        dact = dh[i, half_of(half), :].astype(F32)
        dh[i, half_of(half), :] = (dact * dgel[i, half_of(half), :].astype(F32)).astype(BF16)
        rs_give(DMLP, i, which, mm(dh[i, half_of(half), :], partial[0]))

    def mlp_rest(i):
        ag_rest(MLP, i)
        mlp_half(i, there, 0)

        @pl.when(i < count - 1)
        def _():
            ag_pass(MLP, i + 1)

        @pl.when(s == 0)
        def _():
            rs_pass(MLP, i)

        @pl.when(s == 1)
        def _():
            dmlp_half(i, there, 0)
            dmlp_half(i, here, 1)
            rs_pass(DMLP, i)

    lead(MLP, att_end, lambda i: mlp_half(i, here, 1))
    each_image(mlp_rest)
    turn(MLP)
    line_start(0)

    def dmlp_rest(i):
        @pl.when(i == count - 1)
        def _():
            turn(DMLP)
            line_start(1)

        dmlp_half(i, there, 0)

    @pl.when(s == 0)
    def _():
        each_image(mlp_end)
        turn_weight(partial.at[0], w1_ref)
        turn_weight(partial.at[1], w2_ref)
        turn_weight(sums.at[0], wo_ref)
        for d in range(1, ring):
            line_pass(0, d)
        lead(DMLP, take_grad, lambda i: dmlp_half(i, here, 1))
        follow(DMLP, dmlp_rest)

    @pl.when(s == 1)
    def _():
        last_rows.start()
        last_rows.wait()

    def dmlp_end(i):
        grad = xin[i].astype(F32) + norm_back(rs_take(DMLP, i), 1, i)
        rs_done(DMLP, i)
        dy1[i] = grad
        gath[DATT % 3, i, own, :] = grad.astype(BF16)
        ag_start(DATT, i)

    def datt_part(i, half):
        att[i, half_of(half), :] = mm(
            gath[DATT % 3, i, half_of(half), :], sums[0, :, :local]
        ).astype(BF16)

    def turn_factor(i):
        turn_image(DATT, i)

        @pl.when(i == t % 2)
        def _():
            give_factor(1)

    lead(DATT, dmlp_end, lambda i: datt_part(i, here))

    @pl.when(s == 0)
    def _():
        line_pass(1, 1)

        def gathered(i):
            ag_rest(DATT, i)
            turn_factor(i)

            @pl.when(i < count - 1)
            def _():
                ag_pass(DATT, i + 1)

        each_image(gathered)

    def datt_rest(i):
        @pl.when(s == 1)
        def _():
            ag_rest(DATT, i)

        datt_part(i, there)

        @pl.when(s == 1)
        def _():
            turn_factor(i)

        acc[...] = jnp.zeros_like(acc)
        for h, (lo, hi, start, stop) in enumerate(windows):
            q = only(qkv[0, i, :, lo:hi], start, stop)
            k = only(qkv[1, i, :, lo:hi], start, stop)
            d = only(att[i, :, lo:hi], start, stop)
            low = prob[i, h]
            p = low.astype(F32)
            dp = mm_nt(d, qkv[2, i, :, lo:hi])
            inner = jnp.sum(p * dp, axis=-1, keepdims=True)
            ds = (p * (dp - inner)).astype(BF16)

            @pl.when(i == 0)
            def _():
                bias[h] = ds.astype(F32)

            @pl.when(i > 0)
            def _():
                bias[h] += ds.astype(F32)

            acc[0, :, lo:hi] += mm(ds, k)
            acc[1, :, lo:hi] += mm_tn(ds, q)
            acc[2, :, lo:hi] += mm_tn(low, d)
        tiles = [None] * (lanes // 128)
        for c, by in enumerate((scale, scale, 1.0)):
            first = c * local // 128
            moved = acc[c] * by
            if c * local > first * 128:
                moved = pltpu.roll(moved, c * local - first * 128, 1)
            for n in range(moved.shape[1] // 128):
                tile = moved[:, n * 128 : (n + 1) * 128]
                tiles[first + n] = tile if tiles[first + n] is None else tiles[first + n] + tile
        per = wide // 128
        over_tokens = []
        for c in range(full + 1):
            part = jnp.concatenate(tiles[c * per : (c + 1) * per], axis=1).astype(BF16)
            if c < full:
                dqkv[c, i] = part
            else:
                dtail[i] = part
            over_tokens.append(jnp.sum(part.astype(F32), axis=0, keepdims=True))
        tok_ref[z, pl.ds(i, 1), :lanes] = jnp.concatenate(over_tokens, axis=1)
        last = 3 * local - full * wide
        for which, half in ((0, there), (1, here)):
            da = mm(dtail[i, half_of(half), :last], wq_ref[full * wide :, :])
            for c in range(full):
                da += mm(dqkv[c, i, half_of(half), :], wq_ref[c * wide : (c + 1) * wide, :])
            rs_give(DATT, i, which, da)

        @pl.when((s == 1) & (i < count - 1))
        def _():
            ag_pass(DATT, i + 1)

        rs_pass(DATT, i)

    each_image(datt_rest)

    give_factor(2 + full, *range(2, 2 + full))

    @pl.when(s == 1)
    def _():
        line_pass(0, 1)

    def first_parts():
        own_rest()
        mlp_own()
        share_factor(0)
        share_factor(1)
        choose()

    ig_store = pltpu.make_async_copy(ig_ref, ig_hbm, store_s.at[18])
    out_store = pltpu.make_async_copy(out_ref, out_hbm, store_s.at[19])

    def end_of_chain(r, carry):
        if chained:
            pl.when(r == s)(first_parts)

        @pl.when(r == 0)
        def _():
            line_pass(1, 2)

        @pl.when(r == 1)
        def _():
            line_pass(0, 2)

        if chained:

            @pl.when(r == s)
            def _():
                give_rest(full)

        @pl.when(r == 0)
        def _():

            def datt_end(i):
                grad = dy1[i] + norm_back(rs_take(DATT, i), 0, i)
                ig_ref[i] = grad.astype(BF16)

                @pl.when(s == 1)
                def _():
                    grad_copy(i).start()

            each_image(datt_end)

            ig_store.start()

            @pl.when(s == 0)
            def _():
                each_image(lambda i: out_copy(i).wait_recv())
                out_store.start()

            @pl.when(s == 1)
            def _():
                each_image(lambda i: rs_pass(MLP, i))

            for j in range(3):
                small_copy(0, j).start()

            def fold(h, carry):
                total = jnp.zeros((grid, 2 * seq), F32)
                for r in range(grid):
                    part = wider(bias[h, r * grid : (r + 1) * grid, :], 2 * seq)
                    shift = grid * (grid - 1 - r)
                    total += part if shift == 0 else pltpu.roll(part, shift, 1)
                after = total[:1, :]
                before = jnp.zeros((1, 2 * seq), F32)
                for c in range(1, grid):
                    row = total[c : c + 1, :]
                    late = lane % grid >= c
                    after += pltpu.roll(jnp.where(late, row, 0.0), 2 * seq - c, 1)
                    before += pltpu.roll(jnp.where(late, 0.0, row), grid - c, 1)
                tok_ref[z, pl.ds(count + h, 1), : 4 * seq] = jnp.concatenate([after, before], axis=1)
                return carry

            lax.fori_loop(0, heads, fold, 0)
            for j in range(3):
                small_copy(0, j).wait_recv()
            over_tensor = tiny_s[0] + small_r[0, 0] + small_r[0, 1] + small_r[0, 2]
            row = lax.broadcasted_iota(jnp.int32, over_tensor.shape, 0)
            tok_ref[z, count + heads : count + heads + 1, :] = jnp.sum(
                jnp.where(row == t, over_tensor, 0.0), axis=0, keepdims=True
            )
            over_ring(lambda j: tiny_copy(1, j).start())

            @pl.when(s == 1)
            def _():
                each_image(mlp_end)
                out_store.start()

        return carry

    lax.fori_loop(0, 1 + s, end_of_chain, 0)

    if chained:
        give_rest(0)

        def others(j, carry):
            d = 1 + j // 2
            zs = z - d + 2 * d * (j % 2)

            @pl.when((zs >= 0) & (zs < ring))
            def _():
                mlp_of(zs)

            @pl.when(j == 0)
            def _():
                for c in range(1, full):
                    give_rest(c)
                relay(full)
                relay(0)

            @pl.when(j == 1)
            def _():
                for c in range(1, full):
                    relay(c)

            @pl.when((j == 3) & (s == 1))
            def _():
                line_pass(0, 3)

            @pl.when(j == 3)
            def _():
                line_pass(1, 3)

            return carry

        lax.fori_loop(0, 2 * (ring - 1), others, 0)
    else:

        def whole(b, carry):
            at = block(b)
            parts_ref[0, b] = sum(mm(line[1, i, at, :], act[i]) for i in range(count)).astype(BF16)
            parts_ref[1, b] = sum(mm(line[0, i, at, :], dh[i]) for i in range(count)).astype(BF16)
            parts_ref[2, b] = jnp.concatenate(
                [rest_product(c, at, 0) for c in range(full + 1)], axis=1
            ).astype(BF16)
            return carry

        lax.fori_loop(0, blocks, whole, 0)
        choose()
    stores = []

    def store(src, dst):
        copy = pltpu.make_async_copy(src, dst, store_s.at[len(stores)])
        copy.start()
        stores.append(copy)
        return copy

    if chained:
        store(mlp_ref, mlp_hbm)
    over_ring(lambda j: tiny_copy(1, j).wait_recv())

    def add_slot(j, total):
        return total + tok_ref[j]

    total = lax.fori_loop(0, ring, add_slot, jnp.zeros(tok_ref.shape[1:], F32))
    tiny_s[1] = total
    for j in range(3):
        small_copy(1, j).start()
    tab[...] = jnp.zeros_like(tab)
    tab[:heads, :] = tiny_s[1, count : count + heads, : 4 * seq]
    found = add_thirds(mm_nt(in_thirds(tab[...]), partial[1, : 4 * seq, : 4 * seq]))
    gtab_ref[...] = found[:heads, : gtab_ref.shape[1]]
    store(gtab_ref, gtab_hbm)

    over_ring(lambda j: tiny_copy(0, j).wait_recv())
    mine = width // ring
    rows_of_emb = emb_ref[...].reshape(ring * 8, width)
    rows_of_emb = pltpu.roll(rows_of_emb, (width - z * mine) % width, 1)[:, :mine].astype(BF16)
    right = in_thirds(tok_ref[...].reshape(ring * 8, width)[:, :lanes])
    over_images = mm_tn(jnp.concatenate([rows_of_emb] * 3, axis=0), right)
    time_stores = []
    for c in range(3):
        first = c * local // 128 * 128
        window = over_images[:, first : first + wide]
        if c * local > first:
            window = pltpu.roll(window, wide - (c * local - first), 1)
        exact[c, :mine, :] = window[:, :local]
        time_stores.append(store(exact.at[c], gt_hbm.at[c]))
    if chained:
        settle(full)
        window = sums[full, block(z), :].astype(F32)
        window = pltpu.roll(window, wide - (3 * local - (width - wide)), 1)
        for copy in time_stores:
            copy.wait()
        exact[0] = window.T[:local]
        out_grad_store = store(exact.at[0], go_hbm)
    for j in range(3):
        small_copy(1, j).wait_recv()
    last = count + heads
    small_ref[pl.ds(t, 1), :] = tiny_s[1, last : last + 1, :]
    for j, owner in enumerate((core, far, fcore)):
        small_ref[pl.ds(owner, 1), :] = small_r[1, j, last : last + 1, :]
    ggain_ref[...] = small_ref[:2, :]
    gshift_ref[...] = small_ref[2:, :]
    store(ggain_ref, ggain_hbm)
    store(gshift_ref, gshift_hbm)
    if chained:
        settled = 0
        for c in range(3):
            first = c * local // 128 * 128
            while settled < full and settled * wide < first + wide:
                settle(settled)
                settled += 1
            n, offset = first // wide, first % wide
            window = sums[n, block(z), offset:]
            if offset:
                window = jnp.concatenate([window, sums[n + 1, block(z), :offset]], axis=1)
            window = window.astype(F32)
            if c * local > first:
                window = pltpu.roll(window, wide - (c * local - first), 1)
            if c == 0:
                out_grad_store.wait()
            exact[c] = window[:, :local]
            store(exact.at[c], gq_hbm.at[c])

    def finish(i):
        for k in (MLP, DMLP, DATT):
            ag_done(k, i)
        rs_done(DATT, i)

        @pl.when(s == 1)
        def _():
            out_copy(i).wait_send()
            grad_copy(i).wait_send()

    each_image(finish)
    ig_store.wait()
    out_store.wait()

    def tiny_left(j):
        tiny_copy(0, j).wait_send()
        tiny_copy(1, j).wait_send()

    over_ring(tiny_left)
    for j in range(3):
        small_copy(0, j).wait_send()
        small_copy(1, j).wait_send()
    if chained:
        weights_left()
    waited = time_stores + [out_grad_store] if chained else []
    for copy in stores:
        if all(copy is not done for done in waited):
            copy.wait()


def run_block(x, cot, wq, wt, wo, w1, w2, temb, gain, shift, rel, table, ring):
    count, rows, width = x.shape
    seq = rel.shape[0]
    heads = table.shape[0]
    local = wo.shape[0]
    hidden = w1.shape[1]
    chained = ring == 4 and count == 2 and width % (16 * ring) == 0 and local == width // ring
    blocks = 4
    pieces = 3 if width // 4 % 48 == 0 else 1
    cut = width // blocks
    padded = -(-local // 128) * 128
    lanes = -(-3 * local // 128) * 128
    dims = (count, rows, seq, heads, ring, chained)
    full = 3 * local // padded
    assert pieces == full + 1 and padded * pieces == width
    mine = width // ring
    small = (8, 128)
    out_shape = [
        jax.ShapeDtypeStruct((count, rows, width), BF16),
        jax.ShapeDtypeStruct((count, rows, width), BF16),
        jax.ShapeDtypeStruct((16, 128) if chained else (3, blocks, cut, width), BF16),
        jax.ShapeDtypeStruct((2, cut, width) if chained else small, F32),
        jax.ShapeDtypeStruct((3, cut, local) if chained else small, F32),
        jax.ShapeDtypeStruct((local, cut) if chained else small, F32),
        jax.ShapeDtypeStruct((3, -(-mine // 8) * 8, local), F32),
        jax.ShapeDtypeStruct(table.shape, F32),
        jax.ShapeDtypeStruct((2, width), F32),
        jax.ShapeDtypeStruct((2, width), F32),
    ]
    vm = pltpu.VMEM
    dma = pltpu.SemaphoreType.DMA
    scratch = [
        vm(temb.shape, BF16),
        vm(gain.shape, F32),
        vm(shift.shape, F32),
        vm(rel.shape, jnp.int32),
        vm(table.shape, F32),
        vm((count, rows, width), BF16),
        vm((count, rows, width), BF16),
        vm((2, cut, width) if chained else (2, 8, 128), F32),
        vm((3, -(-mine // 8) * 8, local), F32),
        vm((ring, 8, width), F32),
        vm((ring, 8, width), F32),
        vm(table.shape, F32),
        vm((4, width), F32),
        vm((2, width), F32),
        vm((2, width), F32),
        vm(wq.shape, BF16),
        vm(wo.shape, BF16),
        vm(w1.shape, BF16),
        vm(w2.shape, BF16),
        vm((3, 16, local), F32),
        vm((heads, int(round(seq**0.5)), 2 * seq), F32),
        vm((8, 4 * seq), jnp.int32),
        vm((16, 4 * seq), F32),
        vm((2, width, width), BF16),
        vm((pieces, width, padded), BF16),
        vm((2, pieces, cut, padded) if chained else (16, 128), BF16),
        vm((2, 8, width), F32),
        vm((2, 3, 8, width), F32),
        vm((count, rows, width), BF16),
        vm((3, count, seq, width), BF16),
        vm((2, count, 2, rows, width), F32),
        vm((2, count, 2, rows, width), BF16),
        vm((2, count, rows, width), BF16),
        vm((2, count, 2, rows, width), BF16),
        vm((2, count, rows, width), BF16),
        vm((heads, seq, seq), F32),
        vm((count, heads, seq, seq), BF16),
        vm((3, count, seq, local), BF16),
        vm((count, seq, local), BF16),
        vm((count, seq, hidden), BF16),
        vm((count, seq, hidden), BF16),
        vm((2, count, rows, width), F32),
        vm((2, count, rows, 128), F32),
        vm((count, rows, width), F32),
        vm((count, rows, width), F32),
        vm((full, count, seq, padded), BF16),
        vm((count, seq, lanes - full * padded), BF16),
        vm((count, seq, hidden), BF16),
        vm((3, seq, padded), F32),
        vm((2, 2 * count if chained else count, width, seq), BF16),
        vm((2, ring * count if chained else count, width, seq), BF16),
        vm((count, seq, padded), BF16),
        vm((full, count, seq, padded) if chained else (16, 128), BF16),
        vm((count, seq, lanes - full * padded) if chained else (16, 128), BF16),
        vm((count, seq, padded) if chained else (16, 128), BF16),
        dma((12 + count,)),
        dma((20,)),
        dma((4, count, 3)),
        dma((4, count, 3)),
        dma((4, count, 3)),
        dma((4, count, 3)),
        dma((3, count)),
        dma((3, count)),
        dma((3, pieces)),
        dma((2, pieces)),
        dma((6 + full,)),
        dma((6 + full,)),
        dma((2, 3, ring)),
        dma((2, 3, ring)),
        dma((2, ring)),
        dma((2, ring)),
        dma((2, 3)),
        dma((2, 3)),
    ]
    whole = pl.BlockSpec(memory_space=pltpu.VMEM)
    lies = pl.BlockSpec(memory_space=pl.ANY)
    return pl.pallas_call(
        functools.partial(block_kernel, dims),
        out_shape=out_shape,
        in_specs=[lies] * 12,
        out_specs=[lies] * 2 + [lies if chained else whole] + [lies] * 7,
        scratch_shapes=scratch,
        compiler_params=pltpu.CompilerParams(
            collective_id=0, has_side_effects=True, vmem_limit_bytes=63 * 2**20
        ),
        name="blocks",
    )(x, cot, wq, wt, wo, w1, w2, temb, gain, shift, rel, table)


def per_device(
    images, timesteps, t_table, rel_index, w_qkv, w_time, w_out, w_fc1, w_fc2, rel_table,
    norm_gain, norm_shift, cotangent,
):
    ring = lax.axis_size("dp")
    count = images.shape[0]
    width = images.shape[-1]
    local = w_out.shape[1]
    cut = width // ring
    steps = lax.broadcasted_iota(jnp.int32, (count, t_table.shape[0]), 1)
    embedded = jnp.dot(
        (steps == timesteps[:, None]).astype(BF16), t_table, preferred_element_type=F32
    ).astype(BF16)
    wq = jnp.transpose(w_qkv[0], (1, 2, 0)).reshape(3 * local, width)
    wt = jnp.transpose(w_time[0], (1, 2, 0)).reshape(3 * local, width)
    output, in_grad, parts, mlp, g_qkv, g_out, g_time, g_table, g_gain, g_shift = run_block(
        images, cotangent, wq, wt, w_out[0], w_fc1[0], w_fc2[0], embedded, norm_gain[0], norm_shift[0],
        rel_index, rel_table[0].T, ring,
    )
    if parts.ndim == 4:
        parts = lax.psum_scatter(
            parts.reshape(3, width, width), "dp", scatter_dimension=1, tiled=True
        ).astype(F32)
        g_fc2, g_fc1, rest = parts
        g_qkv = jnp.transpose(rest[:, : 3 * local].reshape(cut, 3, local), (1, 0, 2))
        g_out = rest[:, 3 * local :].T
    else:
        g_fc2, g_fc1 = mlp
    g_time = g_time[:, : width // ring]
    return (
        output, in_grad[None], jnp.transpose(g_qkv, (1, 0, 2))[None],
        jnp.transpose(g_time, (1, 0, 2))[None], g_out[None], g_fc1[None], g_fc2.T[None],
        g_table.T[None], g_gain[None], g_shift[None],
    )


def solution(mesh):
    in_specs = (
        P("dp", "tensor", None),
        P("dp"),
        P(),
        P(),
        P("section", None, None, "tensor"),
        P("section", None, None, "tensor"),
        P("section", "tensor", None),
        P("section", None, "tensor"),
        P("section", "tensor", None),
        P("section", None, "tensor"),
        P("section", None, None),
        P("section", None, None),
        P("dp", "tensor", None),
    )
    out_specs = (
        P("dp", "tensor", None),
        P("section", "dp", "tensor", None),
        P("section", "dp", None, "tensor"),
        P("section", "dp", None, "tensor"),
        P("section", "tensor", "dp"),
        P("section", "dp", "tensor"),
        P("section", "tensor", "dp"),
        P("section", None, "tensor"),
        P("section", None, None),
        P("section", None, None),
    )
    return jax.shard_map(
        per_device, mesh=mesh, in_specs=in_specs, out_specs=out_specs, check_vma=False
    )
```
